32 devices in a mesh: tm: 8 (over z, x), rows: 4 (over y, core).
Axes of the slice: x: 2, y: 2, z: 4, core: 2. Of those that a mesh axis runs over, the one named last changes fastest.
Arguments:
- inputs: bfloat16 [8, 1024, 2048], P('rows', 'tm'), may hold values from -6 to 6
- out_grad: bfloat16 [8, 1024, 2048], P('rows', 'tm'), may hold values from -6 to 6
- reset_flags: int32 [8, 1024], P('rows', 'tm'), may hold values from 0 to 1, as said below
- weights: bfloat16 [2, 2048, 6144], P(None, ('tm', 'rows')), may hold values from -0.125 to 0.125
- ln_gain: float32 [2, 2048], replicated, may hold values from 0.5 to 1.5
- layer_norm_bias: float32 [2, 2048], replicated, may hold values from -3 to 3
- reset_peep: float32 [2, 2048], replicated, may hold values from -1.5 to 1.5
- forget_bias: float32 [2, 2048], replicated, may hold values from 3.2 to 9.5
- reset_bias: float32 [2, 2048], replicated, may hold values from -3 to 3
Outputs:
- outputs: bfloat16 [8, 1024, 2048], P('rows', 'tm')
- input_grad: bfloat16 [8, 1024, 2048], P('rows', 'tm')
- weight_grad: float32 [2, 2048, 6144], P(None, ('tm', 'rows'))
- gain_grad: float32 [2, 2048], P(None, ('tm', 'rows'))
- bias_grad: float32 [2, 2048], P(None, ('tm', 'rows'))
- peep_grad: float32 [2, 2048], P(None, ('tm', 'rows'))
- forget_grad: float32 [2, 2048], P(None, ('tm', 'rows'))
- reset_grad: float32 [2, 2048], P(None, ('tm', 'rows'))
The draws below stay inside these ranges and needn't reach their ends.
Inputs may be any that keep to these rules, and one draw needn't show every extreme that they name: `reset_flags`: position 0 of every row is 1. In each aligned block of 2 rows one row, drawn from the seed, has no other 1; in the other rows the 1s start sentences of 64 to 192 positions.
All inputs are finite; a program needn't handle non-finite values.
Results may differ from the reference program's by a relative error of at most 0.0051.
Values may be sent and summed in bfloat16 or wider, within the bound.
No kernel may reach another device: no remote copies, remote signals or barrier semaphores. Data moves between devices by JAX's collectives and lax.ppermute only.
A program may use at most 256 MiB of HBM per device.

```python
import jax
import jax.numpy as jnp
from jax import lax

D = 2048
PROJ = 6144
LAYERS = 2
ROWS_DEV = 2
SENT = 128
ROWS = 8
LENGTH = 1024


def draw_forget_bias(key, part):
    key = jax.random.fold_in(key, 5)
    pick_key, fast_key, slow_key = jax.random.split(key, 3)
    fast_share = 0.5
    choose = jax.random.uniform(pick_key, (LAYERS, D), jnp.float32)
    fast_bias = jax.random.uniform(fast_key, (LAYERS, D), jnp.float32, minval=3.2, maxval=4.5)
    slow_bias = jax.random.uniform(slow_key, (LAYERS, D), jnp.float32, minval=8.0, maxval=9.5)
    return jnp.where(choose < fast_share, fast_bias, slow_bias)


def draw_reset_flags(key, part):
    key = jax.random.fold_in(key, 11)
    length_key, row_key = jax.random.split(key)
    sentence_count = LENGTH // (SENT // 2) + 2
    sentence_len = jax.random.randint(length_key, (ROWS, sentence_count), SENT // 2, SENT + SENT // 2 + 1)
    starts = jnp.cumsum(sentence_len, axis=1) - sentence_len
    row_index = jnp.broadcast_to(jnp.arange(ROWS)[:, None], starts.shape)
    flags = jnp.zeros((ROWS, LENGTH), jnp.int32).at[row_index, starts].set(1, mode='drop')
    chosen = jax.random.randint(row_key, (ROWS // ROWS_DEV,), 0, ROWS_DEV)
    long_row = jnp.arange(ROWS) % ROWS_DEV == jnp.repeat(chosen, ROWS_DEV)
    first_only = (jnp.arange(LENGTH) == 0).astype(jnp.int32)
    return jnp.where(long_row[:, None], first_only[None, :], flags)


def spiked(entries, stream_key, source, target, parts, factor):
    def block_of(axis_at):
        return (jnp.arange(entries.shape[axis_at]) // (entries.shape[axis_at] // parts)).reshape((-1,) + (1,) * (entries.ndim - 1 - axis_at))

    one_side = jax.random.permutation(stream_key, parts)[block_of(target)]
    other_side = (block_of(target) + parts // 2) % parts
    return jnp.where((block_of(source) == one_side) | (block_of(source) == other_side), factor * entries, entries)


def steps_of(key, extent, pieces, smallest, high):
    loudness, own = 1.0, jax.random.fold_in(key, 6)
    for dim, blocks in pieces:
        heights = jnp.exp(jax.random.uniform(jax.random.fold_in(own, dim), (blocks,), jnp.float32, smallest / len(pieces), high / len(pieces)))
        loudness = loudness * jnp.repeat(heights, extent[dim] // blocks).reshape([-1 if axis == dim else 1 for axis in range(len(extent))])
    return loudness


def centred(stream_key, shape, scale, bound, pieces=(), kind=jnp.bfloat16):
    gain = steps_of(stream_key, shape, pieces, -0.22, 0.18) if pieces else 1.0
    array = jax.random.normal(stream_key, shape, jnp.float32) * scale * gain
    return jnp.minimum(jnp.maximum(array, -bound), bound).astype(kind)


def bell_draw_with(rng, dims, scale, limit, cuts, heavy, kind=jnp.bfloat16):
    entries = scale * jax.random.normal(rng, dims, jnp.float32)
    if cuts:
        entries = entries * steps_of(rng, dims, cuts, -0.22, 0.18)
    return jnp.clip(spiked(entries, jax.random.fold_in(rng, 3), *heavy), -limit, limit).astype(kind)


def setup_inputs(seed: int = 0) -> dict:
    seeds = jax.random.split(jax.random.key(seed), 10)
    inputs = bell_draw_with(seeds[0], (ROWS, LENGTH, D), 1.0, 6.0, ((0, 4), (1, 8)), (1, 2, 8, 2.0))
    out_grad = centred(seeds[1], (ROWS, LENGTH, D), 1.0, 6.0, ((0, 4), (1, 8)))
    reset_flags = draw_reset_flags(jax.random.fold_in(seeds[9], 71), 0)
    weights = centred(seeds[3], (LAYERS, D, PROJ), D ** -0.5, 0.125, ((1, 32),))
    ln_gain = jnp.clip(1.0 + 0.1 * jax.random.normal(seeds[4], (LAYERS, D), jnp.float32), 0.5, 1.5)
    layer_norm_bias = centred(seeds[5], (LAYERS, D), 0.5, 3.0, (), jnp.float32)
    reset_peep = jnp.clip(jax.random.uniform(seeds[6], (LAYERS, D), jnp.float32, -1.5, 1.5), -1.5, 1.5)
    forget_bias = draw_forget_bias(jax.random.fold_in(seeds[9], 71), 0)
    reset_bias = centred(seeds[8], (LAYERS, D), 0.5, 3.0, (), jnp.float32)
    return dict(inputs=inputs, out_grad=out_grad, reset_flags=reset_flags, weights=weights, ln_gain=ln_gain, layer_norm_bias=layer_norm_bias, reset_peep=reset_peep, forget_bias=forget_bias, reset_bias=reset_bias)


@jax.custom_vjp
def low(v):
    return lax.optimization_barrier(v.astype(jnp.bfloat16)).astype(jnp.float32)

@jax.custom_vjp
def low_back(v):
    return v

def low_keep(v):
    return (low(v), None)

def low_pass(kept, grad):
    return (grad,)

def back_keep(v):
    return (v, None)

def back_low(kept, grad):
    return (low(grad),)
low.defvjp(low_keep, low_pass)
low_back.defvjp(back_keep, back_low)

def layer_forward(stream, carry_keep, weight, norm_gain_vector, bias_vec, peep_vec, forget_vec, reset_vec):
    means = lax.optimization_barrier(jnp.mean(stream, axis=-1, keepdims=True))
    centered_input = stream - means
    variance = lax.optimization_barrier(jnp.mean(centered_input * centered_input, axis=-1, keepdims=True))
    normed = low(centered_input * lax.rsqrt(variance + 1e-05) * norm_gain_vector + bias_vec)
    flat = normed.reshape(-1, D)
    mixture = jnp.dot(flat, weight, precision=lax.Precision.HIGHEST, preferred_element_type=jnp.float32)
    mixture = low_back(mixture.reshape(stream.shape[0], stream.shape[1], 3 * D))
    candidate = mixture[..., :D]
    forget = jax.nn.sigmoid(mixture[..., D:2 * D] + forget_vec)
    reset_pre = mixture[..., 2 * D:]

    def advance(state, items):
        cand_now, forget_now, keep_now = items
        previous = keep_now * state
        new_state = forget_now * previous + (1.0 - forget_now) * cand_now
        return (new_state, (new_state, previous))
    timed = (jnp.swapaxes(candidate, 0, 1), jnp.swapaxes(forget, 0, 1), jnp.swapaxes(carry_keep, 0, 1)[:, :, None])
    start_state = jnp.zeros((stream.shape[0], D), jnp.float32)
    last_state, outs_timed = lax.scan(advance, start_state, timed)
    states = jnp.swapaxes(outs_timed[0], 0, 1)
    previous = jnp.swapaxes(outs_timed[1], 0, 1)
    gate = jax.nn.sigmoid(reset_pre + peep_vec * previous + reset_vec)
    return gate * states + (1.0 - gate) * stream

def reference(inputs, out_grad, reset_flags, weights, ln_gain, layer_norm_bias, reset_peep, forget_bias, reset_bias):
    carry_keep = (1 - reset_flags).astype(jnp.float32)

    def forward(stream, weight_all, gains, biases, peeps, forgets, resets):
        for depth in range(LAYERS):
            stream = layer_forward(stream, carry_keep, weight_all[depth], gains[depth], biases[depth], peeps[depth], forgets[depth], resets[depth])
        return stream
    primals = (inputs.astype(jnp.float32), weights.astype(jnp.float32), ln_gain, layer_norm_bias, reset_peep, forget_bias, reset_bias)
    result, pullback = jax.vjp(forward, *primals)
    grads = pullback(out_grad.astype(jnp.float32))
    return (result.astype(jnp.bfloat16), grads[0].astype(jnp.bfloat16), grads[1], grads[2], grads[3], grads[4], grads[5], grads[6])
```

```python
import functools

import jax
import jax.numpy as jnp
import numpy as np
from jax import lax
from jax.experimental import pallas as pl
from jax.experimental.pallas import tpu as pltpu
from jax.sharding import Mesh
from jax.sharding import PartitionSpec as P

LANES = 128
SUBLANES = 8
STEPS = 64
SUB = 32
VMEM_BYTES = 58 * 1024 * 1024
GAIN, BIAS, PEEP, FORGET, RESET = range(5)
BF16 = jnp.bfloat16
F32 = jnp.float32
GROUP = ("pair", "rows")
CORE, LINE, PAIR = 1, 2, 4


def shape_of(dtype, *shape):
    return jax.ShapeDtypeStruct(shape, dtype)


def run(
    kernel, name, grid, ins, in_specs, outs, out_specs, scratch=(), place=None, cost=(0, 0), awaited=()
):
    scalars = 0 if place is None else 1
    first = scalars + len(ins)
    last = first + len(awaited)

    def body(*refs):
        kernel(*refs[:first], *refs[last:])

    function = pl.pallas_call(
        body,
        out_shape=outs,
        grid_spec=pltpu.PrefetchScalarGridSpec(
            num_scalar_prefetch=scalars,
            grid=grid,
            in_specs=list(in_specs) + [pl.BlockSpec(memory_space=pl.ANY)] * len(awaited),
            out_specs=out_specs,
            scratch_shapes=list(scratch),
        ),
        compiler_params=pltpu.CompilerParams(vmem_limit_bytes=VMEM_BYTES),
        cost_estimate=pl.CostEstimate(flops=cost[0], bytes_accessed=cost[1], transcendentals=0),
        name=name,
    )
    return function(*(() if place is None else (place,)), *ins, *awaited)


def quarter(index, width):
    return pl.ds(pl.multiple_of(index * width, width), width)


def fixed_spec(*shape):
    return pl.BlockSpec(shape, lambda *_: (0,) * len(shape))


def block_spec(block, width):
    return pl.BlockSpec((block, width), lambda i, *_: (i, 0))


def turned_spec(block, width, count):
    return pl.BlockSpec((block, width), lambda i, *_: (count - 1 - i, 0))


def rows_spec(rows, width, per, place_of=lambda i: i):
    return pl.BlockSpec(
        (1, rows, STEPS, width), lambda i, *_: (place_of(i) // per, 0, place_of(i) % per, 0)
    )


def row_at(vec_ref, layer, which):
    row = layer * 5 + which
    return vec_ref[row : row + 1, :]


def chunks(total, size, body, unroll=1):
    def one(i, carry):
        body(pl.ds(pl.multiple_of(i * size, size), size))
        return carry

    lax.fori_loop(0, total // size, one, 0, unroll=unroll)


def over_time(body, state, backward=False):
    def one(i, state):
        t = STEPS - 1 - i if backward else i
        return body(pl.ds(pl.multiple_of(t * SUBLANES, SUBLANES), SUBLANES), state)

    return lax.fori_loop(0, STEPS, one, state, unroll=8)


def widen(keep, width):
    return jnp.concatenate([keep] * (width // LANES), axis=1)


def incoming(far):
    state = None
    for ref in reversed(far):
        state = ref[1] if state is None else ref[0] * state + ref[1]
    return state


def exact(order, value):
    return jnp.dot(order, value, preferred_element_type=F32)


def to_time(order_ref, rows, put):
    block = order_ref.shape[0]
    for i in range(STEPS // SUB):
        part = rows[:, i * SUB : (i + 1) * SUB, :].reshape(block, rows.shape[-1])
        put(slice(i * block, (i + 1) * block), exact(order_ref[...], part))


def to_rows(back_ref, value_ref, out_ref):
    block = back_ref.shape[0]
    for i in range(STEPS // SUB):
        part = exact(back_ref[...], value_ref[i * block : (i + 1) * block, :])
        out_ref[0, :, i * SUB : (i + 1) * SUB, :] = part.astype(BF16).reshape(
            out_ref.shape[1], SUB, out_ref.shape[3]
        )


def forget_gate(cf_ref, here, vec_ref, layer):
    width = cf_ref.shape[1] // 2
    return jax.nn.sigmoid(cf_ref[here, width:] + row_at(vec_ref, layer, FORGET))


def fold(value):
    return jnp.sum(value.reshape(-1, SUBLANES, value.shape[-1]), axis=0)


def after(values, *awaited):
    count = len(values)

    def nothing(*refs):
        pass

    return pl.pallas_call(
        nothing,
        out_shape=[shape_of(v.dtype, *v.shape) for v in values],
        in_specs=[pl.BlockSpec(memory_space=pl.ANY)] * (count + len(awaited)),
        out_specs=[pl.BlockSpec(memory_space=pl.ANY)] * count,
        input_output_aliases={i: i for i in range(count)},
        name="after",
    )(*values, *awaited)


def columns_kernel(group, width, weights_ref, *refs):
    out_ref = refs[-1]
    shard = weights_ref.shape[1]
    for s in range(group):
        for third in range(3):
            start = third * group * width + s * width
            out_ref[s, :shard, third * width : (third + 1) * width] = weights_ref[
                0, :, start : start + width
            ]
        if len(refs) == 2:
            flags_ref = refs[0]
            out_ref[s, shard:, :] = jnp.zeros_like(out_ref[s, shard:, :])
            out_ref[s, shard:, : flags_ref.shape[1]] = flags_ref[...]


def columns_of(weights, layer, group, width, flags=(), awaited=()):
    _, shard, total = weights.shape
    rows = shard + sum(flag.shape[0] for flag in flags)
    return run(
        functools.partial(columns_kernel, group, width),
        "columns_of",
        (1,),
        [weights, *flags],
        [pl.BlockSpec((1, shard, total), lambda i, *_: (layer, 0, 0))]
        + [fixed_spec(*flag.shape) for flag in flags],
        shape_of(BF16, group, rows, 3 * width),
        fixed_spec(group, rows, 3 * width),
        cost=(0, 4 * shard * total),
        awaited=awaited,
    )


def first_norm_kernel(group, x_ref, gain_ref, bias_ref, *refs):
    split_ref = refs[-1]
    rows, span, model = x_ref.shape
    width = model // group
    for i in range(rows):

        def part(here):
            wide = x_ref[i, here, :].astype(F32)
            centered = wide - jnp.mean(wide, axis=-1, keepdims=True)
            scale = lax.rsqrt(jnp.mean(centered * centered, axis=-1, keepdims=True) + 1e-05)
            refs[i][here, :] = (
                centered * scale * gain_ref[0:1, :] + bias_ref[0:1, :]
            ).astype(BF16)

        chunks(span, 16, part)
        for s in range(group):
            split_ref[s, i] = x_ref[i, :, s * width : (s + 1) * width]


def first_norm(x, gain, bias, group, awaited):
    rows, span, model = x.shape
    return run(
        functools.partial(first_norm_kernel, group),
        "first_norm",
        (1,),
        [x, gain, bias],
        [fixed_spec(*x.shape), fixed_spec(*gain.shape), fixed_spec(*bias.shape)],
        [shape_of(BF16, span, model)] * rows
        + [shape_of(BF16, group, rows, span, model // group)],
        [fixed_spec(span, model)] * rows + [fixed_spec(group, rows, span, model // group)],
        cost=(20 * rows * span * model, 6 * rows * span * model),
        awaited=awaited,
    )


def project_kernel(layer, gather, slots, place, *refs):
    pieces = refs[:slots]
    w_ref, order_ref, keep_ref, vec_ref = refs[slots : slots + 4]
    cf_ref, whole_ref, tot_ref, held, forget_s = refs[slots + 4 :]
    width = cf_ref.shape[1] // 2
    step = pl.program_id(0)
    gather(place, step, pieces, order_ref, held, whole_ref)
    cf_ref[...] = jnp.dot(whole_ref[...], w_ref[...], preferred_element_type=F32)

    def gates(here):
        forget_s[here, :] = forget_gate(cf_ref, here, vec_ref, layer)

    chunks(cf_ref.shape[0], 64, gates)

    @pl.when(step == 0)
    def _():
        tot_ref[0] = jnp.ones_like(tot_ref[0])
        tot_ref[1] = jnp.zeros_like(tot_ref[1])

    def one(at, state):
        forget = forget_s[at, :]
        decay = forget * widen(keep_ref[at, :], width)
        return state[0] * decay, state[1] * decay + (1.0 - forget) * cf_ref[at, :width]

    product, state = over_time(one, (tot_ref[0], tot_ref[1]))
    tot_ref[0] = product
    tot_ref[1] = state


def gather_rows(per, group, place, step, pieces, order_ref, held, whole_ref):
    half = group // 2
    other = (step // per) ^ place[1]
    for side in range(2):

        @pl.when(other == side)
        def _():
            for k in range(half):
                for i in range(2):
                    held[place[2] ^ k, i] = pieces[2 * (side * half + k) + i][...]

    def put(here, value):
        whole_ref[here, :] = value.astype(BF16)

    to_time(order_ref, held[...].reshape(-1, STEPS, whole_ref.shape[1]), put)


def gather_features(per, group, place, step, pieces, order_ref, held, whole_ref):
    half = group // 2
    width = whole_ref.shape[1] // group
    for side in range(2):

        @pl.when(step // per == side)
        def _():
            for k in range(group):
                at = (place[1] ^ (k // half)) * half + (place[2] ^ (k % half))
                whole_ref[:, quarter(at, width)] = pieces[2 * k + side][...]


def project(place, layer, pieces, matrix, order, keep, vectors, rows, by_rows):
    model, both = matrix.shape
    width = both // 2
    tokens = keep.shape[0]
    block = rows * STEPS
    count = tokens // block
    per = count // 2
    group = model // width
    half = group // 2
    specs = []
    for k in range(group):
        for side in range(2):
            if by_rows:

                def index(i, place, needed=k // half):
                    mine = ((i // per) ^ place[1]) == needed
                    return (jnp.where(mine, i % per, 0), 0)

                specs.append(pl.BlockSpec((STEPS, model), index))
            elif side == 0:
                specs.append(
                    pl.BlockSpec((block, width), lambda i, place: (jnp.minimum(i, per - 1), 0))
                )
            else:
                specs.append(
                    pl.BlockSpec((block, width), lambda i, place: (jnp.maximum(i - per, 0), 0))
                )
    gather = functools.partial(gather_rows if by_rows else gather_features, per, group)
    held = pltpu.VMEM((half, 2, STEPS, model) if by_rows else (2 * SUBLANES, LANES), BF16)
    return run(
        functools.partial(project_kernel, layer, gather, len(pieces)),
        "project",
        (count,),
        [*pieces, matrix, order, keep, vectors],
        specs
        + [
            fixed_spec(model, both),
            fixed_spec(*order.shape),
            block_spec(block, LANES),
            fixed_spec(*vectors.shape),
        ],
        [
            shape_of(F32, tokens, both),
            shape_of(BF16, tokens, model),
            shape_of(F32, 2, rows, width),
        ],
        [block_spec(block, both), block_spec(block, model), fixed_spec(2, rows, width)],
        [held, pltpu.VMEM((block, width), F32)],
        place,
        (2 * tokens * model * both, 4 * tokens * model + 4 * tokens * both + 2 * model * both),
    )


def reset_kernel(x_ref, w_ref, out_ref):
    out_ref[...] = jnp.dot(x_ref[...], w_ref[...], preferred_element_type=F32)


def reset_product(whole, matrix):
    tokens, model = whole.shape
    width = matrix.shape[1]
    block = tokens // 4
    return run(
        reset_kernel,
        "reset_product",
        (4,),
        [whole, matrix],
        [block_spec(block, model), fixed_spec(model, width)],
        shape_of(F32, tokens, width),
        block_spec(block, width),
        cost=(2 * tokens * model * width, 2 * tokens * model + 4 * tokens * width),
    )


def carry_forward(layer, cf_ref, keep_ref, vec_ref, far, carry_s, forget_s, prev_ref, state_s):
    width = prev_ref.shape[1]

    def gates(here):
        forget_s[here, :] = forget_gate(cf_ref, here, vec_ref, layer)

    chunks(forget_s.shape[0], 64, gates)

    @pl.when(pl.program_id(0) == 0)
    def _():
        first = incoming(far)
        carry_s[...] = jnp.zeros_like(carry_s) if first is None else first

    def one(at, state):
        forget = forget_s[at, :]
        prev = widen(keep_ref[at, :], width) * state
        new = forget * prev + (1.0 - forget) * cf_ref[at, :width]
        prev_ref[at, :] = prev
        state_s[at, :] = new
        return new

    carry_s[...] = over_time(one, carry_s[...])


def reset_gate(layer, ur_ref, prev_ref, here, vec_ref):
    return jax.nn.sigmoid(
        ur_ref[here, :]
        + row_at(vec_ref, layer, PEEP) * prev_ref[here, :]
        + row_at(vec_ref, layer, RESET)
    )


def advance_kernel(layer, cf_ref, ur_ref, x_ref, keep_ref, order_ref, vec_ref, *refs):
    xn_ref, stat_ref, carry_s, forget_s, prev_s, state_s, x_s = refs[-7:]
    far = refs[:-7]
    block, width = xn_ref.shape

    def put(here, value):
        x_s[here, :] = value

    to_time(order_ref, x_ref[0], put)
    carry_forward(layer, cf_ref, keep_ref, vec_ref, far, carry_s, forget_s, prev_s, state_s)

    def finish(here):
        gate = reset_gate(layer, ur_ref, prev_s, here, vec_ref)
        xn = gate * state_s[here, :] + (1.0 - gate) * x_s[here, :]
        xn_ref[here, :] = xn
        mean = jnp.mean(xn, axis=-1, keepdims=True)
        off = xn - mean
        spread = sum(off[:, j : j + LANES] * off[:, j : j + LANES] for j in range(0, width, LANES))
        x_s[here, :LANES] = jnp.broadcast_to(mean, (here.size, LANES))
        state_s[here, :LANES] = spread

    chunks(block, 64, finish)
    for b in range(block // LANES):
        here = slice(b * LANES, (b + 1) * LANES)
        row = pl.ds(pl.program_id(0) * (block // LANES) + b, 1)
        stat_ref[0, row, :] = x_s[here, :LANES].T[0:1, :]
        stat_ref[1, row, :] = jnp.sum(state_s[here, :LANES].T, axis=0, keepdims=True)


def advance(layer, cf, ur, x, keep, order, vectors, far):
    tokens, width = ur.shape
    _, rows, span, _ = x.shape
    block = rows * STEPS
    part = block_spec(block, width)
    return run(
        functools.partial(advance_kernel, layer),
        "advance",
        (tokens // block,),
        [cf, ur, x, keep, order, vectors, *far],
        [
            block_spec(block, 2 * width),
            part,
            rows_spec(rows, width, span // STEPS),
            block_spec(block, LANES),
            fixed_spec(*order.shape),
            fixed_spec(*vectors.shape),
        ]
        + [fixed_spec(2, rows, width)] * len(far),
        [shape_of(F32, tokens, width), shape_of(F32, 2, tokens // LANES, LANES)],
        [part, fixed_spec(2, tokens // LANES, LANES)],
        [pltpu.VMEM((rows, width), F32)] + [pltpu.VMEM((block, width), F32)] * 4,
        None,
        (60 * tokens * width, 22 * tokens * width),
    )


def middle_norm_kernel(layer, model, xn_ref, stat_ref, vec_ref, a_ref, b_ref, mean_ref, scale_ref):
    group = stat_ref.shape[0]
    block, width = xn_ref.shape
    for b in range(block // LANES):
        row = pl.ds(pl.program_id(0) * (block // LANES) + b, 1)
        here = slice(b * LANES, (b + 1) * LANES)
        means = [stat_ref[s, 0, row, :] for s in range(group)]
        mean = sum(means) / group
        square = sum(stat_ref[s, 1, row, :] for s in range(group))
        between = sum((part - mean) * (part - mean) for part in means)
        scale = lax.rsqrt((square + between * width) / model + 1e-05)
        mean_ref[here, :] = jnp.broadcast_to(mean, (LANES, LANES)).T
        scale_ref[here, :] = jnp.broadcast_to(scale, (LANES, LANES)).T

    per = pl.num_programs(0) // 2
    for side, normed_ref in enumerate((a_ref, b_ref)):

        @pl.when(pl.program_id(0) // per == side)
        def _():
            def part(here):
                normed_ref[here, :] = (
                    (xn_ref[here, :] - widen(mean_ref[here, :], width))
                    * widen(scale_ref[here, :], width)
                    * row_at(vec_ref, layer, GAIN)
                    + row_at(vec_ref, layer, BIAS)
                ).astype(BF16)

            chunks(block, 64, part)


def middle_norm(layer, model, xn, stats, vectors, rows):
    tokens, width = xn.shape
    block = rows * STEPS
    per = tokens // block // 2
    return run(
        functools.partial(middle_norm_kernel, layer, model),
        "middle_norm",
        (tokens // block,),
        [xn, stats, vectors],
        [block_spec(block, width), fixed_spec(*stats.shape), fixed_spec(*vectors.shape)],
        [shape_of(BF16, tokens // 2, width)] * 2 + [shape_of(F32, tokens, LANES)] * 2,
        [
            pl.BlockSpec((block, width), lambda i, *_: (jnp.minimum(i, per - 1), 0)),
            pl.BlockSpec((block, width), lambda i, *_: (jnp.maximum(i - per, 0), 0)),
        ]
        + [block_spec(block, LANES)] * 2,
        cost=(10 * tokens * width, 8 * tokens * width),
    )


def add_total(decay_s, drive_s, tot_ref):
    @pl.when(pl.program_id(0) == 0)
    def _():
        tot_ref[0] = jnp.ones_like(tot_ref[0])
        tot_ref[1] = jnp.zeros_like(tot_ref[1])

    def one(at, state):
        return state[0] * decay_s[at, :], state[1] + state[0] * drive_s[at, :]

    product, total = over_time(one, (tot_ref[0], tot_ref[1]))
    tot_ref[0] = product
    tot_ref[1] = total


def turn_kernel(layer, cf_ref, ur_ref, x_ref, dh_ref, keep_ref, order_ref, back_ref, vec_ref, *refs):
    prev_ref, dr_ref, dc_ref, high_ref, out_ref, du_ref, tot_ref, small_ref = refs[-14:-6]
    carry_s, forget_s, state_s, dh_s, drive_s, out_s = refs[-6:]
    far = refs[:-14]
    block, width = prev_ref.shape

    def put(here, value):
        dh_s[here, :] = value

    to_time(order_ref, dh_ref[0], put)
    carry_forward(layer, cf_ref, keep_ref, vec_ref, far, carry_s, forget_s, prev_ref, state_s)

    @pl.when(pl.program_id(0) == 0)
    def _():
        small_ref[...] = jnp.zeros_like(small_ref)

    def finish(here):
        state = state_s[here, :]
        x = x_ref[here, :]
        dh = dh_s[here, :]
        prev = prev_ref[here, :]
        gate = reset_gate(layer, ur_ref, prev_ref, here, vec_ref)
        out_s[here, :] = (gate * state + (1.0 - gate) * x).astype(BF16)
        dr = dh * (state - x) * gate * (1.0 - gate)
        dc = dh * gate
        dr_ref[here, :] = dr
        dc_ref[here, :] = dc
        du_ref[here, :] = dr.astype(BF16)
        high_ref[here, :] = dh - dc
        keep = widen(keep_ref[here, :], width)
        decay = keep * forget_s[here, :]
        state_s[here, :] = decay
        drive_s[here, :] = keep * row_at(vec_ref, layer, PEEP) * dr + decay * dc
        small_ref[0] += fold(dr * prev)
        small_ref[1] += fold(dr)

    chunks(block, 32, finish)
    to_rows(back_ref, out_s, out_ref)
    add_total(state_s, drive_s, tot_ref)


def turn(layer, cf, ur, x, dh, keep, order, back, vectors, far):
    tokens, width = ur.shape
    _, rows, span, _ = dh.shape
    block = rows * STEPS
    part = block_spec(block, width)
    by_rows = rows_spec(rows, width, span // STEPS)
    return run(
        functools.partial(turn_kernel, layer),
        "turn",
        (tokens // block,),
        [cf, ur, x, dh, keep, order, back, vectors, *far],
        [
            block_spec(block, 2 * width),
            part,
            part,
            by_rows,
            block_spec(block, LANES),
            fixed_spec(*order.shape),
            fixed_spec(*back.shape),
            fixed_spec(*vectors.shape),
        ]
        + [fixed_spec(2, rows, width)] * len(far),
        [shape_of(F32, tokens, width)] * 4
        + [
            shape_of(BF16, *dh.shape),
            shape_of(BF16, tokens, width),
            shape_of(F32, 2, rows, width),
            shape_of(F32, 2, SUBLANES, width),
        ],
        [part] * 4
        + [by_rows, part, fixed_spec(2, rows, width), fixed_spec(2, SUBLANES, width)],
        [pltpu.VMEM((rows, width), F32)]
        + [pltpu.VMEM((block, width), F32)] * 4
        + [pltpu.VMEM((block, width), BF16)],
        None,
        (80 * tokens * width, 36 * tokens * width),
    )


def retreat_kernel(layer, sums, dc_ref, dr_ref, prev_ref, cf_ref, keep_ref, vec_ref, *refs):
    if sums:
        ur_ref, mixed_ref = refs[:2]
        du_ref, small_ref, stat_ref, carry_s, forget_s, total_s, sum_s, cross_s = refs[-8:]
        far = refs[2:-8]
    else:
        back_ref = refs[0]
        du_ref, rows_ref, small_ref, carry_s, forget_s, total_s = refs[-6:]
        far = refs[1:-6]
    block, width = prev_ref.shape
    peep = row_at(vec_ref, layer, PEEP)

    @pl.when(pl.program_id(0) == 0)
    def _():
        first = incoming(far)
        carry_s[...] = jnp.zeros_like(carry_s) if first is None else first
        small_ref[...] = jnp.zeros_like(small_ref)

    def gates(here):
        forget_s[here, :] = forget_gate(cf_ref, here, vec_ref, layer)

    chunks(block, 64, gates)

    def one(at, state):
        total = dc_ref[at, :] + state
        total_s[at, :] = total
        return widen(keep_ref[at, :], width) * (peep * dr_ref[at, :] + forget_s[at, :] * total)

    carry_s[...] = over_time(one, carry_s[...], True)

    def halves(value):
        return sum(value[:, j : j + LANES] for j in range(0, width, LANES))

    def finish(here):
        forget = forget_s[here, :]
        slow = total_s[here, :] * (1.0 - forget)
        d_forget = slow * forget * (prev_ref[here, :] - cf_ref[here, :width])
        d_cand = slow.astype(BF16)
        d_gate = d_forget.astype(BF16)
        du_ref[here, :width] = d_cand
        du_ref[here, width:] = d_gate
        small_ref[...] += fold(d_forget)
        if sums:
            parts = [d_cand, d_gate, dr_ref[here, :].astype(BF16)]
            inputs = [cf_ref[here, :width], cf_ref[here, width:], ur_ref[here, :]]
            plain = cross = 0.0
            for third in range(3):
                at = slice(third * width, (third + 1) * width)
                du = parts[third].astype(F32)
                plain = plain + du * mixed_ref[0:1, at]
                cross = cross + du * (inputs[third] - mixed_ref[1:2, at])
            sum_s[here, :] = halves(plain)
            cross_s[here, :] = halves(cross)

    chunks(block, 32, finish)
    if sums:
        base = (pl.num_programs(0) - 1 - pl.program_id(0)) * (block // LANES)
        for b in range(block // LANES):
            here = slice(b * LANES, (b + 1) * LANES)
            stat_ref[0, pl.ds(base + b, 1), :] = jnp.sum(sum_s[here, :].T, axis=0, keepdims=True)
            stat_ref[1, pl.ds(base + b, 1), :] = jnp.sum(cross_s[here, :].T, axis=0, keepdims=True)
    else:
        to_rows(back_ref, du_ref, rows_ref)


def retreat(layer, dc, dr, prev, cf, keep, vectors, far, rows, span, awaited, back=None, ur=None, mixed=None):
    tokens, width = dc.shape
    block = rows * STEPS
    count = tokens // block
    sums = back is None
    part = turned_spec(block, width, count)
    both = turned_spec(block, 2 * width, count)
    rows_out = rows_spec(rows, 2 * width, span // STEPS, lambda i: count - 1 - i)
    outs = [shape_of(BF16, tokens, 2 * width)]
    specs = [both]
    scratch = [pltpu.VMEM((rows, width), F32)] + [pltpu.VMEM((block, width), F32)] * 2
    if sums:
        more, more_specs = [ur, mixed], [part, fixed_spec(*mixed.shape)]
        outs += [shape_of(F32, SUBLANES, width), shape_of(F32, 2, tokens // LANES, LANES)]
        specs += [fixed_spec(SUBLANES, width), fixed_spec(2, tokens // LANES, LANES)]
        scratch += [pltpu.VMEM((block, LANES), F32)] * 2
    else:
        more, more_specs = [back], [fixed_spec(*back.shape)]
        outs += [shape_of(BF16, 2, rows, span, 2 * width), shape_of(F32, SUBLANES, width)]
        specs += [rows_out, fixed_spec(SUBLANES, width)]
    return run(
        functools.partial(retreat_kernel, layer, sums),
        "retreat",
        (count,),
        [dc, dr, prev, cf, keep, vectors, *more, *far],
        [part] * 3
        + [both, turned_spec(block, LANES, count), fixed_spec(*vectors.shape)]
        + more_specs
        + [fixed_spec(2, rows, width)] * len(far),
        outs,
        specs,
        scratch,
        None,
        (60 * tokens * width, 30 * tokens * width),
        awaited,
    )


def back_product(pair, reset, w_pair, w_reset):
    contract = (((1,), (1,)), ((), ()))
    return lax.dot_general(pair, w_pair, contract, preferred_element_type=F32) + lax.dot_general(
        reset, w_reset, contract, preferred_element_type=F32
    )


def back_features_kernel(odd, order, pair_ref, reset_ref, wp_ref, wr_ref, odd_ref, even_ref):
    k = pl.program_id(0)
    share = back_product(pair_ref[...], reset_ref[...], wp_ref[...], wr_ref[...])

    @pl.when(k < odd)
    def _():
        odd_ref[0] = share.astype(BF16)

    @pl.when(k >= odd)
    def _():
        even_ref[0] = share


def back_features(order, odd, pair, reset, w_pair, w_reset, awaited):
    tokens, width = reset.shape
    count = order.shape[0]
    by_order = lambda k, order: (order[k], 0)
    return run(
        functools.partial(back_features_kernel, odd),
        "back_features",
        (count,),
        [pair, reset, w_pair, w_reset],
        [
            fixed_spec(*pair.shape),
            fixed_spec(*reset.shape),
            pl.BlockSpec((width, 2 * width), by_order),
            pl.BlockSpec((width, width), by_order),
        ],
        [shape_of(BF16, odd, tokens, width), shape_of(F32, count - odd, tokens, width)],
        [
            pl.BlockSpec((1, tokens, width), lambda k, order: (jnp.minimum(k, odd - 1), 0, 0)),
            pl.BlockSpec((1, tokens, width), lambda k, order: (jnp.maximum(k - odd, 0), 0, 0)),
        ],
        (),
        order,
        (6 * count * tokens * width * width, 8 * count * tokens * width),
        awaited,
    )


def back_tokens_kernel(odd, order, pair_ref, reset_ref, wp_ref, wr_ref, odd_ref, even_ref):
    k = pl.program_id(0)
    local = odd_ref.shape[1]
    pair = pair_ref[0].reshape(local, pair_ref.shape[-1])
    reset = reset_ref[0].reshape(local, reset_ref.shape[-1])
    share = back_product(pair, reset, wp_ref[...], wr_ref[...])

    @pl.when(k < odd)
    def _():
        odd_ref[0] = share.astype(BF16)

    @pl.when(k >= odd)
    def _():
        even_ref[0] = share


def back_tokens(order, odd, pair, reset, w_pair, w_reset, awaited):
    two, rows, span, width = reset.shape
    model = w_pair.shape[0]
    count = order.shape[0]
    half = model // width // 2
    rows_dev = rows // half
    local = rows_dev * span
    by_order = lambda k, order: (order[k] // half, order[k] % half, 0, 0)
    return run(
        functools.partial(back_tokens_kernel, odd),
        "back_tokens",
        (count,),
        [pair, reset, w_pair, w_reset],
        [
            pl.BlockSpec((1, rows_dev, span, 2 * width), by_order),
            pl.BlockSpec((1, rows_dev, span, width), by_order),
            fixed_spec(*w_pair.shape),
            fixed_spec(*w_reset.shape),
        ],
        [shape_of(BF16, odd, local, model), shape_of(F32, count - odd, local, model)],
        [
            pl.BlockSpec((1, local, model), lambda k, order: (jnp.minimum(k, odd - 1), 0, 0)),
            pl.BlockSpec((1, local, model), lambda k, order: (jnp.maximum(k - odd, 0), 0, 0)),
        ],
        (),
        order,
        (6 * count * local * model * width, 8 * count * local * model),
        awaited,
    )


def middle_back_kernel(layer, model, *refs):
    (
        kept_ref, core_ref, pair_ref, line_ref, high_ref, x_ref, mean_ref, scale_ref, stat_ref,
        cf_ref, ur_ref, below_x_ref, keep_ref, order_ref, back_ref, vec_ref,
    ) = refs[:16]
    (
        prev_ref, dr_ref, dc_ref, below_ref, du_ref, rows_ref, tot_ref, small_ref,
        carry_s, forget_s, state_s, drive_s, x_s, plain_s, cross_s, below_s,
    ) = refs[-16:]
    far = refs[16:-16]
    block, width = prev_ref.shape
    below = layer - 1

    def put(here, value):
        x_s[here, :] = value

    to_time(order_ref, below_x_ref[0], put)
    carry_forward(below, cf_ref, keep_ref, vec_ref, far, carry_s, forget_s, prev_ref, state_s)
    for b in range(block // LANES):
        row = pl.ds(pl.program_id(0) * (block // LANES) + b, 1)
        here = slice(b * LANES, (b + 1) * LANES)
        for s, out in enumerate((plain_s, cross_s)):
            out[here, :] = jnp.broadcast_to(stat_ref[s, row, :] / model, (LANES, LANES)).T

    @pl.when(pl.program_id(0) == 0)
    def _():
        small_ref[...] = jnp.zeros_like(small_ref)

    def finish(here):
        back = (
            kept_ref[0, here, :]
            + core_ref[0, here, :].astype(F32)
            + pair_ref[here, :].astype(F32)
            + line_ref[here, :].astype(F32)
        )
        scale = widen(scale_ref[here, :], width)
        xhat = (x_ref[here, :] - widen(mean_ref[here, :], width)) * scale
        dh = high_ref[here, :] + scale * (
            back * row_at(vec_ref, layer, GAIN)
            - widen(plain_s[here, :], width)
            - xhat * widen(cross_s[here, :], width)
        )
        small_ref[0] += fold(back * xhat)
        small_ref[1] += fold(back)
        gate = reset_gate(below, ur_ref, prev_ref, here, vec_ref)
        dr = dh * (state_s[here, :] - x_s[here, :]) * gate * (1.0 - gate)
        dc = dh * gate
        dr_ref[here, :] = dr
        dc_ref[here, :] = dc
        du_ref[here, :] = dr.astype(BF16)
        below_s[here, :] = (dh - dc).astype(BF16)
        keep = widen(keep_ref[here, :], width)
        decay = keep * forget_s[here, :]
        state_s[here, :] = decay
        drive_s[here, :] = keep * row_at(vec_ref, below, PEEP) * dr + decay * dc
        small_ref[2] += fold(dr * prev_ref[here, :])
        small_ref[3] += fold(dr)

    chunks(block, 32, finish)
    to_rows(back_ref, below_s, below_ref)
    to_rows(back_ref, du_ref, rows_ref)
    add_total(state_s, drive_s, tot_ref)


def middle_back(
    layer, model, kept, core, pair, line, high, x, mean, scale, stats, cf, ur, below_x, keep, order,
    back, vectors, far,
):
    tokens, width = ur.shape
    _, rows, span, _ = below_x.shape
    block = rows * STEPS
    part = block_spec(block, width)
    top = pl.BlockSpec((1, block, width), lambda i, *_: (0, i, 0))
    thin = block_spec(block, LANES)
    by_rows = rows_spec(rows, width, span // STEPS)
    held = pltpu.VMEM((block, width), F32)
    return run(
        functools.partial(middle_back_kernel, layer, model),
        "middle_back",
        (tokens // block,),
        [
            kept, core, pair, line, high, x, mean, scale, stats, cf, ur, below_x, keep, order, back,
            vectors, *far,
        ],
        [top, top, part, part, part, part, thin, thin, fixed_spec(*stats.shape)]
        + [
            block_spec(block, 2 * width),
            part,
            by_rows,
            thin,
            fixed_spec(*order.shape),
            fixed_spec(*back.shape),
            fixed_spec(*vectors.shape),
        ]
        + [fixed_spec(2, rows, width)] * len(far),
        [shape_of(F32, tokens, width)] * 3
        + [
            shape_of(BF16, 2, rows, span, width),
            shape_of(BF16, tokens, width),
            shape_of(BF16, 2, rows, span, width),
            shape_of(F32, 2, rows, width),
            shape_of(F32, 4, SUBLANES, width),
        ],
        [part, part, part, by_rows, part, by_rows]
        + [fixed_spec(2, rows, width), fixed_spec(4, SUBLANES, width)],
        [pltpu.VMEM((rows, width), F32)]
        + [held] * 4
        + [pltpu.VMEM((block, LANES), F32)] * 2
        + [pltpu.VMEM((block, width), BF16)],
        None,
        (80 * tokens * width, 44 * tokens * width),
    )


def first_back_kernel(kept_ref, core_ref, pair_ref, line_ref, x_ref, gain_ref, high_ref, out_ref, small_ref):
    local, model = x_ref.shape
    group, _, width = high_ref.shape
    small_ref[...] = jnp.zeros_like(small_ref)

    def part(here):
        wide = x_ref[here, :].astype(F32)
        centered = wide - jnp.mean(wide, axis=-1, keepdims=True)
        scale = lax.rsqrt(jnp.mean(centered * centered, axis=-1, keepdims=True) + 1e-05)
        xhat = centered * scale
        back = (
            kept_ref[0, here, :]
            + core_ref[0, here, :].astype(F32)
            + pair_ref[here, :].astype(F32)
            + line_ref[here, :].astype(F32)
        )
        scaled = back * gain_ref[0:1, :]
        small_ref[0] += fold(back * xhat)
        small_ref[1] += fold(back)
        total = scale * (
            scaled
            - jnp.mean(scaled, axis=-1, keepdims=True)
            - xhat * jnp.mean(scaled * xhat, axis=-1, keepdims=True)
        )
        for s in range(group):
            columns = slice(s * width, (s + 1) * width)
            out_ref[here, columns] = (total[:, columns] + high_ref[s, here, :].astype(F32)).astype(
                BF16
            )

    chunks(local, 16, part)


def first_back(kept, core, pair, line, x, gain, high):
    local, model = x.shape
    top = pl.BlockSpec((1, local, model), lambda i, *_: (0, 0, 0))
    flat = fixed_spec(local, model)
    return run(
        first_back_kernel,
        "first_back",
        (1,),
        [kept, core, pair, line, x, gain, high],
        [top, top, flat, flat, flat, fixed_spec(*gain.shape), fixed_spec(*high.shape)],
        [shape_of(BF16, local, model), shape_of(F32, 2, SUBLANES, model)],
        [flat, fixed_spec(2, SUBLANES, model)],
        cost=(30 * local * model, 16 * local * model),
    )


def weight_kernel(whole_ref, pair_ref, reset_ref, out_ref):
    both = pair_ref.shape[1]
    contract = (((0,), (0,)), ((), ()))
    for du_ref, at in ((pair_ref, slice(0, both)), (reset_ref, slice(both, out_ref.shape[1]))):
        out_ref[:, at] = lax.dot_general(
            whole_ref[...], du_ref[...], contract, preferred_element_type=F32
        ).astype(BF16)


def weight_term(whole, pair, reset, awaited=()):
    tokens, model = whole.shape
    width = reset.shape[1]
    block = model // 4
    return run(
        weight_kernel,
        "weight_term",
        (4,),
        [whole, pair, reset],
        [
            pl.BlockSpec((tokens, block), lambda k, *_: (0, k)),
            fixed_spec(*pair.shape),
            fixed_spec(*reset.shape),
        ],
        shape_of(BF16, model, 3 * width),
        block_spec(block, 3 * width),
        cost=(6 * tokens * model * width, 2 * tokens * model + 6 * model * width),
        awaited=awaited,
    )


def join_kernel(x_ref, out_ref):
    group, rows, width = x_ref.shape
    for s in range(group):
        out_ref[:, s * width : (s + 1) * width] = x_ref[s]


def join(value):
    group, rows, width = value.shape
    return run(
        join_kernel,
        "join",
        (1,),
        [value],
        [fixed_spec(group, rows, width)],
        shape_of(value.dtype, rows, group * width),
        fixed_spec(rows, group * width),
        cost=(0, 4 * rows * group * width),
    )


def join_weights_kernel(*refs):
    out_ref = refs[-1]
    for layer, part_ref in enumerate(refs[:-1]):
        group, shard, total = part_ref.shape
        width = total // 3
        for s in range(group):
            for third in range(3):
                start = third * group * width + s * width
                at = slice(third * width, (third + 1) * width)
                out_ref[layer, :, start : start + width] = part_ref[s, :, at].astype(F32)


def join_weights(parts):
    group, shard, total = parts[0].shape
    shape = (len(parts), shard, group * total)
    return run(
        join_weights_kernel,
        "join_weights",
        (1,),
        parts,
        [fixed_spec(*part.shape) for part in parts],
        shape_of(F32, *shape),
        fixed_spec(*shape),
        cost=(0, 12 * group * shard * total),
    )


def swap(value, bits, size):
    return lax.ppermute(value, GROUP, [(i, i ^ bits) for i in range(size)])


def gather_group(a, b, size):
    pair_a = swap(a, PAIR, size)
    line_b = swap(b, LINE, size)
    a, b = after([a, b], pair_a, line_b)
    pair_b = swap(b, PAIR, size)
    line_a = swap(a, LINE, size)
    far_a = swap(pair_a, LINE, size)
    far_b = swap(line_b, PAIR, size)
    halves = [a, b, line_a, line_b, pair_a, pair_b, far_a, far_b]
    cores = [swap(half, CORE, size) for half in halves]
    return [
        half
        for k in range(0, 8, 2)
        for half in (halves[k], halves[k + 1], cores[k], cores[k + 1])
    ]


def reduce_group(shares, size, first, early, meanwhile):
    far_odd, far_even = shares((7, 6), 1, first)
    far_core = swap(far_odd, CORE, size)
    other = meanwhile((far_odd,))
    far = (far_even[0] + far_core[0].astype(F32)).astype(BF16)
    half = far.shape[0] // 2
    far_a, far_b = after([far[:half], far[half:]], *early, *other)
    by_pair = swap(far_a, PAIR, size)
    by_line = swap(far_b, LINE, size)
    side_odd, side_even = shares((5, 3, 4, 2), 2, (far_a, far_b))
    side_core = swap(side_odd, CORE, size)
    own_odd, own_even = shares((1, 0), 1, (side_odd,))
    own_core = swap(own_odd, CORE, size)
    sides = side_even + side_core.astype(F32)
    zeros = jnp.zeros_like(by_pair)
    pair = (sides[0] + jnp.concatenate([zeros, by_line]).astype(F32)).astype(BF16)
    line = (sides[1] + jnp.concatenate([by_pair, zeros]).astype(F32)).astype(BF16)
    sent = (pair, line)
    pair = swap(pair, PAIR, size)
    line = swap(line, LINE, size)
    return own_even, own_core, pair, line, sent


def sum_group(value, size):
    value = value + swap(value, CORE, size)
    return value + sum(swap(value, bits, size) for bits in (LINE, PAIR, LINE | PAIR))


def exchange(part, size, reverse):
    far = []
    for hop in range(1, size):
        pairs = [(i, i + hop) for i in range(size - hop)]
        if reverse:
            pairs = [(b, a) for a, b in pairs]
        far.append(lax.ppermute(part, "ring", pairs))
    return far


def spread_small(vectors, ring, half, awaited):
    size = 2 * ring * half
    axes = ("ring", "pair", "rows")
    me = lax.axis_index(axes)
    bit = size // 2
    while bit:
        if bit == half // 2:
            (vectors,) = after([vectors], *awaited)
        width = vectors.shape[1] // 2
        mine = jnp.where((me & bit) > 0, 1, 0)
        send = lax.dynamic_slice_in_dim(vectors, (1 - mine) * width, width, 1)
        hold = lax.dynamic_slice_in_dim(vectors, mine * width, width, 1)
        vectors = hold + lax.ppermute(send, axes, [(i, i ^ bit) for i in range(size)])
        bit //= 2
    return vectors


def order_matrix(rows):
    index = np.arange(rows * SUB)
    return (index % rows * SUB + index // rows)[:, None] == index[None, :]


def to_group(value):
    return lax.all_to_all(value, GROUP, split_axis=0, concat_axis=0, tiled=True)


def body(
    inputs,
    out_grad,
    reset_flags,
    weights,
    ln_gain,
    layer_norm_bias,
    reset_peep,
    forget_bias,
    reset_bias,
):
    rows_dev, span, model = inputs.shape
    layers, shard, _ = weights.shape
    ring = lax.axis_size("ring")
    half = lax.axis_size("rows")
    group = 2 * half
    place = jnp.stack([lax.axis_index("ring"), lax.axis_index("pair"), lax.axis_index("rows")])
    place = place.astype(jnp.int32)
    me = lax.axis_index(GROUP)
    width = model // group
    rows = rows_dev * half
    local = rows_dev * span
    tokens = 2 * rows * span
    order = jnp.asarray(order_matrix(rows), BF16)
    back = jnp.asarray(order_matrix(rows).T, BF16)

    def gather_columns(value):
        value = value.reshape(group * shard, 3 * width)
        return [
            lax.all_gather(part, "ring", axis=0, tiled=True)
            for part in (value[:, : 2 * width], value[:, 2 * width :])
        ]

    flags = jnp.pad(reset_flags.astype(BF16), ((0, 2 * SUBLANES - rows_dev), (0, 0)))
    mine = to_group(columns_of(weights, 0, group, width, (flags,)))
    pair_w1, reset_w1 = gather_columns(mine[:, :shard])
    flags = mine[:, shard : shard + rows_dev, :span].reshape(2, rows, span)
    keep = (1.0 - flags.astype(F32)).transpose(0, 2, 1).reshape(tokens, 1)
    keep = jnp.broadcast_to(keep, (tokens, LANES))
    *normed, split = first_norm(inputs, ln_gain, layer_norm_bias, group, (mine,))
    vectors = jnp.stack([ln_gain, layer_norm_bias, reset_peep, forget_bias, reset_bias], axis=1)
    vectors = lax.dynamic_slice_in_dim(vectors.reshape(layers * 5, model), me * width, width, 1)
    vectors = jnp.pad(vectors, ((0, 16 - layers * 5), (0, 0)))
    pieces1 = gather_group(*normed, group)

    cf1, whole1, part = project(place, 0, pieces1, pair_w1, order, keep, vectors, rows, True)
    far1 = exchange(part, ring, False)
    columns, split = after([columns_of(weights, 1, group, width, (), (mine,)), split], *far1)
    pair_w2, reset_w2 = gather_columns(to_group(columns))
    x1 = to_group(split).reshape(2, rows, span, width)
    ur1 = reset_product(whole1, reset_w1)
    (gradient,) = after([out_grad.reshape(local, group, width).swapaxes(0, 1)], ur1)
    gradient = to_group(gradient).reshape(2, rows, span, width)
    x2, stats = advance(0, cf1, ur1, x1, keep, order, vectors, far1)
    (stats,) = after([stats], gradient)
    stats = lax.all_gather(stats, GROUP)
    *normed, mean2, scale2 = middle_norm(1, model, x2, stats, vectors, rows)

    def mixed():
        def thirds(value):
            high = value.astype(BF16)
            middle = (value - high.astype(F32)).astype(BF16)
            low = (value - high.astype(F32) - middle.astype(F32)).astype(BF16)
            return [high, middle, low]

        lines = jnp.stack(thirds(ln_gain[1]) + thirds(layer_norm_bias[1]))
        lines = jnp.pad(lines, ((0, 10), (0, 0)))
        both = jnp.concatenate(
            [jnp.dot(lines, w, preferred_element_type=F32) for w in (pair_w2, reset_w2)], axis=1
        )
        return jnp.pad(jnp.sum(both[:6].reshape(2, 3, 3 * width), axis=1), ((0, 6), (0, 0)))

    pieces2 = gather_group(*normed, group)

    cf2, whole2, part = project(place, 1, pieces2, pair_w2, order, keep, vectors, rows, False)
    far = exchange(part, ring, False)
    ur2 = reset_product(whole2, reset_w2)
    prev2, dr2, dc2, high2, out, du_r2, part, sums2 = turn(
        1, cf2, ur2, x2, gradient, keep, order, back, vectors, far
    )
    far = exchange(part, ring, True)

    def scatter(term):
        return lax.psum_scatter(term, "ring", scatter_dimension=0, tiled=True)

    (out,) = after([out.reshape(group, local, width)], *far)
    out = to_group(out)
    du_p2, forget2, stats = retreat(
        1, dc2, dr2, prev2, cf2, keep, vectors, far, rows, span, (), ur=ur2, mixed=mixed()
    )
    outputs = join(out).reshape(rows_dev, span, model)

    def slices(slots):
        return jnp.stack([me ^ k for k in slots]).astype(jnp.int32)

    kept, core, pair, line, sent = reduce_group(
        lambda slots, odd, awaited: back_features(
            slices(slots), odd, du_p2, du_r2, pair_w2, reset_w2, awaited
        ),
        group,
        (out,),
        (),
        lambda awaited: (),
    )
    term2 = weight_term(whole2, du_p2, du_r2, sent)
    (stats,) = after([stats], term2)
    stats = sum_group(stats, group)
    (kept,) = after([kept], outputs)
    term2 = scatter(term2)

    prev1, dr1, dc1, high1, du_r1, rows_r1, part, sums1 = middle_back(
        1, model, kept, core, pair, line, high2, x2, mean2, scale2, stats, cf1, ur1, x1, keep,
        order, back, vectors, far1,
    )
    far = exchange(part, ring, True)
    (high1,) = after([high1.reshape(group, local, width)], *far)
    high = to_group(high1)
    du_p1, rows_p1, forget1 = retreat(
        0, dc1, dr1, prev1, cf1, keep, vectors, far, rows, span, (), back=back
    )
    first = []

    def weight_first(awaited):
        first.append(weight_term(whole1, du_p1, du_r1, awaited))
        return first

    kept, core, pair, line, sent = reduce_group(
        lambda slots, odd, awaited: back_tokens(
            slices(slots), odd, rows_p1, rows_r1, pair_w1, reset_w1, awaited
        ),
        group,
        (high,),
        (term2,),
        weight_first,
    )
    (term2,) = after([term2.reshape(group, shard, 3 * width)], pair, line)
    second = to_group(term2)
    first = to_group(scatter(first[0]).reshape(group, shard, 3 * width))
    input_grad, gains1 = first_back(
        kept, core, pair, line, inputs.reshape(local, model), ln_gain, high
    )
    input_grad = input_grad.reshape(rows_dev, span, model)
    weight_grad = join_weights([first, second])

    def total(value):
        return jnp.sum(value, axis=-2)

    sums1 = total(sums1)
    sums2 = total(sums2)
    narrow = jnp.stack(
        [
            sums1[2], total(forget1), sums1[3],
            sums1[0], sums1[1], sums2[0], total(forget2), sums2[1],
        ]
    )
    narrow = lax.dynamic_update_slice(jnp.zeros((8, model), F32), narrow, (0, me * width))
    small = jnp.concatenate([total(gains1), narrow])
    small = spread_small(small, ring, half, (first,)).reshape(2, 5, shard)
    return (outputs, input_grad, weight_grad) + tuple(small[:, i] for i in range(5))


def solution(mesh):
    ring = mesh.shape["tm"] // 2
    fine = Mesh(
        mesh.devices.reshape(ring, 2, mesh.shape["rows"]), ("ring", "pair", "rows")
    )
    tm = ("ring", "pair")
    everything = ("ring", "pair", "rows")
    return jax.shard_map(
        body,
        mesh=fine,
        in_specs=(
            P("rows", tm, None),
            P("rows", tm, None),
            P("rows", tm),
            P(None, everything, None),
            P(),
            P(),
            P(),
            P(),
            P(),
        ),
        out_specs=(
            P("rows", tm, None),
            P("rows", tm, None),
            P(None, everything, None),
            P(None, everything),
            P(None, everything),
            P(None, everything),
            P(None, everything),
            P(None, everything),
        ),
        check_vma=False,
    )
```

```python
import functools

import jax
import jax.numpy as jnp
import numpy as np
from jax import lax
from jax.experimental import pallas as pl
from jax.experimental.pallas import tpu as pltpu
from jax.sharding import Mesh
from jax.sharding import PartitionSpec as P

LANES = 128
SUBLANES = 8
STEPS = 64
SUB = 32
VMEM_BYTES = 58 * 1024 * 1024
GAIN, BIAS, PEEP, FORGET, RESET = range(5)
BF16 = jnp.bfloat16
F32 = jnp.float32
GROUP = ("pair", "rows")
CORE, LINE, PAIR = 1, 2, 4


def shape_of(dtype, *shape):
    return jax.ShapeDtypeStruct(shape, dtype)


def run(
    kernel, name, grid, ins, in_specs, outs, out_specs, scratch=(), place=None, cost=(0, 0), awaited=()
):
    scalars = 0 if place is None else 1
    first = scalars + len(ins)
    last = first + len(awaited)

    def body(*refs):
        kernel(*refs[:first], *refs[last:])

    function = pl.pallas_call(
        body,
        out_shape=outs,
        grid_spec=pltpu.PrefetchScalarGridSpec(
            num_scalar_prefetch=scalars,
            grid=grid,
            in_specs=list(in_specs) + [pl.BlockSpec(memory_space=pl.ANY)] * len(awaited),
            out_specs=out_specs,
            scratch_shapes=list(scratch),
        ),
        compiler_params=pltpu.CompilerParams(vmem_limit_bytes=VMEM_BYTES),
        cost_estimate=pl.CostEstimate(flops=cost[0], bytes_accessed=cost[1], transcendentals=0),
        name=name,
    )
    return function(*(() if place is None else (place,)), *ins, *awaited)


def quarter(index, width):
    return pl.ds(pl.multiple_of(index * width, width), width)


def fixed_spec(*shape):
    return pl.BlockSpec(shape, lambda *_: (0,) * len(shape))


def block_spec(block, width):
    return pl.BlockSpec((block, width), lambda i, *_: (i, 0))


def turned_spec(block, width, count):
    return pl.BlockSpec((block, width), lambda i, *_: (count - 1 - i, 0))


def rows_spec(rows, width, per, place_of=lambda i: i):
    return pl.BlockSpec(
        (1, rows, STEPS, width), lambda i, *_: (place_of(i) // per, 0, place_of(i) % per, 0)
    )


def split_spec(half, rows_dev, width, per, which):
    return pl.BlockSpec(
        (1, half, 1, rows_dev, STEPS, width), lambda i, *_: (i // per, 0, which, 0, i % per, 0)
    )


def row_at(vec_ref, layer, which):
    row = layer * 5 + which
    return vec_ref[row : row + 1, :]


def chunks(total, size, body, unroll=1):
    def one(i, carry):
        body(pl.ds(pl.multiple_of(i * size, size), size))
        return carry

    lax.fori_loop(0, total // size, one, 0, unroll=unroll)


def over_time(body, state, backward=False):
    def one(i, state):
        t = STEPS - 1 - i if backward else i
        return body(pl.ds(pl.multiple_of(t * SUBLANES, SUBLANES), SUBLANES), state)

    return lax.fori_loop(0, STEPS, one, state, unroll=8)


def widen(keep, width):
    return jnp.concatenate([keep] * (width // LANES), axis=1)


def incoming(far):
    state = None
    for ref in reversed(far):
        state = ref[1] if state is None else ref[0] * state + ref[1]
    return state


def exact(order, value):
    return jnp.dot(order, value, preferred_element_type=F32)


def to_time(order_ref, rows, put):
    block = order_ref.shape[0]
    for i in range(STEPS // SUB):
        part = rows[:, i * SUB : (i + 1) * SUB, :].reshape(block, rows.shape[-1])
        put(slice(i * block, (i + 1) * block), exact(order_ref[...], part))


def to_rows(back_ref, value_ref, out_ref):
    block = back_ref.shape[0]
    for i in range(STEPS // SUB):
        part = exact(back_ref[...], value_ref[i * block : (i + 1) * block, :])
        out_ref[0, :, i * SUB : (i + 1) * SUB, :] = part.astype(BF16).reshape(
            out_ref.shape[1], SUB, out_ref.shape[3]
        )


def forget_gate(cf_ref, here, vec_ref, layer):
    width = cf_ref.shape[1] // 2
    return jax.nn.sigmoid(cf_ref[here, width:] + row_at(vec_ref, layer, FORGET))


def fold(value):
    return jnp.sum(value.reshape(-1, SUBLANES, value.shape[-1]), axis=0)


def after(values, *awaited):
    count = len(values)

    def nothing(*refs):
        pass

    return pl.pallas_call(
        nothing,
        out_shape=[shape_of(v.dtype, *v.shape) for v in values],
        in_specs=[pl.BlockSpec(memory_space=pl.ANY)] * (count + len(awaited)),
        out_specs=[pl.BlockSpec(memory_space=pl.ANY)] * count,
        input_output_aliases={i: i for i in range(count)},
        name="after",
    )(*values, *awaited)


def columns_kernel(group, width, weights_ref, out_ref):
    for s in range(group):
        for third in range(3):
            start = third * group * width + s * width
            out_ref[s, :, third * width : (third + 1) * width] = weights_ref[
                0, :, start : start + width
            ]


def columns_of(weights, layer, group, width, awaited=()):
    _, shard, total = weights.shape
    return run(
        functools.partial(columns_kernel, group, width),
        "columns_of",
        (1,),
        [weights],
        [pl.BlockSpec((1, shard, total), lambda i, *_: (layer, 0, 0))],
        shape_of(BF16, group, shard, 3 * width),
        fixed_spec(group, shard, 3 * width),
        cost=(0, 4 * shard * total),
        awaited=awaited,
    )


def stack_columns_kernel(place, *refs):
    pieces, (pair_ref, reset_ref, flags_ref) = refs[:-3], refs[-3:]
    group = len(pieces)
    half = group // 2
    shard = pair_ref.shape[0] // group
    both = pair_ref.shape[1]
    for k in range(group):
        at = (place[1] ^ (k // half)) * half + (place[2] ^ (k % half))
        here = pl.ds(pl.multiple_of(at * shard, shard), shard)
        pair_ref[here, :] = pieces[k][:shard, :both]
        reset_ref[here, :] = pieces[k][:shard, both:]
        flags_ref[at] = pieces[k][shard:, :LANES]


def stack_columns(place, pieces, shard, awaited):
    group = len(pieces)
    rows, total = pieces[0].shape
    outs = [
        (group * shard, total // 3 * 2),
        (group * shard, total // 3),
        (group, rows - shard, LANES),
    ]
    return run(
        stack_columns_kernel,
        "stack_columns",
        (1,),
        pieces,
        [fixed_spec(rows, total)] * group,
        [shape_of(BF16, *out) for out in outs],
        [fixed_spec(*out) for out in outs],
        (),
        place,
        (0, 4 * group * shard * total),
        awaited,
    )


def send_columns_kernel(group, width, place, weights_ref, flags_ref, *outs):
    half = group // 2
    shard = weights_ref.shape[1]
    for k in range(group):
        at = (place[1] ^ (k // half)) * half + (place[2] ^ (k % half))
        for third in range(3):
            start = pl.multiple_of(third * group * width + at * width, width)
            outs[k][:shard, third * width : (third + 1) * width] = weights_ref[
                0, :, pl.ds(start, width)
            ]
        outs[k][shard:, :] = jnp.zeros_like(outs[k][shard:, :])
        outs[k][shard:, : flags_ref.shape[1]] = flags_ref[...]


def send_columns(place, weights, layer, group, width, flags):
    _, shard, total = weights.shape
    rows = shard + flags.shape[0]
    return run(
        functools.partial(send_columns_kernel, group, width),
        "send_columns",
        (1,),
        [weights, flags],
        [pl.BlockSpec((1, shard, total), lambda i, *_: (layer, 0, 0)), fixed_spec(*flags.shape)],
        [shape_of(BF16, rows, 3 * width)] * group,
        [fixed_spec(rows, 3 * width)] * group,
        (),
        place,
        (0, 4 * shard * total),
    )


def first_norm_kernel(group, x_ref, grad_ref, gain_ref, bias_ref, *refs):
    split_ref = refs[-1]
    rows, span, model = x_ref.shape
    width = model // group
    for i in range(rows):

        def part(here):
            wide = x_ref[i, here, :].astype(F32)
            centered = wide - jnp.mean(wide, axis=-1, keepdims=True)
            scale = lax.rsqrt(jnp.mean(centered * centered, axis=-1, keepdims=True) + 1e-05)
            refs[i][here, :] = (
                centered * scale * gain_ref[0:1, :] + bias_ref[0:1, :]
            ).astype(BF16)

        chunks(span, 16, part)
        for s in range(group):
            columns = slice(s * width, (s + 1) * width)
            split_ref[s, 0, i] = x_ref[i, :, columns]
            split_ref[s, 1, i] = grad_ref[i, :, columns]


def first_norm(x, grad, gain, bias, group, awaited):
    rows, span, model = x.shape
    split = (group, 2, rows, span, model // group)
    return run(
        functools.partial(first_norm_kernel, group),
        "first_norm",
        (1,),
        [x, grad, gain, bias],
        [fixed_spec(*a.shape) for a in (x, grad, gain, bias)],
        [shape_of(BF16, span, model)] * rows + [shape_of(BF16, *split)],
        [fixed_spec(span, model)] * rows + [fixed_spec(*split)],
        cost=(20 * rows * span * model, 8 * rows * span * model),
        awaited=awaited,
    )


def project_kernel(layer, gather, slots, place, *refs):
    pieces = refs[:slots]
    w_ref, order_ref, keep_ref, vec_ref = refs[slots : slots + 4]
    cf_ref, whole_ref, tot_ref, held, forget_s = refs[slots + 4 :]
    width = cf_ref.shape[1] // 2
    step = pl.program_id(0)
    gather(place, step, pieces, order_ref, held, whole_ref)
    cf_ref[...] = jnp.dot(whole_ref[...], w_ref[...], preferred_element_type=F32)

    def gates(here):
        forget_s[here, :] = forget_gate(cf_ref, here, vec_ref, layer)

    chunks(cf_ref.shape[0], 64, gates)

    @pl.when(step == 0)
    def _():
        tot_ref[0] = jnp.ones_like(tot_ref[0])
        tot_ref[1] = jnp.zeros_like(tot_ref[1])

    def one(at, state):
        forget = forget_s[at, :]
        decay = forget * widen(keep_ref[at, :], width)
        return state[0] * decay, state[1] * decay + (1.0 - forget) * cf_ref[at, :width]

    product, state = over_time(one, (tot_ref[0], tot_ref[1]))
    tot_ref[0] = product
    tot_ref[1] = state


def gather_rows(per, group, place, step, pieces, order_ref, held, whole_ref):
    half = group // 2
    other = (step // per) ^ place[1]
    for side in range(2):

        @pl.when(other == side)
        def _():
            for k in range(half):
                for i in range(2):
                    held[place[2] ^ k, i] = pieces[2 * (side * half + k) + i][...]

    def put(here, value):
        whole_ref[here, :] = value.astype(BF16)

    to_time(order_ref, held[...].reshape(-1, STEPS, whole_ref.shape[1]), put)


def gather_features(per, group, place, step, pieces, order_ref, held, whole_ref):
    half = group // 2
    width = whole_ref.shape[1] // group
    for side in range(2):

        @pl.when(step // per == side)
        def _():
            for k in range(group):
                at = (place[1] ^ (k // half)) * half + (place[2] ^ (k % half))
                whole_ref[:, quarter(at, width)] = pieces[2 * k + side][...]


def project(place, layer, pieces, matrix, order, keep, vectors, rows, by_rows):
    model, both = matrix.shape
    width = both // 2
    tokens = keep.shape[0]
    block = rows * STEPS
    count = tokens // block
    per = count // 2
    group = model // width
    half = group // 2
    specs = []
    for k in range(group):
        for side in range(2):
            if by_rows:

                def index(i, place, needed=k // half):
                    mine = ((i // per) ^ place[1]) == needed
                    return (jnp.where(mine, i % per, 0), 0)

                specs.append(pl.BlockSpec((STEPS, model), index))
            elif side == 0:
                specs.append(
                    pl.BlockSpec((block, width), lambda i, place: (jnp.minimum(i, per - 1), 0))
                )
            else:
                specs.append(
                    pl.BlockSpec((block, width), lambda i, place: (jnp.maximum(i - per, 0), 0))
                )
    gather = functools.partial(gather_rows if by_rows else gather_features, per, group)
    held = pltpu.VMEM((half, 2, STEPS, model) if by_rows else (2 * SUBLANES, LANES), BF16)
    return run(
        functools.partial(project_kernel, layer, gather, len(pieces)),
        "project",
        (count,),
        [*pieces, matrix, order, keep, vectors],
        specs
        + [
            fixed_spec(model, both),
            fixed_spec(*order.shape),
            block_spec(block, LANES),
            fixed_spec(*vectors.shape),
        ],
        [
            shape_of(F32, tokens, both),
            shape_of(BF16, tokens, model),
            shape_of(F32, 2, rows, width),
        ],
        [block_spec(block, both), block_spec(block, model), fixed_spec(2, rows, width)],
        [held, pltpu.VMEM((block, width), F32)],
        place,
        (2 * tokens * model * both, 4 * tokens * model + 4 * tokens * both + 2 * model * both),
    )


def reset_kernel(x_ref, w_ref, out_ref):
    out_ref[...] = jnp.dot(x_ref[...], w_ref[...], preferred_element_type=F32)


def reset_product(whole, matrix):
    tokens, model = whole.shape
    width = matrix.shape[1]
    block = tokens // 4
    return run(
        reset_kernel,
        "reset_product",
        (4,),
        [whole, matrix],
        [block_spec(block, model), fixed_spec(model, width)],
        shape_of(F32, tokens, width),
        block_spec(block, width),
        cost=(2 * tokens * model * width, 2 * tokens * model + 4 * tokens * width),
    )


def carry_forward(layer, cf_ref, keep_ref, vec_ref, far, carry_s, forget_s, prev_ref, state_s):
    width = prev_ref.shape[1]

    def gates(here):
        forget_s[here, :] = forget_gate(cf_ref, here, vec_ref, layer)

    chunks(forget_s.shape[0], 64, gates)

    @pl.when(pl.program_id(0) == 0)
    def _():
        first = incoming(far)
        carry_s[...] = jnp.zeros_like(carry_s) if first is None else first

    def one(at, state):
        forget = forget_s[at, :]
        prev = widen(keep_ref[at, :], width) * state
        new = forget * prev + (1.0 - forget) * cf_ref[at, :width]
        prev_ref[at, :] = prev
        state_s[at, :] = new
        return new

    carry_s[...] = over_time(one, carry_s[...])


def reset_gate(layer, ur_ref, prev_ref, here, vec_ref):
    return jax.nn.sigmoid(
        ur_ref[here, :]
        + row_at(vec_ref, layer, PEEP) * prev_ref[here, :]
        + row_at(vec_ref, layer, RESET)
    )


def advance_kernel(layer, cf_ref, ur_ref, x_ref, keep_ref, order_ref, vec_ref, *refs):
    xn_ref, stat_ref, carry_s, forget_s, prev_s, state_s, x_s = refs[-7:]
    far = refs[:-7]
    block, width = xn_ref.shape

    def put(here, value):
        x_s[here, :] = value

    to_time(order_ref, x_ref[...].reshape(-1, STEPS, width), put)
    carry_forward(layer, cf_ref, keep_ref, vec_ref, far, carry_s, forget_s, prev_s, state_s)

    def finish(here):
        gate = reset_gate(layer, ur_ref, prev_s, here, vec_ref)
        xn = gate * state_s[here, :] + (1.0 - gate) * x_s[here, :]
        xn_ref[here, :] = xn
        mean = jnp.mean(xn, axis=-1, keepdims=True)
        off = xn - mean
        spread = sum(off[:, j : j + LANES] * off[:, j : j + LANES] for j in range(0, width, LANES))
        x_s[here, :LANES] = jnp.broadcast_to(mean, (here.size, LANES))
        state_s[here, :LANES] = spread

    chunks(block, 64, finish)
    for b in range(block // LANES):
        here = slice(b * LANES, (b + 1) * LANES)
        row = pl.ds(pl.program_id(0) * (block // LANES) + b, 1)
        stat_ref[0, row, :] = x_s[here, :LANES].T[0:1, :]
        stat_ref[1, row, :] = jnp.sum(state_s[here, :LANES].T, axis=0, keepdims=True)


def advance(layer, cf, ur, x, keep, order, vectors, far):
    tokens, width = ur.shape
    _, half, _, rows_dev, span, _ = x.shape
    rows = half * rows_dev
    block = rows * STEPS
    part = block_spec(block, width)
    return run(
        functools.partial(advance_kernel, layer),
        "advance",
        (tokens // block,),
        [cf, ur, x, keep, order, vectors, *far],
        [
            block_spec(block, 2 * width),
            part,
            split_spec(half, rows_dev, width, span // STEPS, 0),
            block_spec(block, LANES),
            fixed_spec(*order.shape),
            fixed_spec(*vectors.shape),
        ]
        + [fixed_spec(2, rows, width)] * len(far),
        [shape_of(F32, tokens, width), shape_of(F32, 2, tokens // LANES, LANES)],
        [part, fixed_spec(2, tokens // LANES, LANES)],
        [pltpu.VMEM((rows, width), F32)] + [pltpu.VMEM((block, width), F32)] * 4,
        None,
        (60 * tokens * width, 22 * tokens * width),
    )


def middle_norm_kernel(layer, model, xn_ref, stat_ref, vec_ref, a_ref, b_ref, mean_ref, scale_ref):
    group = stat_ref.shape[0]
    block, width = xn_ref.shape
    for b in range(block // LANES):
        row = pl.ds(pl.program_id(0) * (block // LANES) + b, 1)
        here = slice(b * LANES, (b + 1) * LANES)
        means = [stat_ref[s, 0, row, :] for s in range(group)]
        mean = sum(means) / group
        square = sum(stat_ref[s, 1, row, :] for s in range(group))
        between = sum((part - mean) * (part - mean) for part in means)
        scale = lax.rsqrt((square + between * width) / model + 1e-05)
        mean_ref[here, :] = jnp.broadcast_to(mean, (LANES, LANES)).T
        scale_ref[here, :] = jnp.broadcast_to(scale, (LANES, LANES)).T

    per = pl.num_programs(0) // 2
    for side, normed_ref in enumerate((a_ref, b_ref)):

        @pl.when(pl.program_id(0) // per == side)
        def _():
            def part(here):
                normed_ref[here, :] = (
                    (xn_ref[here, :] - widen(mean_ref[here, :], width))
                    * widen(scale_ref[here, :], width)
                    * row_at(vec_ref, layer, GAIN)
                    + row_at(vec_ref, layer, BIAS)
                ).astype(BF16)

            chunks(block, 64, part)


def middle_norm(layer, model, xn, stats, vectors, rows):
    tokens, width = xn.shape
    block = rows * STEPS
    per = tokens // block // 2
    return run(
        functools.partial(middle_norm_kernel, layer, model),
        "middle_norm",
        (tokens // block,),
        [xn, stats, vectors],
        [block_spec(block, width), fixed_spec(*stats.shape), fixed_spec(*vectors.shape)],
        [shape_of(BF16, tokens // 2, width)] * 2 + [shape_of(F32, tokens, LANES)] * 2,
        [
            pl.BlockSpec((block, width), lambda i, *_: (jnp.minimum(i, per - 1), 0)),
            pl.BlockSpec((block, width), lambda i, *_: (jnp.maximum(i - per, 0), 0)),
        ]
        + [block_spec(block, LANES)] * 2,
        cost=(10 * tokens * width, 8 * tokens * width),
    )


def add_total(decay_s, drive_s, tot_ref):
    @pl.when(pl.program_id(0) == 0)
    def _():
        tot_ref[0] = jnp.ones_like(tot_ref[0])
        tot_ref[1] = jnp.zeros_like(tot_ref[1])

    def one(at, state):
        return state[0] * decay_s[at, :], state[1] + state[0] * drive_s[at, :]

    product, total = over_time(one, (tot_ref[0], tot_ref[1]))
    tot_ref[0] = product
    tot_ref[1] = total


def turn_kernel(layer, cf_ref, ur_ref, x_ref, dh_ref, keep_ref, order_ref, back_ref, vec_ref, *refs):
    prev_ref, dr_ref, dc_ref, high_ref, out_ref, du_ref, tot_ref, small_ref = refs[-14:-6]
    carry_s, forget_s, state_s, dh_s, drive_s, out_s = refs[-6:]
    far = refs[:-14]
    block, width = prev_ref.shape

    def put(here, value):
        dh_s[here, :] = value

    to_time(order_ref, dh_ref[...].reshape(-1, STEPS, width), put)
    carry_forward(layer, cf_ref, keep_ref, vec_ref, far, carry_s, forget_s, prev_ref, state_s)

    @pl.when(pl.program_id(0) == 0)
    def _():
        small_ref[...] = jnp.zeros_like(small_ref)

    def finish(here):
        state = state_s[here, :]
        x = x_ref[here, :]
        dh = dh_s[here, :]
        prev = prev_ref[here, :]
        gate = reset_gate(layer, ur_ref, prev_ref, here, vec_ref)
        out_s[here, :] = (gate * state + (1.0 - gate) * x).astype(BF16)
        dr = dh * (state - x) * gate * (1.0 - gate)
        dc = dh * gate
        dr_ref[here, :] = dr
        dc_ref[here, :] = dc
        du_ref[here, :] = dr.astype(BF16)
        high_ref[here, :] = dh - dc
        keep = widen(keep_ref[here, :], width)
        decay = keep * forget_s[here, :]
        state_s[here, :] = decay
        drive_s[here, :] = keep * row_at(vec_ref, layer, PEEP) * dr + decay * dc
        small_ref[0] += fold(dr * prev)
        small_ref[1] += fold(dr)

    chunks(block, 32, finish)
    to_rows(back_ref, out_s, out_ref)
    add_total(state_s, drive_s, tot_ref)


def turn(layer, cf, ur, x, dh, keep, order, back, vectors, far):
    tokens, width = ur.shape
    _, half, _, rows_dev, span, _ = dh.shape
    rows = half * rows_dev
    block = rows * STEPS
    part = block_spec(block, width)
    by_rows = rows_spec(rows, width, span // STEPS)
    return run(
        functools.partial(turn_kernel, layer),
        "turn",
        (tokens // block,),
        [cf, ur, x, dh, keep, order, back, vectors, *far],
        [
            block_spec(block, 2 * width),
            part,
            part,
            split_spec(half, rows_dev, width, span // STEPS, 1),
            block_spec(block, LANES),
            fixed_spec(*order.shape),
            fixed_spec(*back.shape),
            fixed_spec(*vectors.shape),
        ]
        + [fixed_spec(2, rows, width)] * len(far),
        [shape_of(F32, tokens, width)] * 4
        + [
            shape_of(BF16, 2, rows, span, width),
            shape_of(BF16, tokens, width),
            shape_of(F32, 2, rows, width),
            shape_of(F32, 2, SUBLANES, width),
        ],
        [part] * 4
        + [by_rows, part, fixed_spec(2, rows, width), fixed_spec(2, SUBLANES, width)],
        [pltpu.VMEM((rows, width), F32)]
        + [pltpu.VMEM((block, width), F32)] * 4
        + [pltpu.VMEM((block, width), BF16)],
        None,
        (80 * tokens * width, 36 * tokens * width),
    )


def retreat_kernel(layer, sums, dc_ref, dr_ref, prev_ref, cf_ref, keep_ref, vec_ref, *refs):
    if sums:
        ur_ref, mixed_ref = refs[:2]
        du_ref, small_ref, stat_ref, carry_s, forget_s, total_s, sum_s, cross_s = refs[-8:]
        far = refs[2:-8]
    else:
        back_ref = refs[0]
        du_ref, rows_ref, small_ref, carry_s, forget_s, total_s = refs[-6:]
        far = refs[1:-6]
    block, width = prev_ref.shape
    peep = row_at(vec_ref, layer, PEEP)

    @pl.when(pl.program_id(0) == 0)
    def _():
        first = incoming(far)
        carry_s[...] = jnp.zeros_like(carry_s) if first is None else first
        small_ref[...] = jnp.zeros_like(small_ref)

    def gates(here):
        forget_s[here, :] = forget_gate(cf_ref, here, vec_ref, layer)

    chunks(block, 64, gates)

    def one(at, state):
        total = dc_ref[at, :] + state
        total_s[at, :] = total
        return widen(keep_ref[at, :], width) * (peep * dr_ref[at, :] + forget_s[at, :] * total)

    carry_s[...] = over_time(one, carry_s[...], True)

    def halves(value):
        return sum(value[:, j : j + LANES] for j in range(0, width, LANES))

    def finish(here):
        forget = forget_s[here, :]
        slow = total_s[here, :] * (1.0 - forget)
        d_forget = slow * forget * (prev_ref[here, :] - cf_ref[here, :width])
        d_cand = slow.astype(BF16)
        d_gate = d_forget.astype(BF16)
        du_ref[here, :width] = d_cand
        du_ref[here, width:] = d_gate
        small_ref[...] += fold(d_forget)
        if sums:
            parts = [d_cand, d_gate, dr_ref[here, :].astype(BF16)]
            inputs = [cf_ref[here, :width], cf_ref[here, width:], ur_ref[here, :]]
            plain = cross = 0.0
            for third in range(3):
                at = slice(third * width, (third + 1) * width)
                du = parts[third].astype(F32)
                plain = plain + du * mixed_ref[0:1, at]
                cross = cross + du * (inputs[third] - mixed_ref[1:2, at])
            sum_s[here, :] = halves(plain)
            cross_s[here, :] = halves(cross)

    chunks(block, 32, finish)
    if sums:
        base = (pl.num_programs(0) - 1 - pl.program_id(0)) * (block // LANES)
        for b in range(block // LANES):
            here = slice(b * LANES, (b + 1) * LANES)
            stat_ref[0, pl.ds(base + b, 1), :] = jnp.sum(sum_s[here, :].T, axis=0, keepdims=True)
            stat_ref[1, pl.ds(base + b, 1), :] = jnp.sum(cross_s[here, :].T, axis=0, keepdims=True)
    else:
        to_rows(back_ref, du_ref, rows_ref)


def retreat(layer, dc, dr, prev, cf, keep, vectors, far, rows, span, awaited, back=None, ur=None, mixed=None):
    tokens, width = dc.shape
    block = rows * STEPS
    count = tokens // block
    sums = back is None
    part = turned_spec(block, width, count)
    both = turned_spec(block, 2 * width, count)
    rows_out = rows_spec(rows, 2 * width, span // STEPS, lambda i: count - 1 - i)
    outs = [shape_of(BF16, tokens, 2 * width)]
    specs = [both]
    scratch = [pltpu.VMEM((rows, width), F32)] + [pltpu.VMEM((block, width), F32)] * 2
    if sums:
        more, more_specs = [ur, mixed], [part, fixed_spec(*mixed.shape)]
        outs += [shape_of(F32, SUBLANES, width), shape_of(F32, 2, tokens // LANES, LANES)]
        specs += [fixed_spec(SUBLANES, width), fixed_spec(2, tokens // LANES, LANES)]
        scratch += [pltpu.VMEM((block, LANES), F32)] * 2
    else:
        more, more_specs = [back], [fixed_spec(*back.shape)]
        outs += [shape_of(BF16, 2, rows, span, 2 * width), shape_of(F32, SUBLANES, width)]
        specs += [rows_out, fixed_spec(SUBLANES, width)]
    return run(
        functools.partial(retreat_kernel, layer, sums),
        "retreat",
        (count,),
        [dc, dr, prev, cf, keep, vectors, *more, *far],
        [part] * 3
        + [both, turned_spec(block, LANES, count), fixed_spec(*vectors.shape)]
        + more_specs
        + [fixed_spec(2, rows, width)] * len(far),
        outs,
        specs,
        scratch,
        None,
        (60 * tokens * width, 30 * tokens * width),
        awaited,
    )


def back_product(pair, reset, w_pair, w_reset):
    contract = (((1,), (1,)), ((), ()))
    return lax.dot_general(pair, w_pair, contract, preferred_element_type=F32) + lax.dot_general(
        reset, w_reset, contract, preferred_element_type=F32
    )


def back_features_kernel(odd, order, pair_ref, reset_ref, wp_ref, wr_ref, odd_ref, even_ref):
    k = pl.program_id(0)
    share = back_product(pair_ref[...], reset_ref[...], wp_ref[...], wr_ref[...])

    @pl.when(k < odd)
    def _():
        odd_ref[0] = share.astype(BF16)

    @pl.when(k >= odd)
    def _():
        even_ref[0] = share


def back_features(order, odd, pair, reset, w_pair, w_reset, awaited):
    tokens, width = reset.shape
    count = order.shape[0]
    by_order = lambda k, order: (order[k], 0)
    return run(
        functools.partial(back_features_kernel, odd),
        "back_features",
        (count,),
        [pair, reset, w_pair, w_reset],
        [
            fixed_spec(*pair.shape),
            fixed_spec(*reset.shape),
            pl.BlockSpec((width, 2 * width), by_order),
            pl.BlockSpec((width, width), by_order),
        ],
        [shape_of(BF16, odd, tokens, width), shape_of(F32, count - odd, tokens, width)],
        [
            pl.BlockSpec((1, tokens, width), lambda k, order: (jnp.minimum(k, odd - 1), 0, 0)),
            pl.BlockSpec((1, tokens, width), lambda k, order: (jnp.maximum(k - odd, 0), 0, 0)),
        ],
        (),
        order,
        (6 * count * tokens * width * width, 8 * count * tokens * width),
        awaited,
    )


def back_tokens_kernel(odd, order, pair_ref, reset_ref, wp_ref, wr_ref, odd_ref, even_ref):
    k = pl.program_id(0)
    local = odd_ref.shape[1]
    pair = pair_ref[0].reshape(local, pair_ref.shape[-1])
    reset = reset_ref[0].reshape(local, reset_ref.shape[-1])
    share = back_product(pair, reset, wp_ref[...], wr_ref[...])

    @pl.when(k < odd)
    def _():
        odd_ref[0] = share.astype(BF16)

    @pl.when(k >= odd)
    def _():
        even_ref[0] = share


def back_tokens(order, odd, pair, reset, w_pair, w_reset, awaited):
    two, rows, span, width = reset.shape
    model = w_pair.shape[0]
    count = order.shape[0]
    half = model // width // 2
    rows_dev = rows // half
    local = rows_dev * span
    by_order = lambda k, order: (order[k] // half, order[k] % half, 0, 0)
    return run(
        functools.partial(back_tokens_kernel, odd),
        "back_tokens",
        (count,),
        [pair, reset, w_pair, w_reset],
        [
            pl.BlockSpec((1, rows_dev, span, 2 * width), by_order),
            pl.BlockSpec((1, rows_dev, span, width), by_order),
            fixed_spec(*w_pair.shape),
            fixed_spec(*w_reset.shape),
        ],
        [shape_of(BF16, odd, local, model), shape_of(F32, count - odd, local, model)],
        [
            pl.BlockSpec((1, local, model), lambda k, order: (jnp.minimum(k, odd - 1), 0, 0)),
            pl.BlockSpec((1, local, model), lambda k, order: (jnp.maximum(k - odd, 0), 0, 0)),
        ],
        (),
        order,
        (6 * count * local * model * width, 8 * count * local * model),
        awaited,
    )


def middle_back_kernel(layer, model, *refs):
    (
        kept_ref, core_ref, pair_ref, line_ref, high_ref, x_ref, mean_ref, scale_ref, stat_ref,
        cf_ref, ur_ref, below_x_ref, keep_ref, order_ref, back_ref, vec_ref,
    ) = refs[:16]
    (
        prev_ref, dr_ref, dc_ref, below_ref, du_ref, rows_ref, tot_ref, small_ref,
        carry_s, forget_s, state_s, drive_s, x_s, plain_s, cross_s, below_s,
    ) = refs[-16:]
    far = refs[16:-16]
    block, width = prev_ref.shape
    below = layer - 1

    def put(here, value):
        x_s[here, :] = value

    to_time(order_ref, below_x_ref[...].reshape(-1, STEPS, width), put)
    carry_forward(below, cf_ref, keep_ref, vec_ref, far, carry_s, forget_s, prev_ref, state_s)
    for b in range(block // LANES):
        row = pl.ds(pl.program_id(0) * (block // LANES) + b, 1)
        here = slice(b * LANES, (b + 1) * LANES)
        for s, out in enumerate((plain_s, cross_s)):
            out[here, :] = jnp.broadcast_to(stat_ref[s, row, :] / model, (LANES, LANES)).T

    @pl.when(pl.program_id(0) == 0)
    def _():
        small_ref[...] = jnp.zeros_like(small_ref)

    def finish(here):
        back = (
            kept_ref[0, here, :]
            + core_ref[0, here, :].astype(F32)
            + pair_ref[here, :].astype(F32)
            + line_ref[here, :].astype(F32)
        )
        scale = widen(scale_ref[here, :], width)
        xhat = (x_ref[here, :] - widen(mean_ref[here, :], width)) * scale
        dh = high_ref[here, :] + scale * (
            back * row_at(vec_ref, layer, GAIN)
            - widen(plain_s[here, :], width)
            - xhat * widen(cross_s[here, :], width)
        )
        small_ref[0] += fold(back * xhat)
        small_ref[1] += fold(back)
        gate = reset_gate(below, ur_ref, prev_ref, here, vec_ref)
        dr = dh * (state_s[here, :] - x_s[here, :]) * gate * (1.0 - gate)
        dc = dh * gate
        dr_ref[here, :] = dr
        dc_ref[here, :] = dc
        du_ref[here, :] = dr.astype(BF16)
        below_s[here, :] = (dh - dc).astype(BF16)
        keep = widen(keep_ref[here, :], width)
        decay = keep * forget_s[here, :]
        state_s[here, :] = decay
        drive_s[here, :] = keep * row_at(vec_ref, below, PEEP) * dr + decay * dc
        small_ref[2] += fold(dr * prev_ref[here, :])
        small_ref[3] += fold(dr)

    chunks(block, 32, finish)
    to_rows(back_ref, below_s, below_ref)
    to_rows(back_ref, du_ref, rows_ref)
    add_total(state_s, drive_s, tot_ref)


def middle_back(
    layer, model, kept, core, pair, line, high, x, mean, scale, stats, cf, ur, below_x, keep, order,
    back, vectors, far,
):
    tokens, width = ur.shape
    _, half, _, rows_dev, span, _ = below_x.shape
    rows = half * rows_dev
    block = rows * STEPS
    part = block_spec(block, width)
    top = pl.BlockSpec((1, block, width), lambda i, *_: (0, i, 0))
    thin = block_spec(block, LANES)
    by_rows = rows_spec(rows, width, span // STEPS)
    held = pltpu.VMEM((block, width), F32)
    return run(
        functools.partial(middle_back_kernel, layer, model),
        "middle_back",
        (tokens // block,),
        [
            kept, core, pair, line, high, x, mean, scale, stats, cf, ur, below_x, keep, order, back,
            vectors, *far,
        ],
        [top, top, part, part, part, part, thin, thin, fixed_spec(*stats.shape)]
        + [
            block_spec(block, 2 * width),
            part,
            split_spec(half, rows_dev, width, span // STEPS, 0),
            thin,
            fixed_spec(*order.shape),
            fixed_spec(*back.shape),
            fixed_spec(*vectors.shape),
        ]
        + [fixed_spec(2, rows, width)] * len(far),
        [shape_of(F32, tokens, width)] * 3
        + [
            shape_of(BF16, 2, rows, span, width),
            shape_of(BF16, tokens, width),
            shape_of(BF16, 2, rows, span, width),
            shape_of(F32, 2, rows, width),
            shape_of(F32, 4, SUBLANES, width),
        ],
        [part, part, part, by_rows, part, by_rows]
        + [fixed_spec(2, rows, width), fixed_spec(4, SUBLANES, width)],
        [pltpu.VMEM((rows, width), F32)]
        + [held] * 4
        + [pltpu.VMEM((block, LANES), F32)] * 2
        + [pltpu.VMEM((block, width), BF16)],
        None,
        (80 * tokens * width, 44 * tokens * width),
    )


def first_back_kernel(kept_ref, core_ref, pair_ref, line_ref, x_ref, gain_ref, high_ref, out_ref, small_ref):
    local, model = x_ref.shape
    group, _, width = high_ref.shape
    small_ref[...] = jnp.zeros_like(small_ref)

    def part(here):
        wide = x_ref[here, :].astype(F32)
        centered = wide - jnp.mean(wide, axis=-1, keepdims=True)
        scale = lax.rsqrt(jnp.mean(centered * centered, axis=-1, keepdims=True) + 1e-05)
        xhat = centered * scale
        back = (
            kept_ref[0, here, :]
            + core_ref[0, here, :].astype(F32)
            + pair_ref[here, :].astype(F32)
            + line_ref[here, :].astype(F32)
        )
        scaled = back * gain_ref[0:1, :]
        small_ref[0] += fold(back * xhat)
        small_ref[1] += fold(back)
        total = scale * (
            scaled
            - jnp.mean(scaled, axis=-1, keepdims=True)
            - xhat * jnp.mean(scaled * xhat, axis=-1, keepdims=True)
        )
        for s in range(group):
            columns = slice(s * width, (s + 1) * width)
            out_ref[here, columns] = (total[:, columns] + high_ref[s, here, :].astype(F32)).astype(
                BF16
            )

    chunks(local, 16, part)


def first_back(kept, core, pair, line, x, gain, high):
    local, model = x.shape
    top = pl.BlockSpec((1, local, model), lambda i, *_: (0, 0, 0))
    flat = fixed_spec(local, model)
    return run(
        first_back_kernel,
        "first_back",
        (1,),
        [kept, core, pair, line, x, gain, high],
        [top, top, flat, flat, flat, fixed_spec(*gain.shape), fixed_spec(*high.shape)],
        [shape_of(BF16, local, model), shape_of(F32, 2, SUBLANES, model)],
        [flat, fixed_spec(2, SUBLANES, model)],
        cost=(30 * local * model, 16 * local * model),
    )


def weight_kernel(whole_ref, pair_ref, reset_ref, out_ref):
    both = pair_ref.shape[1]
    contract = (((0,), (0,)), ((), ()))
    for du_ref, at in ((pair_ref, slice(0, both)), (reset_ref, slice(both, out_ref.shape[1]))):
        out_ref[:, at] = lax.dot_general(
            whole_ref[...], du_ref[...], contract, preferred_element_type=F32
        ).astype(BF16)


def weight_term(whole, pair, reset, awaited=()):
    tokens, model = whole.shape
    width = reset.shape[1]
    block = model // 4
    return run(
        weight_kernel,
        "weight_term",
        (4,),
        [whole, pair, reset],
        [
            pl.BlockSpec((tokens, block), lambda k, *_: (0, k)),
            fixed_spec(*pair.shape),
            fixed_spec(*reset.shape),
        ],
        shape_of(BF16, model, 3 * width),
        block_spec(block, 3 * width),
        cost=(6 * tokens * model * width, 2 * tokens * model + 6 * model * width),
        awaited=awaited,
    )


def join_kernel(x_ref, out_ref):
    group, rows, width = x_ref.shape
    for s in range(group):
        out_ref[:, s * width : (s + 1) * width] = x_ref[s]


def join(value):
    group, rows, width = value.shape
    return run(
        join_kernel,
        "join",
        (1,),
        [value],
        [fixed_spec(group, rows, width)],
        shape_of(value.dtype, rows, group * width),
        fixed_spec(rows, group * width),
        cost=(0, 4 * rows * group * width),
    )


def join_weights_kernel(*refs):
    out_ref = refs[-1]
    for layer, part_ref in enumerate(refs[:-1]):
        group, shard, total = part_ref.shape
        width = total // 3
        for s in range(group):
            for third in range(3):
                start = third * group * width + s * width
                at = slice(third * width, (third + 1) * width)
                out_ref[layer, :, start : start + width] = part_ref[s, :, at].astype(F32)


def join_weights(parts):
    group, shard, total = parts[0].shape
    shape = (len(parts), shard, group * total)
    return run(
        join_weights_kernel,
        "join_weights",
        (1,),
        parts,
        [fixed_spec(*part.shape) for part in parts],
        shape_of(F32, *shape),
        fixed_spec(*shape),
        cost=(0, 12 * group * shard * total),
    )


def swap(value, bits, size):
    return lax.ppermute(value, GROUP, [(i, i ^ bits) for i in range(size)])


def gather_group(a, b, size):
    pair_a = swap(a, PAIR, size)
    line_b = swap(b, LINE, size)
    a, b = after([a, b], pair_a, line_b)
    pair_b = swap(b, PAIR, size)
    line_a = swap(a, LINE, size)
    far_a = swap(pair_a, LINE, size)
    far_b = swap(line_b, PAIR, size)
    halves = [a, b, line_a, line_b, pair_a, pair_b, far_a, far_b]
    cores = [swap(half, CORE, size) for half in halves]
    return [
        half
        for k in range(0, 8, 2)
        for half in (halves[k], halves[k + 1], cores[k], cores[k + 1])
    ]


def reduce_group(shares, size, stats, early, soon, filler):
    far_odd, far_even = shares((7, 6), 1, early)
    far_core = swap(far_odd, CORE, size)
    stats = [part + swap(part, CORE, size) for part in stats]
    side_odd, side_even = shares((5, 3, 4, 2), 2, (far_odd, *soon, *stats))
    side_core = swap(side_odd, CORE, size)
    far = (far_even[0] + far_core[0].astype(F32)).astype(BF16)
    half = far.shape[0] // 2
    stats = [part + swap(part, LINE, size) for part in stats]
    far_a, far_b = after([far[:half], far[half:]], side_odd, *stats)
    by_pair = swap(far_a, PAIR, size)
    by_line = swap(far_b, LINE, size)
    filled = filler((far_a, far_b))
    if stats:
        stats = after(stats, far_a, far_b)
    stats = [part + swap(part, PAIR, size) for part in stats]
    own_odd, own_even = shares((1, 0), 1, (filled, *stats))
    (side_even,) = after([side_even], own_odd)
    sides = side_even + side_core.astype(F32)
    zeros = jnp.zeros_like(by_pair)
    pair = (sides[0] + jnp.concatenate([zeros, by_line]).astype(F32)).astype(BF16)
    line = (sides[1] + jnp.concatenate([by_pair, zeros]).astype(F32)).astype(BF16)
    own_core = swap(own_odd, CORE, size)
    pair = swap(pair, PAIR, size)
    line = swap(line, LINE, size)
    return own_even, own_core, pair, line, stats


def exchange(part, size, reverse):
    far = []
    for hop in range(1, size):
        pairs = [(i, i + hop) for i in range(size - hop)]
        if reverse:
            pairs = [(b, a) for a, b in pairs]
        far.append(lax.ppermute(part, "ring", pairs))
    return far


def spread_small(vectors, ring, half, awaited):
    size = 2 * ring * half
    axes = ("ring", "pair", "rows")
    me = lax.axis_index(axes)
    bit = size // 2
    while bit:
        if awaited and bit < size // 2:
            (vectors,) = after([vectors], awaited.pop(0))
        width = vectors.shape[1] // 2
        mine = jnp.where((me & bit) > 0, 1, 0)
        send = lax.dynamic_slice_in_dim(vectors, (1 - mine) * width, width, 1)
        hold = lax.dynamic_slice_in_dim(vectors, mine * width, width, 1)
        vectors = hold + lax.ppermute(send, axes, [(i, i ^ bit) for i in range(size)])
        bit //= 2
    return vectors


def order_matrix(rows):
    index = np.arange(rows * SUB)
    return (index % rows * SUB + index // rows)[:, None] == index[None, :]


def to_group(value):
    return lax.all_to_all(value, GROUP, split_axis=0, concat_axis=0, tiled=True)


def body(
    inputs,
    out_grad,
    reset_flags,
    weights,
    ln_gain,
    layer_norm_bias,
    reset_peep,
    forget_bias,
    reset_bias,
):
    rows_dev, span, model = inputs.shape
    layers, shard, _ = weights.shape
    ring = lax.axis_size("ring")
    half = lax.axis_size("rows")
    group = 2 * half
    place = jnp.stack([lax.axis_index("ring"), lax.axis_index("pair"), lax.axis_index("rows")])
    place = place.astype(jnp.int32)
    me = lax.axis_index(GROUP)
    width = model // group
    rows = rows_dev * half
    local = rows_dev * span
    tokens = 2 * rows * span
    order = jnp.asarray(order_matrix(rows), BF16)
    back = jnp.asarray(order_matrix(rows).T, BF16)

    def gather_columns(value):
        value = value.reshape(group * shard, 3 * width)
        return [
            lax.all_gather(part, "ring", axis=0, tiled=True)
            for part in (value[:, : 2 * width], value[:, 2 * width :])
        ]

    flags = jnp.pad(reset_flags.astype(BF16), ((0, 2 * SUBLANES - rows_dev), (0, 0)))
    columns = columns_of(weights, 1, group, width)
    mine = send_columns(place, weights, 0, group, width, flags)
    got = [mine[0]] + [swap(mine[k], k, group) for k in range(1, group)]
    *normed, split = first_norm(inputs, out_grad, ln_gain, layer_norm_bias, group, (mine[0],))
    pair_mine, reset_mine, flags = stack_columns(place, got, shard, (normed[0], columns))
    pair_w1 = lax.all_gather(pair_mine, "ring", axis=0, tiled=True)
    reset_w1 = lax.all_gather(reset_mine, "ring", axis=0, tiled=True)
    flags = flags[:, :rows_dev, :span].reshape(2, rows, span)
    keep = (1.0 - flags.astype(F32)).transpose(0, 2, 1).reshape(tokens, 1)
    keep = jnp.broadcast_to(keep, (tokens, LANES))
    vectors = jnp.stack([ln_gain, layer_norm_bias, reset_peep, forget_bias, reset_bias], axis=1)
    vectors = lax.dynamic_slice_in_dim(vectors.reshape(layers * 5, model), me * width, width, 1)
    vectors = jnp.pad(vectors, ((0, 16 - layers * 5), (0, 0)))
    pieces1 = gather_group(*after(normed, pair_mine), group)

    cf1, whole1, part = project(place, 0, pieces1, pair_w1, order, keep, vectors, rows, True)
    far1 = exchange(part, ring, False)
    (split,) = after([split], *pieces1)
    split = to_group(split).reshape(2, half, 2, rows_dev, span, width)
    (columns,) = after([columns], split, *far1)
    columns = to_group(columns)
    ur1 = reset_product(whole1, reset_w1)
    (columns,) = after([columns], ur1)
    pair_w2, reset_w2 = gather_columns(columns)
    x2, stats = advance(0, cf1, ur1, split, keep, order, vectors, far1)
    stats = lax.all_gather(stats, GROUP)
    *normed, mean2, scale2 = middle_norm(1, model, x2, stats, vectors, rows)

    def mixed():
        def thirds(value):
            high = value.astype(BF16)
            middle = (value - high.astype(F32)).astype(BF16)
            low = (value - high.astype(F32) - middle.astype(F32)).astype(BF16)
            return [high, middle, low]

        lines = jnp.stack(thirds(ln_gain[1]) + thirds(layer_norm_bias[1]))
        lines = jnp.pad(lines, ((0, 10), (0, 0)))
        both = jnp.concatenate(
            [jnp.dot(lines, w, preferred_element_type=F32) for w in (pair_w2, reset_w2)], axis=1
        )
        return jnp.pad(jnp.sum(both[:6].reshape(2, 3, 3 * width), axis=1), ((0, 6), (0, 0)))

    pieces2 = gather_group(*normed, group)

    cf2, whole2, part = project(place, 1, pieces2, pair_w2, order, keep, vectors, rows, False)
    far = exchange(part, ring, False)
    ur2 = reset_product(whole2, reset_w2)
    prev2, dr2, dc2, high2, out, du_r2, part, sums2 = turn(
        1, cf2, ur2, x2, split, keep, order, back, vectors, far
    )
    far = exchange(part, ring, True)

    def scatter(term):
        return lax.psum_scatter(term, "ring", scatter_dimension=0, tiled=True)

    (out,) = after([out.reshape(group, local, width)], *far)
    out = to_group(out)
    du_p2, forget2, stats = retreat(
        1, dc2, dr2, prev2, cf2, keep, vectors, far, rows, span, (), ur=ur2, mixed=mixed()
    )
    outputs = join(out).reshape(rows_dev, span, model)

    def slices(slots):
        return jnp.stack([me ^ k for k in slots]).astype(jnp.int32)

    terms = []

    def weigh(whole, du_p, du_r):
        def work(awaited):
            term = weight_term(whole, du_p, du_r, awaited)
            terms.append(scatter(term).reshape(group, shard, 3 * width))
            return term

        return work

    kept, core, pair, line, (stats,) = reduce_group(
        lambda slots, odd, awaited: back_features(
            slices(slots), odd, du_p2, du_r2, pair_w2, reset_w2, awaited
        ),
        group,
        (stats,),
        (out,),
        (),
        weigh(whole2, du_p2, du_r2),
    )
    (kept,) = after([kept], outputs)

    prev1, dr1, dc1, high1, du_r1, rows_r1, part, sums1 = middle_back(
        1, model, kept, core, pair, line, high2, x2, mean2, scale2, stats, cf1, ur1, split, keep,
        order, back, vectors, far1,
    )
    far = exchange(part, ring, True)
    (high1,) = after([high1.reshape(group, local, width)], *far)
    high = to_group(high1)
    du_p1, rows_p1, forget1 = retreat(
        0, dc1, dr1, prev1, cf1, keep, vectors, far, rows, span, (), back=back
    )
    kept, core, pair, line, _ = reduce_group(
        lambda slots, odd, awaited: back_tokens(
            slices(slots), odd, rows_p1, rows_r1, pair_w1, reset_w1, awaited
        ),
        group,
        (),
        (high,),
        (terms[0],),
        weigh(whole1, du_p1, du_r1),
    )
    (term2,) = after(terms[:1], kept)
    second = to_group(term2)
    first = to_group(terms[1])
    input_grad, gains1 = first_back(
        kept, core, pair, line, inputs.reshape(local, model), ln_gain, high
    )
    input_grad = input_grad.reshape(rows_dev, span, model)
    weight_grad = join_weights([first, second])

    def total(value):
        return jnp.sum(value, axis=-2)

    sums1 = total(sums1)
    sums2 = total(sums2)
    narrow = jnp.stack(
        [
            sums1[2], total(forget1), sums1[3],
            sums1[0], sums1[1], sums2[0], total(forget2), sums2[1],
        ]
    )
    narrow = lax.dynamic_update_slice(jnp.zeros((8, model), F32), narrow, (0, me * width))
    small = jnp.concatenate([total(gains1), narrow])
    small = spread_small(small, ring, half, [second, first]).reshape(2, 5, shard)
    return (outputs, input_grad, weight_grad) + tuple(small[:, i] for i in range(5))


def solution(mesh):
    ring = mesh.shape["tm"] // 2
    fine = Mesh(
        mesh.devices.reshape(ring, 2, mesh.shape["rows"]), ("ring", "pair", "rows")
    )
    tm = ("ring", "pair")
    everything = ("ring", "pair", "rows")
    return jax.shard_map(
        body,
        mesh=fine,
        in_specs=(
            P("rows", tm, None),
            P("rows", tm, None),
            P("rows", tm),
            P(None, everything, None),
            P(),
            P(),
            P(),
            P(),
            P(),
        ),
        out_specs=(
            P("rows", tm, None),
            P("rows", tm, None),
            P(None, everything, None),
            P(None, everything),
            P(None, everything),
            P(None, everything),
            P(None, everything),
            P(None, everything),
        ),
        check_vma=False,
    )
```

```python
import functools

import jax
import jax.numpy as jnp
import numpy as np
from jax import lax
from jax.experimental import pallas as pl
from jax.experimental.pallas import tpu as pltpu
from jax.sharding import Mesh
from jax.sharding import PartitionSpec as P

LANES = 128
SUBLANES = 8
STEPS = 64
SUB = 32
VMEM_BYTES = 58 * 1024 * 1024
GAIN, BIAS, PEEP, FORGET, RESET = range(5)
BF16 = jnp.bfloat16
F32 = jnp.float32
GROUP = ("pair", "rows")
CORE, LINE, PAIR = 1, 2, 4


def shape_of(dtype, *shape):
    return jax.ShapeDtypeStruct(shape, dtype)


def run(
    kernel, name, grid, ins, in_specs, outs, out_specs, scratch=(), place=None, cost=(0, 0), awaited=()
):
    scalars = 0 if place is None else 1
    first = scalars + len(ins)
    last = first + len(awaited)

    def body(*refs):
        kernel(*refs[:first], *refs[last:])

    function = pl.pallas_call(
        body,
        out_shape=outs,
        grid_spec=pltpu.PrefetchScalarGridSpec(
            num_scalar_prefetch=scalars,
            grid=grid,
            in_specs=list(in_specs) + [pl.BlockSpec(memory_space=pl.ANY)] * len(awaited),
            out_specs=out_specs,
            scratch_shapes=list(scratch),
        ),
        compiler_params=pltpu.CompilerParams(vmem_limit_bytes=VMEM_BYTES),
        cost_estimate=pl.CostEstimate(flops=cost[0], bytes_accessed=cost[1], transcendentals=0),
        name=name,
    )
    return function(*(() if place is None else (place,)), *ins, *awaited)


def quarter(index, width):
    return pl.ds(pl.multiple_of(index * width, width), width)


def fixed_spec(*shape):
    return pl.BlockSpec(shape, lambda *_: (0,) * len(shape))


def block_spec(block, width):
    return pl.BlockSpec((block, width), lambda i, *_: (i, 0))


def turned_spec(block, width, count):
    return pl.BlockSpec((block, width), lambda i, *_: (count - 1 - i, 0))


def rows_spec(rows, width, per, place_of=lambda i: i):
    return pl.BlockSpec(
        (1, rows, STEPS, width), lambda i, *_: (place_of(i) // per, 0, place_of(i) % per, 0)
    )


def split_spec(half, rows_dev, width, per, which):
    return pl.BlockSpec(
        (1, half, 1, rows_dev, STEPS, width), lambda i, *_: (i // per, 0, which, 0, i % per, 0)
    )


def row_at(vec_ref, layer, which):
    row = layer * 5 + which
    return vec_ref[row : row + 1, :]


def chunks(total, size, body, unroll=1):
    def one(i, carry):
        body(pl.ds(pl.multiple_of(i * size, size), size))
        return carry

    lax.fori_loop(0, total // size, one, 0, unroll=unroll)


def over_time(body, state, backward=False):
    def one(i, state):
        t = STEPS - 1 - i if backward else i
        return body(pl.ds(pl.multiple_of(t * SUBLANES, SUBLANES), SUBLANES), state)

    return lax.fori_loop(0, STEPS, one, state, unroll=8)


def widen(keep, width):
    return jnp.concatenate([keep] * (width // LANES), axis=1)


def incoming(far):
    state = None
    for ref in reversed(far):
        state = ref[1] if state is None else ref[0] * state + ref[1]
    return state


def exact(order, value):
    return jnp.dot(order, value, preferred_element_type=F32)


def to_time(order_ref, rows, put):
    block = order_ref.shape[0]
    for i in range(STEPS // SUB):
        part = rows[:, i * SUB : (i + 1) * SUB, :].reshape(block, rows.shape[-1])
        put(slice(i * block, (i + 1) * block), exact(order_ref[...], part))


def to_rows(back_ref, value_ref, out_ref):
    block = back_ref.shape[0]
    for i in range(STEPS // SUB):
        part = exact(back_ref[...], value_ref[i * block : (i + 1) * block, :])
        out_ref[0, :, i * SUB : (i + 1) * SUB, :] = part.astype(BF16).reshape(
            out_ref.shape[1], SUB, out_ref.shape[3]
        )


def forget_gate(cf_ref, here, vec_ref, layer):
    width = cf_ref.shape[1] // 2
    return jax.nn.sigmoid(cf_ref[here, width:] + row_at(vec_ref, layer, FORGET))


def fold(value):
    return jnp.sum(value.reshape(-1, SUBLANES, value.shape[-1]), axis=0)


def after(values, *awaited):
    count = len(values)

    def nothing(*refs):
        pass

    return pl.pallas_call(
        nothing,
        out_shape=[shape_of(v.dtype, *v.shape) for v in values],
        in_specs=[pl.BlockSpec(memory_space=pl.ANY)] * (count + len(awaited)),
        out_specs=[pl.BlockSpec(memory_space=pl.ANY)] * count,
        input_output_aliases={i: i for i in range(count)},
        name="after",
    )(*values, *awaited)


def columns_kernel(group, width, weights_ref, out_ref):
    for s in range(group):
        for third in range(3):
            start = third * group * width + s * width
            out_ref[s, :, third * width : (third + 1) * width] = weights_ref[
                0, :, start : start + width
            ]


def columns_of(weights, layer, group, width, awaited=()):
    _, shard, total = weights.shape
    return run(
        functools.partial(columns_kernel, group, width),
        "columns_of",
        (1,),
        [weights],
        [pl.BlockSpec((1, shard, total), lambda i, *_: (layer, 0, 0))],
        shape_of(BF16, group, shard, 3 * width),
        fixed_spec(group, shard, 3 * width),
        cost=(0, 4 * shard * total),
        awaited=awaited,
    )


def stack_columns_kernel(place, *refs):
    pieces, (pair_ref, reset_ref, flags_ref) = refs[:-3], refs[-3:]
    group = len(pieces)
    half = group // 2
    shard = pair_ref.shape[0] // group
    both = pair_ref.shape[1]
    for k in range(group):
        at = (place[1] ^ (k // half)) * half + (place[2] ^ (k % half))
        here = pl.ds(pl.multiple_of(at * shard, shard), shard)
        pair_ref[here, :] = pieces[k][:shard, :both]
        reset_ref[here, :] = pieces[k][:shard, both:]
        flags_ref[at] = pieces[k][shard:, :LANES]


def stack_columns(place, pieces, shard, awaited):
    group = len(pieces)
    rows, total = pieces[0].shape
    outs = [
        (group * shard, total // 3 * 2),
        (group * shard, total // 3),
        (group, rows - shard, LANES),
    ]
    return run(
        stack_columns_kernel,
        "stack_columns",
        (1,),
        pieces,
        [fixed_spec(rows, total)] * group,
        [shape_of(BF16, *out) for out in outs],
        [fixed_spec(*out) for out in outs],
        (),
        place,
        (0, 4 * group * shard * total),
        awaited,
    )


def send_columns_kernel(group, width, place, weights_ref, flags_ref, *outs):
    half = group // 2
    shard = weights_ref.shape[1]
    below = flags_ref[...].astype(F32)
    fill = jnp.zeros((outs[0].shape[0] - shard - below.shape[0], below.shape[1]), F32)
    below = jnp.concatenate([below, fill]).astype(BF16)
    for k in range(group):
        at = (place[1] ^ (k // half)) * half + (place[2] ^ (k % half))
        for third in range(3):
            start = pl.multiple_of(third * group * width + at * width, width)
            outs[k][:shard, third * width : (third + 1) * width] = weights_ref[
                0, :, pl.ds(start, width)
            ]
        outs[k][shard:, :] = jnp.zeros_like(outs[k][shard:, :])
        outs[k][shard:, : flags_ref.shape[1]] = below


def send_columns(place, weights, layer, group, width, flags):
    _, shard, total = weights.shape
    rows = shard + 2 * SUBLANES
    return run(
        functools.partial(send_columns_kernel, group, width),
        "send_columns",
        (1,),
        [weights, flags],
        [pl.BlockSpec((1, shard, total), lambda i, *_: (layer, 0, 0)), fixed_spec(*flags.shape)],
        [shape_of(BF16, rows, 3 * width)] * group,
        [fixed_spec(rows, 3 * width)] * group,
        (),
        place,
        (0, 4 * shard * total),
    )


def first_norm_kernel(group, x_ref, grad_ref, gain_ref, bias_ref, *refs):
    split_ref = refs[-1]
    rows, span, model = x_ref.shape
    width = model // group
    for i in range(rows):

        def part(here):
            wide = x_ref[i, here, :].astype(F32)
            centered = wide - jnp.mean(wide, axis=-1, keepdims=True)
            scale = lax.rsqrt(jnp.mean(centered * centered, axis=-1, keepdims=True) + 1e-05)
            refs[i][here, :] = (
                centered * scale * gain_ref[0:1, :] + bias_ref[0:1, :]
            ).astype(BF16)

        chunks(span, 16, part)
        for s in range(group):
            columns = slice(s * width, (s + 1) * width)
            split_ref[s, 0, i] = x_ref[i, :, columns]
            split_ref[s, 1, i] = grad_ref[i, :, columns]


def first_norm(x, grad, gain, bias, group, awaited):
    rows, span, model = x.shape
    split = (group, 2, rows, span, model // group)
    return run(
        functools.partial(first_norm_kernel, group),
        "first_norm",
        (1,),
        [x, grad, gain, bias],
        [fixed_spec(*a.shape) for a in (x, grad, gain, bias)],
        [shape_of(BF16, span, model)] * rows + [shape_of(BF16, *split)],
        [fixed_spec(span, model)] * rows + [fixed_spec(*split)],
        cost=(20 * rows * span * model, 8 * rows * span * model),
        awaited=awaited,
    )


def project_kernel(layer, gather, slots, place, *refs):
    pieces = refs[:slots]
    w_ref, order_ref, keep_ref, vec_ref = refs[slots : slots + 4]
    cf_ref, whole_ref, tot_ref, held, forget_s = refs[slots + 4 :]
    width = cf_ref.shape[1] // 2
    step = pl.program_id(0)
    gather(place, step, pieces, order_ref, held, whole_ref)
    cf_ref[...] = jnp.dot(whole_ref[...], w_ref[...], preferred_element_type=F32)

    def gates(here):
        forget_s[here, :] = forget_gate(cf_ref, here, vec_ref, layer)

    chunks(cf_ref.shape[0], 64, gates)

    @pl.when(step == 0)
    def _():
        tot_ref[0] = jnp.ones_like(tot_ref[0])
        tot_ref[1] = jnp.zeros_like(tot_ref[1])

    def one(at, state):
        forget = forget_s[at, :]
        decay = forget * widen(keep_ref[at, :], width)
        return state[0] * decay, state[1] * decay + (1.0 - forget) * cf_ref[at, :width]

    product, state = over_time(one, (tot_ref[0], tot_ref[1]))
    tot_ref[0] = product
    tot_ref[1] = state


def gather_rows(per, group, place, step, pieces, order_ref, held, whole_ref):
    half = group // 2
    other = (step // per) ^ place[1]
    for side in range(2):

        @pl.when(other == side)
        def _():
            for k in range(half):
                for i in range(2):
                    held[place[2] ^ k, i] = pieces[2 * (side * half + k) + i][...]

    def put(here, value):
        whole_ref[here, :] = value.astype(BF16)

    to_time(order_ref, held[...].reshape(-1, STEPS, whole_ref.shape[1]), put)


def gather_features(per, group, place, step, pieces, order_ref, held, whole_ref):
    half = group // 2
    width = whole_ref.shape[1] // group
    for side in range(2):

        @pl.when(step // per == side)
        def _():
            for k in range(group):
                at = (place[1] ^ (k // half)) * half + (place[2] ^ (k % half))
                whole_ref[:, quarter(at, width)] = pieces[2 * k + side][...]


def project(place, layer, pieces, matrix, order, keep, vectors, rows, by_rows):
    model = matrix.shape[0]
    width = vectors.shape[1]
    both = 2 * width
    tokens = keep.shape[0]
    block = rows * STEPS
    count = tokens // block
    per = count // 2
    group = model // width
    half = group // 2
    specs = []
    for k in range(group):
        for side in range(2):
            if by_rows:

                def index(i, place, needed=k // half):
                    mine = ((i // per) ^ place[1]) == needed
                    return (jnp.where(mine, i % per, 0), 0)

                specs.append(pl.BlockSpec((STEPS, model), index))
            elif side == 0:
                specs.append(
                    pl.BlockSpec((block, width), lambda i, place: (jnp.minimum(i, per - 1), 0))
                )
            else:
                specs.append(
                    pl.BlockSpec((block, width), lambda i, place: (jnp.maximum(i - per, 0), 0))
                )
    gather = functools.partial(gather_rows if by_rows else gather_features, per, group)
    held = pltpu.VMEM((half, 2, STEPS, model) if by_rows else (2 * SUBLANES, LANES), BF16)
    return run(
        functools.partial(project_kernel, layer, gather, len(pieces)),
        "project",
        (count,),
        [*pieces, matrix, order, keep, vectors],
        specs
        + [
            fixed_spec(model, both),
            fixed_spec(*order.shape),
            block_spec(block, LANES),
            fixed_spec(*vectors.shape),
        ],
        [
            shape_of(F32, tokens, both),
            shape_of(BF16, tokens, model),
            shape_of(F32, 2, rows, width),
        ],
        [block_spec(block, both), block_spec(block, model), fixed_spec(2, rows, width)],
        [held, pltpu.VMEM((block, width), F32)],
        place,
        (2 * tokens * model * both, 4 * tokens * model + 4 * tokens * both + 2 * model * both),
    )


def reset_kernel(x_ref, w_ref, out_ref):
    out_ref[...] = jnp.dot(x_ref[...], w_ref[...], preferred_element_type=F32)


def reset_product(whole, matrix, width):
    tokens, model = whole.shape
    last = matrix.shape[1] // width - 1
    block = tokens // 4
    return run(
        reset_kernel,
        "reset_product",
        (4,),
        [whole, matrix],
        [block_spec(block, model), pl.BlockSpec((model, width), lambda *_: (0, last))],
        shape_of(F32, tokens, width),
        block_spec(block, width),
        cost=(2 * tokens * model * width, 2 * tokens * model + 4 * tokens * width),
    )


def carry_forward(layer, cf_ref, keep_ref, vec_ref, far, carry_s, forget_s, prev_ref, state_s):
    width = prev_ref.shape[1]

    def gates(here):
        forget_s[here, :] = forget_gate(cf_ref, here, vec_ref, layer)

    chunks(forget_s.shape[0], 64, gates)

    @pl.when(pl.program_id(0) == 0)
    def _():
        first = incoming(far)
        carry_s[...] = jnp.zeros_like(carry_s) if first is None else first

    def one(at, state):
        forget = forget_s[at, :]
        prev = widen(keep_ref[at, :], width) * state
        new = forget * prev + (1.0 - forget) * cf_ref[at, :width]
        prev_ref[at, :] = prev
        state_s[at, :] = new
        return new

    carry_s[...] = over_time(one, carry_s[...])


def reset_gate(layer, ur_ref, prev_ref, here, vec_ref):
    return jax.nn.sigmoid(
        ur_ref[here, :]
        + row_at(vec_ref, layer, PEEP) * prev_ref[here, :]
        + row_at(vec_ref, layer, RESET)
    )


def advance_kernel(layer, cf_ref, ur_ref, x_ref, keep_ref, order_ref, vec_ref, *refs):
    xn_ref, stat_ref, carry_s, forget_s, prev_s, state_s, x_s = refs[-7:]
    far = refs[:-7]
    block, width = xn_ref.shape

    def put(here, value):
        x_s[here, :] = value

    to_time(order_ref, x_ref[...].reshape(-1, STEPS, width), put)
    carry_forward(layer, cf_ref, keep_ref, vec_ref, far, carry_s, forget_s, prev_s, state_s)

    def finish(here):
        gate = reset_gate(layer, ur_ref, prev_s, here, vec_ref)
        xn = gate * state_s[here, :] + (1.0 - gate) * x_s[here, :]
        xn_ref[here, :] = xn
        mean = jnp.mean(xn, axis=-1, keepdims=True)
        off = xn - mean
        spread = sum(off[:, j : j + LANES] * off[:, j : j + LANES] for j in range(0, width, LANES))
        x_s[here, :LANES] = jnp.broadcast_to(mean, (here.size, LANES))
        state_s[here, :LANES] = spread

    chunks(block, 64, finish)
    for b in range(block // LANES):
        here = slice(b * LANES, (b + 1) * LANES)
        row = pl.ds(pl.program_id(0) * (block // LANES) + b, 1)
        stat_ref[0, row, :] = x_s[here, :LANES].T[0:1, :]
        stat_ref[1, row, :] = jnp.sum(state_s[here, :LANES].T, axis=0, keepdims=True)


def advance(layer, cf, ur, x, keep, order, vectors, far):
    tokens, width = ur.shape
    _, half, _, rows_dev, span, _ = x.shape
    rows = half * rows_dev
    block = rows * STEPS
    part = block_spec(block, width)
    return run(
        functools.partial(advance_kernel, layer),
        "advance",
        (tokens // block,),
        [cf, ur, x, keep, order, vectors, *far],
        [
            block_spec(block, 2 * width),
            part,
            split_spec(half, rows_dev, width, span // STEPS, 0),
            block_spec(block, LANES),
            fixed_spec(*order.shape),
            fixed_spec(*vectors.shape),
        ]
        + [fixed_spec(2, rows, width)] * len(far),
        [shape_of(F32, tokens, width), shape_of(F32, 2, tokens // LANES, LANES)],
        [part, fixed_spec(2, tokens // LANES, LANES)],
        [pltpu.VMEM((rows, width), F32)] + [pltpu.VMEM((block, width), F32)] * 4,
        None,
        (60 * tokens * width, 22 * tokens * width),
    )


def middle_norm_kernel(layer, model, xn_ref, stat_ref, vec_ref, a_ref, b_ref, mean_ref, scale_ref):
    group = stat_ref.shape[0]
    block, width = xn_ref.shape
    for b in range(block // LANES):
        row = pl.ds(pl.program_id(0) * (block // LANES) + b, 1)
        here = slice(b * LANES, (b + 1) * LANES)
        means = [stat_ref[s, 0, row, :] for s in range(group)]
        mean = sum(means) / group
        square = sum(stat_ref[s, 1, row, :] for s in range(group))
        between = sum((part - mean) * (part - mean) for part in means)
        scale = lax.rsqrt((square + between * width) / model + 1e-05)
        mean_ref[here, :] = jnp.broadcast_to(mean, (LANES, LANES)).T
        scale_ref[here, :] = jnp.broadcast_to(scale, (LANES, LANES)).T

    per = pl.num_programs(0) // 2
    for side, normed_ref in enumerate((a_ref, b_ref)):

        @pl.when(pl.program_id(0) // per == side)
        def _():
            def part(here):
                normed_ref[here, :] = (
                    (xn_ref[here, :] - widen(mean_ref[here, :], width))
                    * widen(scale_ref[here, :], width)
                    * row_at(vec_ref, layer, GAIN)
                    + row_at(vec_ref, layer, BIAS)
                ).astype(BF16)

            chunks(block, 64, part)


def middle_norm(layer, model, xn, stats, vectors, rows):
    tokens, width = xn.shape
    block = rows * STEPS
    per = tokens // block // 2
    return run(
        functools.partial(middle_norm_kernel, layer, model),
        "middle_norm",
        (tokens // block,),
        [xn, stats, vectors],
        [block_spec(block, width), fixed_spec(*stats.shape), fixed_spec(*vectors.shape)],
        [shape_of(BF16, tokens // 2, width)] * 2 + [shape_of(F32, tokens, LANES)] * 2,
        [
            pl.BlockSpec((block, width), lambda i, *_: (jnp.minimum(i, per - 1), 0)),
            pl.BlockSpec((block, width), lambda i, *_: (jnp.maximum(i - per, 0), 0)),
        ]
        + [block_spec(block, LANES)] * 2,
        cost=(10 * tokens * width, 8 * tokens * width),
    )


def add_total(decay_s, drive_s, tot_ref):
    @pl.when(pl.program_id(0) == 0)
    def _():
        tot_ref[0] = jnp.ones_like(tot_ref[0])
        tot_ref[1] = jnp.zeros_like(tot_ref[1])

    def one(at, state):
        return state[0] * decay_s[at, :], state[1] + state[0] * drive_s[at, :]

    product, total = over_time(one, (tot_ref[0], tot_ref[1]))
    tot_ref[0] = product
    tot_ref[1] = total


def turn_kernel(layer, cf_ref, ur_ref, x_ref, dh_ref, keep_ref, order_ref, back_ref, vec_ref, *refs):
    prev_ref, dr_ref, dc_ref, high_ref, out_ref, du_ref, tot_ref, small_ref = refs[-14:-6]
    carry_s, forget_s, state_s, dh_s, drive_s, out_s = refs[-6:]
    far = refs[:-14]
    block, width = prev_ref.shape

    def put(here, value):
        dh_s[here, :] = value

    to_time(order_ref, dh_ref[...].reshape(-1, STEPS, width), put)
    carry_forward(layer, cf_ref, keep_ref, vec_ref, far, carry_s, forget_s, prev_ref, state_s)

    @pl.when(pl.program_id(0) == 0)
    def _():
        small_ref[...] = jnp.zeros_like(small_ref)

    def finish(here):
        state = state_s[here, :]
        x = x_ref[here, :]
        dh = dh_s[here, :]
        prev = prev_ref[here, :]
        gate = reset_gate(layer, ur_ref, prev_ref, here, vec_ref)
        out_s[here, :] = (gate * state + (1.0 - gate) * x).astype(BF16)
        dr = dh * (state - x) * gate * (1.0 - gate)
        dc = dh * gate
        dr_ref[here, :] = dr
        dc_ref[here, :] = dc
        du_ref[here, :] = dr.astype(BF16)
        high_ref[here, :] = dh - dc
        keep = widen(keep_ref[here, :], width)
        decay = keep * forget_s[here, :]
        state_s[here, :] = decay
        drive_s[here, :] = keep * row_at(vec_ref, layer, PEEP) * dr + decay * dc
        small_ref[0] += fold(dr * prev)
        small_ref[1] += fold(dr)

    chunks(block, 32, finish)
    to_rows(back_ref, out_s, out_ref)
    add_total(state_s, drive_s, tot_ref)


def turn(layer, cf, ur, x, dh, keep, order, back, vectors, far):
    tokens, width = ur.shape
    _, half, _, rows_dev, span, _ = dh.shape
    rows = half * rows_dev
    block = rows * STEPS
    part = block_spec(block, width)
    by_rows = rows_spec(rows, width, span // STEPS)
    return run(
        functools.partial(turn_kernel, layer),
        "turn",
        (tokens // block,),
        [cf, ur, x, dh, keep, order, back, vectors, *far],
        [
            block_spec(block, 2 * width),
            part,
            part,
            split_spec(half, rows_dev, width, span // STEPS, 1),
            block_spec(block, LANES),
            fixed_spec(*order.shape),
            fixed_spec(*back.shape),
            fixed_spec(*vectors.shape),
        ]
        + [fixed_spec(2, rows, width)] * len(far),
        [shape_of(F32, tokens, width)] * 4
        + [
            shape_of(BF16, 2, rows, span, width),
            shape_of(BF16, tokens, width),
            shape_of(F32, 2, rows, width),
            shape_of(F32, 2, SUBLANES, width),
        ],
        [part] * 4
        + [by_rows, part, fixed_spec(2, rows, width), fixed_spec(2, SUBLANES, width)],
        [pltpu.VMEM((rows, width), F32)]
        + [pltpu.VMEM((block, width), F32)] * 4
        + [pltpu.VMEM((block, width), BF16)],
        None,
        (80 * tokens * width, 36 * tokens * width),
    )


def retreat_kernel(layer, sums, dc_ref, dr_ref, prev_ref, cf_ref, keep_ref, vec_ref, *refs):
    if sums:
        ur_ref, mixed_ref = refs[:2]
        du_ref, small_ref, stat_ref, carry_s, forget_s, total_s, sum_s, cross_s = refs[-8:]
        far = refs[2:-8]
    else:
        back_ref = refs[0]
        du_ref, rows_ref, small_ref, carry_s, forget_s, total_s = refs[-6:]
        far = refs[1:-6]
    block, width = prev_ref.shape
    peep = row_at(vec_ref, layer, PEEP)

    @pl.when(pl.program_id(0) == 0)
    def _():
        first = incoming(far)
        carry_s[...] = jnp.zeros_like(carry_s) if first is None else first
        small_ref[...] = jnp.zeros_like(small_ref)

    def gates(here):
        forget_s[here, :] = forget_gate(cf_ref, here, vec_ref, layer)

    chunks(block, 64, gates)

    def one(at, state):
        total = dc_ref[at, :] + state
        total_s[at, :] = total
        return widen(keep_ref[at, :], width) * (peep * dr_ref[at, :] + forget_s[at, :] * total)

    carry_s[...] = over_time(one, carry_s[...], True)

    def halves(value):
        return sum(value[:, j : j + LANES] for j in range(0, width, LANES))

    def finish(here):
        forget = forget_s[here, :]
        slow = total_s[here, :] * (1.0 - forget)
        d_forget = slow * forget * (prev_ref[here, :] - cf_ref[here, :width])
        d_cand = slow.astype(BF16)
        d_gate = d_forget.astype(BF16)
        du_ref[here, :width] = d_cand
        du_ref[here, width:] = d_gate
        small_ref[...] += fold(d_forget)
        if sums:
            parts = [d_cand, d_gate, dr_ref[here, :].astype(BF16)]
            inputs = [cf_ref[here, :width], cf_ref[here, width:], ur_ref[here, :]]
            plain = cross = 0.0
            for third in range(3):
                at = slice(third * width, (third + 1) * width)
                du = parts[third].astype(F32)
                plain = plain + du * mixed_ref[0:1, at]
                cross = cross + du * (inputs[third] - mixed_ref[1:2, at])
            sum_s[here, :] = halves(plain)
            cross_s[here, :] = halves(cross)

    chunks(block, 32, finish)
    if sums:
        base = (pl.num_programs(0) - 1 - pl.program_id(0)) * (block // LANES)
        for b in range(block // LANES):
            here = slice(b * LANES, (b + 1) * LANES)
            stat_ref[0, pl.ds(base + b, 1), :] = jnp.sum(sum_s[here, :].T, axis=0, keepdims=True)
            stat_ref[1, pl.ds(base + b, 1), :] = jnp.sum(cross_s[here, :].T, axis=0, keepdims=True)
    else:
        to_rows(back_ref, du_ref, rows_ref)


def retreat(layer, dc, dr, prev, cf, keep, vectors, far, rows, span, awaited, back=None, ur=None, mixed=None):
    tokens, width = dc.shape
    block = rows * STEPS
    count = tokens // block
    sums = back is None
    part = turned_spec(block, width, count)
    both = turned_spec(block, 2 * width, count)
    rows_out = rows_spec(rows, 2 * width, span // STEPS, lambda i: count - 1 - i)
    outs = [shape_of(BF16, tokens, 2 * width)]
    specs = [both]
    scratch = [pltpu.VMEM((rows, width), F32)] + [pltpu.VMEM((block, width), F32)] * 2
    if sums:
        more, more_specs = [ur, mixed], [part, fixed_spec(*mixed.shape)]
        outs += [shape_of(F32, SUBLANES, width), shape_of(F32, 2, tokens // LANES, LANES)]
        specs += [fixed_spec(SUBLANES, width), fixed_spec(2, tokens // LANES, LANES)]
        scratch += [pltpu.VMEM((block, LANES), F32)] * 2
    else:
        more, more_specs = [back], [fixed_spec(*back.shape)]
        outs += [shape_of(BF16, 2, rows, span, 2 * width), shape_of(F32, SUBLANES, width)]
        specs += [rows_out, fixed_spec(SUBLANES, width)]
    return run(
        functools.partial(retreat_kernel, layer, sums),
        "retreat",
        (count,),
        [dc, dr, prev, cf, keep, vectors, *more, *far],
        [part] * 3
        + [both, turned_spec(block, LANES, count), fixed_spec(*vectors.shape)]
        + more_specs
        + [fixed_spec(2, rows, width)] * len(far),
        outs,
        specs,
        scratch,
        None,
        (60 * tokens * width, 30 * tokens * width),
        awaited,
    )


def back_product(pair, reset, w_pair, w_reset):
    contract = (((1,), (1,)), ((), ()))
    return lax.dot_general(pair, w_pair, contract, preferred_element_type=F32) + lax.dot_general(
        reset, w_reset, contract, preferred_element_type=F32
    )


def put_shares(share_of, outs):
    odd, even = outs
    for k in range(odd.shape[0]):
        odd[k] = share_of(k).astype(BF16)
        even[k] = share_of(odd.shape[0] + k)


def share_outs(count, rows, columns):
    return [shape_of(dtype, count // 2, rows, columns) for dtype in (BF16, F32)]


def back_features_kernel(count, order, pair_ref, reset_ref, *refs):
    def share_of(k):
        return back_product(
            pair_ref[...], reset_ref[...], refs[2 * k][...], refs[2 * k + 1][...]
        )

    put_shares(share_of, refs[-2:])


def back_features(order, pair, reset, matrix, awaited):
    tokens, width = reset.shape
    count = order.shape[0]
    block = tokens // 4
    specs = []
    for k in range(count):
        specs.append(pl.BlockSpec((width, 2 * width), lambda i, order, k=k: (order[k], 0)))
        specs.append(pl.BlockSpec((width, width), lambda i, order, k=k: (order[k], 2)))
    outs = share_outs(count, tokens, width)
    return run(
        functools.partial(back_features_kernel, count),
        "back_features",
        (4,),
        [pair, reset] + [matrix, matrix] * count,
        [block_spec(block, 2 * width), block_spec(block, width)] + specs,
        outs,
        [pl.BlockSpec((out.shape[0], block, width), lambda i, order: (0, i, 0)) for out in outs],
        (),
        order,
        (6 * count * tokens * width * width, 8 * count * tokens * width),
        awaited,
    )


def back_tokens_kernel(count, order, wp_ref, wr_ref, *refs):
    local = refs[-1].shape[1]

    def share_of(k):
        pair, reset = refs[2 * k : 2 * k + 2]
        return back_product(
            pair[0].reshape(local, pair.shape[-1]),
            reset[0].reshape(local, reset.shape[-1]),
            wp_ref[...],
            wr_ref[...],
        )

    put_shares(share_of, refs[-2:])


def back_tokens(order, pair, reset, w_pair, w_reset, awaited):
    two, rows, span, width = reset.shape
    model = w_pair.shape[0]
    count = order.shape[0]
    half = model // width // 2
    rows_dev = rows // half
    local = rows_dev * span
    block = model // 4
    specs = []
    for k in range(count):
        by_order = lambda i, order, k=k: (order[k] // half, order[k] % half, 0, 0)
        for columns in (2 * width, width):
            specs.append(pl.BlockSpec((1, rows_dev, span, columns), by_order))
    outs = share_outs(count, local, model)
    return run(
        functools.partial(back_tokens_kernel, count),
        "back_tokens",
        (4,),
        [w_pair, w_reset] + [pair, reset] * count,
        [block_spec(block, 2 * width), block_spec(block, width)] + specs,
        outs,
        [pl.BlockSpec((out.shape[0], local, block), lambda i, order: (0, 0, i)) for out in outs],
        (),
        order,
        (6 * count * local * model * width, 8 * count * local * model),
        awaited,
    )


def middle_back_kernel(layer, model, *refs):
    (
        kept_ref, core_ref, pair_ref, line_ref, high_ref, x_ref, mean_ref, scale_ref, stat_ref,
        cf_ref, ur_ref, below_x_ref, keep_ref, order_ref, back_ref, vec_ref,
    ) = refs[:16]
    (
        prev_ref, dr_ref, dc_ref, below_ref, du_ref, rows_ref, tot_ref, small_ref,
        carry_s, forget_s, state_s, drive_s, x_s, plain_s, cross_s, below_s,
    ) = refs[-16:]
    far = refs[16:-16]
    block, width = prev_ref.shape
    below = layer - 1

    def put(here, value):
        x_s[here, :] = value

    to_time(order_ref, below_x_ref[...].reshape(-1, STEPS, width), put)
    carry_forward(below, cf_ref, keep_ref, vec_ref, far, carry_s, forget_s, prev_ref, state_s)
    for b in range(block // LANES):
        row = pl.ds(pl.program_id(0) * (block // LANES) + b, 1)
        here = slice(b * LANES, (b + 1) * LANES)
        for s, out in enumerate((plain_s, cross_s)):
            out[here, :] = jnp.broadcast_to(stat_ref[s, row, :] / model, (LANES, LANES)).T

    @pl.when(pl.program_id(0) == 0)
    def _():
        small_ref[...] = jnp.zeros_like(small_ref)

    def finish(here):
        back = (
            kept_ref[0, here, :]
            + core_ref[0, here, :].astype(F32)
            + pair_ref[here, :].astype(F32)
            + line_ref[here, :].astype(F32)
        )
        scale = widen(scale_ref[here, :], width)
        xhat = (x_ref[here, :] - widen(mean_ref[here, :], width)) * scale
        dh = high_ref[here, :] + scale * (
            back * row_at(vec_ref, layer, GAIN)
            - widen(plain_s[here, :], width)
            - xhat * widen(cross_s[here, :], width)
        )
        small_ref[0] += fold(back * xhat)
        small_ref[1] += fold(back)
        gate = reset_gate(below, ur_ref, prev_ref, here, vec_ref)
        dr = dh * (state_s[here, :] - x_s[here, :]) * gate * (1.0 - gate)
        dc = dh * gate
        dr_ref[here, :] = dr
        dc_ref[here, :] = dc
        du_ref[here, :] = dr.astype(BF16)
        below_s[here, :] = (dh - dc).astype(BF16)
        keep = widen(keep_ref[here, :], width)
        decay = keep * forget_s[here, :]
        state_s[here, :] = decay
        drive_s[here, :] = keep * row_at(vec_ref, below, PEEP) * dr + decay * dc
        small_ref[2] += fold(dr * prev_ref[here, :])
        small_ref[3] += fold(dr)

    chunks(block, 32, finish)
    to_rows(back_ref, below_s, below_ref)
    to_rows(back_ref, du_ref, rows_ref)
    add_total(state_s, drive_s, tot_ref)


def middle_back(
    layer, model, kept, core, pair, line, high, x, mean, scale, stats, cf, ur, below_x, keep, order,
    back, vectors, far,
):
    tokens, width = ur.shape
    _, half, _, rows_dev, span, _ = below_x.shape
    rows = half * rows_dev
    block = rows * STEPS
    part = block_spec(block, width)
    last = kept.shape[0] - 1
    top = pl.BlockSpec((1, block, width), lambda i, *_: (last, i, 0))
    thin = block_spec(block, LANES)
    by_rows = rows_spec(rows, width, span // STEPS)
    held = pltpu.VMEM((block, width), F32)
    return run(
        functools.partial(middle_back_kernel, layer, model),
        "middle_back",
        (tokens // block,),
        [
            kept, core, pair, line, high, x, mean, scale, stats, cf, ur, below_x, keep, order, back,
            vectors, *far,
        ],
        [top, top, part, part, part, part, thin, thin, fixed_spec(*stats.shape)]
        + [
            block_spec(block, 2 * width),
            part,
            split_spec(half, rows_dev, width, span // STEPS, 0),
            thin,
            fixed_spec(*order.shape),
            fixed_spec(*back.shape),
            fixed_spec(*vectors.shape),
        ]
        + [fixed_spec(2, rows, width)] * len(far),
        [shape_of(F32, tokens, width)] * 3
        + [
            shape_of(BF16, 2, rows, span, width),
            shape_of(BF16, tokens, width),
            shape_of(BF16, 2, rows, span, width),
            shape_of(F32, 2, rows, width),
            shape_of(F32, 4, SUBLANES, width),
        ],
        [part, part, part, by_rows, part, by_rows]
        + [fixed_spec(2, rows, width), fixed_spec(4, SUBLANES, width)],
        [pltpu.VMEM((rows, width), F32)]
        + [held] * 4
        + [pltpu.VMEM((block, LANES), F32)] * 2
        + [pltpu.VMEM((block, width), BF16)],
        None,
        (80 * tokens * width, 44 * tokens * width),
    )


def first_back_kernel(kept_ref, core_ref, pair_ref, line_ref, x_ref, gain_ref, high_ref, out_ref, small_ref):
    local, model = x_ref.shape
    group, _, width = high_ref.shape

    @pl.when(pl.program_id(0) == 0)
    def _():
        small_ref[...] = jnp.zeros_like(small_ref)

    def part(here):
        wide = x_ref[here, :].astype(F32)
        centered = wide - jnp.mean(wide, axis=-1, keepdims=True)
        scale = lax.rsqrt(jnp.mean(centered * centered, axis=-1, keepdims=True) + 1e-05)
        xhat = centered * scale
        back = (
            kept_ref[0, here, :]
            + core_ref[0, here, :].astype(F32)
            + pair_ref[here, :].astype(F32)
            + line_ref[here, :].astype(F32)
        )
        scaled = back * gain_ref[0:1, :]
        small_ref[0] += fold(back * xhat)
        small_ref[1] += fold(back)
        total = scale * (
            scaled
            - jnp.mean(scaled, axis=-1, keepdims=True)
            - xhat * jnp.mean(scaled * xhat, axis=-1, keepdims=True)
        )
        for s in range(group):
            columns = slice(s * width, (s + 1) * width)
            out_ref[here, columns] = (total[:, columns] + high_ref[s, here, :].astype(F32)).astype(
                BF16
            )

    chunks(local, 16, part)


def first_back(kept, core, pair, line, x, gain, high):
    local, model = x.shape
    group, _, width = high.shape
    last = kept.shape[0] - 1
    block = local // 4
    top = pl.BlockSpec((1, block, model), lambda i, *_: (last, i, 0))
    flat = block_spec(block, model)
    return run(
        first_back_kernel,
        "first_back",
        (4,),
        [kept, core, pair, line, x, gain, high],
        [top, top, flat, flat, flat, fixed_spec(*gain.shape)]
        + [pl.BlockSpec((group, block, width), lambda i, *_: (0, i, 0))],
        [shape_of(BF16, local, model), shape_of(F32, 2, SUBLANES, model)],
        [flat, fixed_spec(2, SUBLANES, model)],
        cost=(30 * local * model, 16 * local * model),
    )


def weight_kernel(whole_ref, pair_ref, reset_ref, out_ref):
    both = pair_ref.shape[1]
    contract = (((0,), (0,)), ((), ()))
    for du_ref, at in ((pair_ref, slice(0, both)), (reset_ref, slice(both, out_ref.shape[1]))):
        out_ref[:, at] = lax.dot_general(
            whole_ref[...], du_ref[...], contract, preferred_element_type=F32
        ).astype(BF16)


def weight_term(whole, pair, reset, awaited=()):
    tokens, model = whole.shape
    width = reset.shape[1]
    block = model // 4
    return run(
        weight_kernel,
        "weight_term",
        (4,),
        [whole, pair, reset],
        [
            pl.BlockSpec((tokens, block), lambda k, *_: (0, k)),
            fixed_spec(*pair.shape),
            fixed_spec(*reset.shape),
        ],
        shape_of(BF16, model, 3 * width),
        block_spec(block, 3 * width),
        cost=(6 * tokens * model * width, 2 * tokens * model + 6 * model * width),
        awaited=awaited,
    )


def join_kernel(x_ref, out_ref):
    group, rows, width = x_ref.shape
    for s in range(group):
        out_ref[:, s * width : (s + 1) * width] = x_ref[s]


def join(value):
    group, rows, width = value.shape
    return run(
        join_kernel,
        "join",
        (1,),
        [value],
        [fixed_spec(group, rows, width)],
        shape_of(value.dtype, rows, group * width),
        fixed_spec(rows, group * width),
        cost=(0, 4 * rows * group * width),
    )


def join_weights_kernel(part_ref, out_ref):
    layers, _, total = out_ref.shape
    group = part_ref.shape[0]
    width = total // group // 3
    for layer in range(layers):
        for s in range(group):
            for third in range(3):
                start = third * group * width + s * width
                at = (3 * layer + third) * width
                out_ref[layer, :, start : start + width] = part_ref[s, :, at : at + width].astype(
                    F32
                )


def join_weights(part, layers):
    group, shard, total = part.shape
    shape = (layers, shard, group * total // layers)
    return run(
        join_weights_kernel,
        "join_weights",
        (1,),
        [part],
        [fixed_spec(*part.shape)],
        shape_of(F32, *shape),
        fixed_spec(*shape),
        cost=(0, 12 * group * shard * total),
    )


def swap(value, bits, size):
    return lax.ppermute(value, GROUP, [(i, i ^ bits) for i in range(size)])


def gather_group(a, b, size, awaited=()):
    pair_a = swap(a, PAIR, size)
    line_b = swap(b, LINE, size)
    a, b = after([a, b], pair_a, line_b, *awaited)
    pair_b = swap(b, PAIR, size)
    line_a = swap(a, LINE, size)
    far_a = swap(pair_a, LINE, size)
    far_b = swap(line_b, PAIR, size)
    halves = [a, b, line_a, line_b, pair_a, pair_b, far_a, far_b]
    cores = [swap(half, CORE, size) for half in halves]
    return [
        half
        for k in range(0, 8, 2)
        for half in (halves[k], halves[k + 1], cores[k], cores[k + 1])
    ]


def reduce_group(shares, size, stats, soon, filler):
    far_odd, far_even = shares((7, 6), ())
    far_core = swap(far_odd, CORE, size)
    filled = filler((far_odd,))
    far = (far_even[0] + far_core[0].astype(F32)).astype(BF16)
    half = far.shape[0] // 2
    far_a, far_b = after([far[:half], far[half:]], filled)
    by_pair = swap(far_a, PAIR, size)
    by_line = swap(far_b, LINE, size)
    odd, even = shares((5, 3, 1, 4, 2, 0), (far_a, far_b))
    core = swap(odd, CORE, size)
    if soon:
        (even,) = after([even], *soon)
    stats = [part + swap(part, CORE, size) for part in stats]
    zeros = jnp.zeros_like(by_pair)
    by_line = jnp.concatenate([zeros, by_line]).astype(F32)
    by_pair = jnp.concatenate([by_pair, zeros]).astype(F32)
    pair = (even[0] + core[0].astype(F32) + by_line).astype(BF16)
    line = (even[1] + core[1].astype(F32) + by_pair).astype(BF16)
    if stats:
        stats = after(stats, pair, line)
        stats = [
            part + sum(swap(part, bits, size) for bits in (LINE, PAIR, LINE | PAIR))
            for part in stats
        ]
    return even, core, swap(pair, PAIR, size), swap(line, LINE, size), stats


def exchange(part, size, reverse):
    far = []
    for hop in range(1, size):
        pairs = [(i, i + hop) for i in range(size - hop)]
        if reverse:
            pairs = [(b, a) for a, b in pairs]
        far.append(lax.ppermute(part, "ring", pairs))
    return far


def spread_small(vectors, ring, size, awaited):
    me = lax.axis_index("ring")
    width = vectors.shape[1] // ring

    def part(hop):
        start = lax.rem(me + hop, ring) * width
        return lax.dynamic_slice_in_dim(vectors, start, width, 1)

    arrived = [
        lax.ppermute(part(hop), "ring", [(i, (i + hop) % ring) for i in range(ring)])
        for hop in range(1, ring)
    ]
    vectors = part(0) + sum(arrived)
    me = lax.axis_index(GROUP)
    bit = size // 2
    while bit:
        if bit == size // 2:
            (vectors,) = after([vectors], *awaited)
        width = vectors.shape[1] // 2
        mine = (me & bit) > 0
        low, high = vectors[:, :width], vectors[:, width:]
        vectors = jnp.where(mine, high, low) + swap(jnp.where(mine, low, high), bit, size)
        bit //= 2
    return vectors


def order_matrix(rows):
    index = np.arange(rows * SUB)
    return (index % rows * SUB + index // rows)[:, None] == index[None, :]


def to_group(value):
    return lax.all_to_all(value, GROUP, split_axis=0, concat_axis=0, tiled=True)


def body(
    inputs,
    out_grad,
    reset_flags,
    weights,
    ln_gain,
    layer_norm_bias,
    reset_peep,
    forget_bias,
    reset_bias,
):
    rows_dev, span, model = inputs.shape
    layers, shard, _ = weights.shape
    ring = lax.axis_size("ring")
    half = lax.axis_size("rows")
    group = 2 * half
    place = jnp.stack([lax.axis_index("ring"), lax.axis_index("pair"), lax.axis_index("rows")])
    place = place.astype(jnp.int32)
    me = lax.axis_index(GROUP)
    width = model // group
    rows = rows_dev * half
    local = rows_dev * span
    tokens = 2 * rows * span
    order = jnp.asarray(order_matrix(rows), BF16)
    back = jnp.asarray(order_matrix(rows).T, BF16)

    columns = columns_of(weights, 1, group, width)
    mine = send_columns(place, weights, 0, group, width, reset_flags)
    got = [mine[0]] + [swap(mine[k], k, group) for k in range(1, group)]
    *normed, split = first_norm(inputs, out_grad, ln_gain, layer_norm_bias, group, (mine[0],))
    pair_mine, reset_mine, flags = stack_columns(place, got, shard, (normed[0], columns))
    pair_w1 = lax.all_gather(pair_mine, "ring", axis=0, tiled=True)
    reset_w1 = lax.all_gather(reset_mine, "ring", axis=0, tiled=True)
    flags = flags[:, :rows_dev, :span].reshape(2, rows, span)
    keep = (1.0 - flags.astype(F32)).transpose(0, 2, 1).reshape(tokens, 1)
    keep = jnp.broadcast_to(keep, (tokens, LANES))
    vectors = jnp.stack([ln_gain, layer_norm_bias, reset_peep, forget_bias, reset_bias], axis=1)
    vectors = lax.dynamic_slice_in_dim(vectors.reshape(layers * 5, model), me * width, width, 1)
    vectors = jnp.pad(vectors, ((0, 16 - layers * 5), (0, 0)))
    pieces1 = gather_group(*after(normed, pair_mine), group, (keep, vectors))

    cf1, whole1, part = project(place, 0, pieces1, pair_w1, order, keep, vectors, rows, True)
    far1 = exchange(part, ring, False)
    (split,) = after([split], *pieces1)
    split = to_group(split).reshape(2, half, 2, rows_dev, span, width)
    (columns,) = after([columns], split, *far1)
    columns = to_group(columns)
    ur1 = reset_product(whole1, reset_w1, width)
    (columns,) = after([columns], ur1)
    w2 = lax.all_gather(
        columns.reshape(group * shard, 3 * width), "ring", axis=0, tiled=True
    )
    x2, stats = advance(0, cf1, ur1, split, keep, order, vectors, far1)
    stats = lax.all_gather(stats, GROUP)
    *normed, mean2, scale2 = middle_norm(1, model, x2, stats, vectors, rows)

    def mixed():
        def thirds(value):
            high = value.astype(BF16)
            middle = (value - high.astype(F32)).astype(BF16)
            low = (value - high.astype(F32) - middle.astype(F32)).astype(BF16)
            return [high, middle, low]

        lines = jnp.stack(thirds(ln_gain[1]) + thirds(layer_norm_bias[1]))
        lines = jnp.pad(lines, ((0, 10), (0, 0)))
        both = jnp.dot(lines, w2, preferred_element_type=F32)
        return jnp.pad(jnp.sum(both[:6].reshape(2, 3, 3 * width), axis=1), ((0, 6), (0, 0)))

    pieces2 = gather_group(*normed, group)

    cf2, whole2, part = project(place, 1, pieces2, w2, order, keep, vectors, rows, False)
    far = exchange(part, ring, False)
    ur2 = reset_product(whole2, w2, width)
    prev2, dr2, dc2, high2, out, du_r2, part, sums2 = turn(
        1, cf2, ur2, x2, split, keep, order, back, vectors, far
    )
    far = exchange(part, ring, True)

    def scatter(term):
        return lax.psum_scatter(term, "ring", scatter_dimension=0, tiled=True)

    out = to_group(out.reshape(group, local, width))
    du_p2, forget2, stats = retreat(
        1, dc2, dr2, prev2, cf2, keep, vectors, far, rows, span, (), ur=ur2, mixed=mixed()
    )
    outputs = join(out).reshape(rows_dev, span, model)

    def slices(slots):
        return jnp.stack([me ^ k for k in slots]).astype(jnp.int32)

    terms = []

    def weigh(whole, du_p, du_r):
        def work(awaited):
            term = weight_term(whole, du_p, du_r, awaited)
            terms.append(scatter(term).reshape(group, shard, 3 * width))
            return term

        return work

    kept, core, pair, line, (stats,) = reduce_group(
        lambda slots, awaited: back_features(
            slices(slots), du_p2, du_r2, w2, (out, *awaited)
        ),
        group,
        (stats,),
        (),
        weigh(whole2, du_p2, du_r2),
    )
    (kept,) = after([kept], outputs)

    prev1, dr1, dc1, high1, du_r1, rows_r1, part, sums1 = middle_back(
        1, model, kept, core, pair, line, high2, x2, mean2, scale2, stats, cf1, ur1, split, keep,
        order, back, vectors, far1,
    )
    far = exchange(part, ring, True)
    high = to_group(high1.reshape(group, local, width))
    du_p1, rows_p1, forget1 = retreat(
        0, dc1, dr1, prev1, cf1, keep, vectors, far, rows, span, (), back=back
    )
    kept, core, pair, line, _ = reduce_group(
        lambda slots, awaited: back_tokens(
            slices(slots), rows_p1, rows_r1, pair_w1, reset_w1, (high, *awaited)
        ),
        group,
        (),
        terms[:1],
        weigh(whole1, du_p1, du_r1),
    )
    (both,) = after([jnp.concatenate([terms[1], terms[0]], axis=2)], pair, line)
    both = to_group(both)
    input_grad, gains1 = first_back(
        kept, core, pair, line, inputs.reshape(local, model), ln_gain, high
    )
    input_grad = input_grad.reshape(rows_dev, span, model)
    weight_grad = join_weights(both, layers)

    def total(value):
        return jnp.sum(value, axis=-2)

    sums1 = total(sums1)
    sums2 = total(sums2)
    narrow = jnp.stack(
        [
            sums1[2], total(forget1), sums1[3],
            sums1[0], sums1[1], sums2[0], total(forget2), sums2[1],
        ]
    )
    narrow = lax.dynamic_update_slice(jnp.zeros((8, model), F32), narrow, (0, me * width))
    small = jnp.concatenate([total(gains1), narrow])
    small = spread_small(small, ring, group, (both,)).reshape(2, 5, shard)
    return (outputs, input_grad, weight_grad) + tuple(small[:, i] for i in range(5))


def solution(mesh):
    ring = mesh.shape["tm"] // 2
    fine = Mesh(
        mesh.devices.reshape(ring, 2, mesh.shape["rows"]), ("ring", "pair", "rows")
    )
    tm = ("ring", "pair")
    everything = ("ring", "pair", "rows")
    return jax.shard_map(
        body,
        mesh=fine,
        in_specs=(
            P("rows", tm, None),
            P("rows", tm, None),
            P("rows", tm),
            P(None, everything, None),
            P(),
            P(),
            P(),
            P(),
            P(),
        ),
        out_specs=(
            P("rows", tm, None),
            P("rows", tm, None),
            P(None, everything, None),
            P(None, everything),
            P(None, everything),
            P(None, everything),
            P(None, everything),
            P(None, everything),
        ),
        check_vma=False,
    )
```

```python
import functools

import jax
import jax.numpy as jnp
import numpy as np
from jax import lax
from jax.experimental import pallas as pl
from jax.experimental.pallas import tpu as pltpu
from jax.sharding import Mesh
from jax.sharding import PartitionSpec as P

LANES = 128
SUBLANES = 8
STEPS = 64
SUB = 32
VMEM_BYTES = 58 * 1024 * 1024
GAIN, BIAS, PEEP, FORGET, RESET = range(5)
BF16 = jnp.bfloat16
F32 = jnp.float32
GROUP = ("pair", "rows")
CORE, LINE, PAIR = 1, 2, 4


def shape_of(dtype, *shape):
    return jax.ShapeDtypeStruct(shape, dtype)


def run(
    kernel, name, grid, ins, in_specs, outs, out_specs, scratch=(), place=None, cost=(0, 0), awaited=(),
    aliases=None,
):
    scalars = 0 if place is None else 1
    first = scalars + len(ins)
    last = first + len(awaited)

    def body(*refs):
        kernel(*refs[:first], *refs[last:])

    function = pl.pallas_call(
        body,
        out_shape=outs,
        grid_spec=pltpu.PrefetchScalarGridSpec(
            num_scalar_prefetch=scalars,
            grid=grid,
            in_specs=list(in_specs) + [pl.BlockSpec(memory_space=pl.ANY)] * len(awaited),
            out_specs=out_specs,
            scratch_shapes=list(scratch),
        ),
        compiler_params=pltpu.CompilerParams(vmem_limit_bytes=VMEM_BYTES),
        cost_estimate=pl.CostEstimate(flops=cost[0], bytes_accessed=cost[1], transcendentals=0),
        input_output_aliases=aliases or {},
        name=name,
    )
    return function(*(() if place is None else (place,)), *ins, *awaited)


def quarter(index, width):
    return pl.ds(pl.multiple_of(index * width, width), width)


def fixed_spec(*shape):
    return pl.BlockSpec(shape, lambda *_: (0,) * len(shape))


def block_spec(block, width):
    return pl.BlockSpec((block, width), lambda i, *_: (i, 0))


def turned_spec(block, width, count):
    return pl.BlockSpec((block, width), lambda i, *_: (count - 1 - i, 0))


def rows_spec(rows, width, per, place_of=lambda i: i):
    return pl.BlockSpec(
        (1, rows, STEPS, width), lambda i, *_: (place_of(i) // per, 0, place_of(i) % per, 0)
    )


def split_spec(half, rows_dev, width, per, which):
    return pl.BlockSpec(
        (1, half, 1, rows_dev, STEPS, width), lambda i, *_: (i // per, 0, which, 0, i % per, 0)
    )


def row_at(vec_ref, layer, which):
    row = layer * 5 + which
    return vec_ref[row : row + 1, :]


def chunks(total, size, body, unroll=1):
    def one(i, carry):
        body(pl.ds(pl.multiple_of(i * size, size), size))
        return carry

    lax.fori_loop(0, total // size, one, 0, unroll=unroll)


def over_time(body, state, backward=False):
    def one(i, state):
        t = STEPS - 1 - i if backward else i
        return body(pl.ds(pl.multiple_of(t * SUBLANES, SUBLANES), SUBLANES), state)

    return lax.fori_loop(0, STEPS, one, state, unroll=8)


def widen(keep, width):
    return jnp.concatenate([keep] * (width // LANES), axis=1)


def incoming(far):
    state = None
    for ref in reversed(far):
        state = ref[1] if state is None else ref[0] * state + ref[1]
    return state


def exact(order, value):
    return jnp.dot(order, value, preferred_element_type=F32)


def to_time(order_ref, rows, put):
    block = order_ref.shape[0]
    for i in range(STEPS // SUB):
        part = rows[:, i * SUB : (i + 1) * SUB, :].reshape(block, rows.shape[-1])
        put(slice(i * block, (i + 1) * block), exact(order_ref[...], part))


def to_rows(back_ref, value_ref, out_ref):
    block = back_ref.shape[0]
    for i in range(STEPS // SUB):
        part = exact(back_ref[...], value_ref[i * block : (i + 1) * block, :])
        at = slice(i * SUB, (i + 1) * SUB)
        part = part.astype(BF16)
        if len(out_ref.shape) == 4:
            out_ref[0, :, at, :] = part.reshape(out_ref.shape[1], SUB, out_ref.shape[3])
        else:
            _, half, _, rows_dev, _, width = out_ref.shape
            out_ref[0, :, 0, :, at, :] = part.reshape(half, rows_dev, SUB, width)


def forget_gate(cf_ref, here, vec_ref, layer):
    width = cf_ref.shape[1] // 2
    return jax.nn.sigmoid(cf_ref[here, width:] + row_at(vec_ref, layer, FORGET))


def fold(value):
    return jnp.sum(value.reshape(-1, SUBLANES, value.shape[-1]), axis=0)


def after(values, *awaited):
    count = len(values)

    def nothing(*refs):
        pass

    return pl.pallas_call(
        nothing,
        out_shape=[shape_of(v.dtype, *v.shape) for v in values],
        in_specs=[pl.BlockSpec(memory_space=pl.ANY)] * (count + len(awaited)),
        out_specs=[pl.BlockSpec(memory_space=pl.ANY)] * count,
        input_output_aliases={i: i for i in range(count)},
        name="after",
    )(*values, *awaited)


def columns_kernel(group, width, weights_ref, out_ref):
    for s in range(group):
        for third in range(3):
            start = third * group * width + s * width
            out_ref[s, :, third * width : (third + 1) * width] = weights_ref[
                0, :, start : start + width
            ]


def columns_of(weights, layer, group, width, awaited=()):
    _, shard, total = weights.shape
    return run(
        functools.partial(columns_kernel, group, width),
        "columns_of",
        (1,),
        [weights],
        [pl.BlockSpec((1, shard, total), lambda i, *_: (layer, 0, 0))],
        shape_of(BF16, group, shard, 3 * width),
        fixed_spec(group, shard, 3 * width),
        cost=(0, 4 * shard * total),
        awaited=awaited,
    )


def stack_columns_kernel(place, *refs):
    pieces, (pair_ref, reset_ref, flags_ref) = refs[:-3], refs[-3:]
    group = len(pieces)
    half = group // 2
    shard = pair_ref.shape[0] // group
    both = pair_ref.shape[1]
    for k in range(group):
        at = (place[1] ^ (k // half)) * half + (place[2] ^ (k % half))
        here = pl.ds(pl.multiple_of(at * shard, shard), shard)
        pair_ref[here, :] = pieces[k][:shard, :both]
        reset_ref[here, :] = pieces[k][:shard, both:]
        flags_ref[at] = pieces[k][shard:, :LANES]


def stack_columns(place, pieces, shard, awaited):
    group = len(pieces)
    rows, total = pieces[0].shape
    outs = [
        (group * shard, total // 3 * 2),
        (group * shard, total // 3),
        (group, rows - shard, LANES),
    ]
    return run(
        stack_columns_kernel,
        "stack_columns",
        (1,),
        pieces,
        [fixed_spec(rows, total)] * group,
        [shape_of(BF16, *out) for out in outs],
        [fixed_spec(*out) for out in outs],
        (),
        place,
        (0, 4 * group * shard * total),
        awaited,
    )


def send_columns_kernel(group, width, place, weights_ref, flags_ref, *outs):
    half = group // 2
    shard = weights_ref.shape[1]
    below = flags_ref[...].astype(F32)
    fill = jnp.zeros((outs[0].shape[0] - shard - below.shape[0], below.shape[1]), F32)
    below = jnp.concatenate([below, fill]).astype(BF16)
    for k in range(group):
        at = (place[1] ^ (k // half)) * half + (place[2] ^ (k % half))
        for third in range(3):
            start = pl.multiple_of(third * group * width + at * width, width)
            outs[k][:shard, third * width : (third + 1) * width] = weights_ref[
                0, :, pl.ds(start, width)
            ]
        outs[k][shard:, :] = jnp.zeros_like(outs[k][shard:, :])
        outs[k][shard:, : flags_ref.shape[1]] = below


def send_columns(place, weights, layer, group, width, flags):
    _, shard, total = weights.shape
    rows = shard + 2 * SUBLANES
    return run(
        functools.partial(send_columns_kernel, group, width),
        "send_columns",
        (1,),
        [weights, flags],
        [pl.BlockSpec((1, shard, total), lambda i, *_: (layer, 0, 0)), fixed_spec(*flags.shape)],
        [shape_of(BF16, rows, 3 * width)] * group,
        [fixed_spec(rows, 3 * width)] * group,
        (),
        place,
        (0, 4 * shard * total),
    )


def first_norm_kernel(group, x_ref, grad_ref, gain_ref, bias_ref, *refs):
    split_ref = refs[-1]
    rows, span, model = x_ref.shape
    width = model // group
    for i in range(rows):

        def part(here):
            wide = x_ref[i, here, :].astype(F32)
            centered = wide - jnp.mean(wide, axis=-1, keepdims=True)
            scale = lax.rsqrt(jnp.mean(centered * centered, axis=-1, keepdims=True) + 1e-05)
            refs[i][here, :] = (
                centered * scale * gain_ref[0:1, :] + bias_ref[0:1, :]
            ).astype(BF16)

        chunks(span, 16, part)
        for s in range(group):
            columns = slice(s * width, (s + 1) * width)
            split_ref[s, 0, i] = x_ref[i, :, columns]
            split_ref[s, 1, i] = grad_ref[i, :, columns]


def first_norm(x, grad, gain, bias, group, awaited):
    rows, span, model = x.shape
    split = (group, 2, rows, span, model // group)
    return run(
        functools.partial(first_norm_kernel, group),
        "first_norm",
        (1,),
        [x, grad, gain, bias],
        [fixed_spec(*a.shape) for a in (x, grad, gain, bias)],
        [shape_of(BF16, span, model)] * rows + [shape_of(BF16, *split)],
        [fixed_spec(span, model)] * rows + [fixed_spec(*split)],
        cost=(20 * rows * span * model, 8 * rows * span * model),
        awaited=awaited,
    )


def project_kernel(layer, gather, slots, place, *refs):
    pieces = refs[:slots]
    w_ref, order_ref, keep_ref, vec_ref = refs[slots : slots + 4]
    cf_ref, whole_ref, tot_ref, held, forget_s = refs[slots + 4 :]
    width = cf_ref.shape[1] // 2
    step = pl.program_id(0)
    gather(place, step, pieces, order_ref, held, whole_ref)
    cf_ref[...] = jnp.dot(whole_ref[...], w_ref[...], preferred_element_type=F32)

    def gates(here):
        forget_s[here, :] = forget_gate(cf_ref, here, vec_ref, layer)

    chunks(cf_ref.shape[0], 64, gates)

    @pl.when(step == 0)
    def _():
        tot_ref[0] = jnp.ones_like(tot_ref[0])
        tot_ref[1] = jnp.zeros_like(tot_ref[1])

    def one(at, state):
        forget = forget_s[at, :]
        decay = forget * widen(keep_ref[at, :], width)
        return state[0] * decay, state[1] * decay + (1.0 - forget) * cf_ref[at, :width]

    product, state = over_time(one, (tot_ref[0], tot_ref[1]))
    tot_ref[0] = product
    tot_ref[1] = state


def gather_rows(per, group, place, step, pieces, order_ref, held, whole_ref):
    half = group // 2
    other = (step // per) ^ place[1]
    for side in range(2):

        @pl.when(other == side)
        def _():
            for k in range(half):
                for i in range(2):
                    held[place[2] ^ k, i] = pieces[2 * (side * half + k) + i][...]

    def put(here, value):
        whole_ref[here, :] = value.astype(BF16)

    to_time(order_ref, held[...].reshape(-1, STEPS, whole_ref.shape[1]), put)


def gather_features(per, group, place, step, pieces, order_ref, held, whole_ref):
    half = group // 2
    width = whole_ref.shape[1] // group
    for side in range(2):

        @pl.when(step // per == side)
        def _():
            for k in range(group):
                at = (place[1] ^ (k // half)) * half + (place[2] ^ (k % half))
                whole_ref[:, quarter(at, width)] = pieces[2 * k + side][...]


def project(place, layer, pieces, matrix, order, keep, vectors, rows, by_rows):
    model = matrix.shape[0]
    width = vectors.shape[1]
    both = 2 * width
    tokens = keep.shape[0]
    block = rows * STEPS
    count = tokens // block
    per = count // 2
    group = model // width
    half = group // 2
    specs = []
    for k in range(group):
        for side in range(2):
            if by_rows:

                def index(i, place, needed=k // half):
                    mine = ((i // per) ^ place[1]) == needed
                    return (jnp.where(mine, i % per, 0), 0)

                specs.append(pl.BlockSpec((STEPS, model), index))
            elif side == 0:
                specs.append(
                    pl.BlockSpec((block, width), lambda i, place: (jnp.minimum(i, per - 1), 0))
                )
            else:
                specs.append(
                    pl.BlockSpec((block, width), lambda i, place: (jnp.maximum(i - per, 0), 0))
                )
    gather = functools.partial(gather_rows if by_rows else gather_features, per, group)
    held = pltpu.VMEM((half, 2, STEPS, model) if by_rows else (2 * SUBLANES, LANES), BF16)
    return run(
        functools.partial(project_kernel, layer, gather, len(pieces)),
        "project",
        (count,),
        [*pieces, matrix, order, keep, vectors],
        specs
        + [
            fixed_spec(model, both),
            fixed_spec(*order.shape),
            block_spec(block, LANES),
            fixed_spec(*vectors.shape),
        ],
        [
            shape_of(F32, tokens, both),
            shape_of(BF16, tokens, model),
            shape_of(F32, 2, rows, width),
        ],
        [block_spec(block, both), block_spec(block, model), fixed_spec(2, rows, width)],
        [held, pltpu.VMEM((block, width), F32)],
        place,
        (2 * tokens * model * both, 4 * tokens * model + 4 * tokens * both + 2 * model * both),
    )


def reset_kernel(x_ref, w_ref, out_ref):
    out_ref[...] = jnp.dot(x_ref[...], w_ref[...], preferred_element_type=F32)


def reset_product(whole, matrix, width):
    tokens, model = whole.shape
    last = matrix.shape[1] // width - 1
    block = tokens // 4
    return run(
        reset_kernel,
        "reset_product",
        (4,),
        [whole, matrix],
        [block_spec(block, model), pl.BlockSpec((model, width), lambda *_: (0, last))],
        shape_of(F32, tokens, width),
        block_spec(block, width),
        cost=(2 * tokens * model * width, 2 * tokens * model + 4 * tokens * width),
    )


def carry_forward(layer, cf_ref, keep_ref, vec_ref, far, carry_s, forget_s, prev_ref, state_s):
    width = prev_ref.shape[1]

    def gates(here):
        forget_s[here, :] = forget_gate(cf_ref, here, vec_ref, layer)

    chunks(forget_s.shape[0], 64, gates)

    @pl.when(pl.program_id(0) == 0)
    def _():
        first = incoming(far)
        carry_s[...] = jnp.zeros_like(carry_s) if first is None else first

    def one(at, state):
        forget = forget_s[at, :]
        prev = widen(keep_ref[at, :], width) * state
        new = forget * prev + (1.0 - forget) * cf_ref[at, :width]
        prev_ref[at, :] = prev
        state_s[at, :] = new
        return new

    carry_s[...] = over_time(one, carry_s[...])


def reset_gate(layer, ur_ref, prev_ref, here, vec_ref):
    return jax.nn.sigmoid(
        ur_ref[here, :]
        + row_at(vec_ref, layer, PEEP) * prev_ref[here, :]
        + row_at(vec_ref, layer, RESET)
    )


def advance_kernel(layer, cf_ref, ur_ref, x_ref, keep_ref, order_ref, vec_ref, *refs):
    xn_ref, stat_ref, carry_s, forget_s, prev_s, state_s, x_s = refs[-7:]
    far = refs[:-7]
    block, width = xn_ref.shape

    def put(here, value):
        x_s[here, :] = value

    to_time(order_ref, x_ref[...].reshape(-1, STEPS, width), put)
    carry_forward(layer, cf_ref, keep_ref, vec_ref, far, carry_s, forget_s, prev_s, state_s)

    def finish(here):
        gate = reset_gate(layer, ur_ref, prev_s, here, vec_ref)
        xn = gate * state_s[here, :] + (1.0 - gate) * x_s[here, :]
        xn_ref[here, :] = xn
        mean = jnp.mean(xn, axis=-1, keepdims=True)
        off = xn - mean
        spread = sum(off[:, j : j + LANES] * off[:, j : j + LANES] for j in range(0, width, LANES))
        x_s[here, :LANES] = jnp.broadcast_to(mean, (here.size, LANES))
        state_s[here, :LANES] = spread

    chunks(block, 64, finish)
    for b in range(block // LANES):
        here = slice(b * LANES, (b + 1) * LANES)
        row = pl.ds(pl.program_id(0) * (block // LANES) + b, 1)
        stat_ref[0, row, :] = x_s[here, :LANES].T[0:1, :]
        stat_ref[1, row, :] = jnp.sum(state_s[here, :LANES].T, axis=0, keepdims=True)


def advance(layer, cf, ur, x, keep, order, vectors, far):
    tokens, width = ur.shape
    _, half, _, rows_dev, span, _ = x.shape
    rows = half * rows_dev
    block = rows * STEPS
    part = block_spec(block, width)
    return run(
        functools.partial(advance_kernel, layer),
        "advance",
        (tokens // block,),
        [cf, ur, x, keep, order, vectors, *far],
        [
            block_spec(block, 2 * width),
            part,
            split_spec(half, rows_dev, width, span // STEPS, 0),
            block_spec(block, LANES),
            fixed_spec(*order.shape),
            fixed_spec(*vectors.shape),
        ]
        + [fixed_spec(2, rows, width)] * len(far),
        [shape_of(F32, tokens, width), shape_of(F32, 2, tokens // LANES, LANES)],
        [part, fixed_spec(2, tokens // LANES, LANES)],
        [pltpu.VMEM((rows, width), F32)] + [pltpu.VMEM((block, width), F32)] * 4,
        None,
        (60 * tokens * width, 22 * tokens * width),
    )


def middle_norm_kernel(layer, model, xn_ref, stat_ref, vec_ref, a_ref, b_ref, mean_ref, scale_ref):
    group = stat_ref.shape[0]
    block, width = xn_ref.shape
    for b in range(block // LANES):
        row = pl.ds(pl.program_id(0) * (block // LANES) + b, 1)
        here = slice(b * LANES, (b + 1) * LANES)
        means = [stat_ref[s, 0, row, :] for s in range(group)]
        mean = sum(means) / group
        square = sum(stat_ref[s, 1, row, :] for s in range(group))
        between = sum((part - mean) * (part - mean) for part in means)
        scale = lax.rsqrt((square + between * width) / model + 1e-05)
        mean_ref[here, :] = jnp.broadcast_to(mean, (LANES, LANES)).T
        scale_ref[here, :] = jnp.broadcast_to(scale, (LANES, LANES)).T

    per = pl.num_programs(0) // 2
    for side, normed_ref in enumerate((a_ref, b_ref)):

        @pl.when(pl.program_id(0) // per == side)
        def _():
            def part(here):
                normed_ref[here, :] = (
                    (xn_ref[here, :] - widen(mean_ref[here, :], width))
                    * widen(scale_ref[here, :], width)
                    * row_at(vec_ref, layer, GAIN)
                    + row_at(vec_ref, layer, BIAS)
                ).astype(BF16)

            chunks(block, 64, part)


def middle_norm(layer, model, xn, stats, vectors, rows):
    tokens, width = xn.shape
    block = rows * STEPS
    per = tokens // block // 2
    return run(
        functools.partial(middle_norm_kernel, layer, model),
        "middle_norm",
        (tokens // block,),
        [xn, stats, vectors],
        [block_spec(block, width), fixed_spec(*stats.shape), fixed_spec(*vectors.shape)],
        [shape_of(BF16, tokens // 2, width)] * 2 + [shape_of(F32, tokens, LANES)] * 2,
        [
            pl.BlockSpec((block, width), lambda i, *_: (jnp.minimum(i, per - 1), 0)),
            pl.BlockSpec((block, width), lambda i, *_: (jnp.maximum(i - per, 0), 0)),
        ]
        + [block_spec(block, LANES)] * 2,
        cost=(10 * tokens * width, 8 * tokens * width),
    )


def add_total(decay_s, drive_s, tot_ref):
    @pl.when(pl.program_id(0) == 0)
    def _():
        tot_ref[0] = jnp.ones_like(tot_ref[0])
        tot_ref[1] = jnp.zeros_like(tot_ref[1])

    def one(at, state):
        return state[0] * decay_s[at, :], state[1] + state[0] * drive_s[at, :]

    product, total = over_time(one, (tot_ref[0], tot_ref[1]))
    tot_ref[0] = product
    tot_ref[1] = total


def turn_kernel(layer, cf_ref, ur_ref, x_ref, dh_ref, keep_ref, order_ref, back_ref, vec_ref, *refs):
    prev_ref, dr_ref, dc_ref, high_ref, out_ref, du_ref, tot_ref, small_ref = refs[-14:-6]
    carry_s, forget_s, state_s, dh_s, drive_s, out_s = refs[-6:]
    far = refs[:-14]
    block, width = prev_ref.shape

    def put(here, value):
        dh_s[here, :] = value

    to_time(order_ref, dh_ref[...].reshape(-1, STEPS, width), put)
    carry_forward(layer, cf_ref, keep_ref, vec_ref, far, carry_s, forget_s, prev_ref, state_s)

    @pl.when(pl.program_id(0) == 0)
    def _():
        small_ref[...] = jnp.zeros_like(small_ref)

    def finish(here):
        state = state_s[here, :]
        x = x_ref[here, :]
        dh = dh_s[here, :]
        prev = prev_ref[here, :]
        gate = reset_gate(layer, ur_ref, prev_ref, here, vec_ref)
        out_s[here, :] = (gate * state + (1.0 - gate) * x).astype(BF16)
        dr = dh * (state - x) * gate * (1.0 - gate)
        dc = dh * gate
        dr_ref[here, :] = dr
        dc_ref[here, :] = dc
        du_ref[here, :] = dr.astype(BF16)
        high_ref[here, :] = dh - dc
        keep = widen(keep_ref[here, :], width)
        decay = keep * forget_s[here, :]
        state_s[here, :] = decay
        drive_s[here, :] = keep * row_at(vec_ref, layer, PEEP) * dr + decay * dc
        small_ref[0] += fold(dr * prev)
        small_ref[1] += fold(dr)

    chunks(block, 32, finish)
    to_rows(back_ref, out_s, out_ref)
    add_total(state_s, drive_s, tot_ref)


def turn(layer, cf, ur, x, dh, keep, order, back, vectors, far):
    tokens, width = ur.shape
    _, half, _, rows_dev, span, _ = dh.shape
    rows = half * rows_dev
    block = rows * STEPS
    part = block_spec(block, width)
    by_rows = split_spec(half, rows_dev, width, span // STEPS, 0)
    return run(
        functools.partial(turn_kernel, layer),
        "turn",
        (tokens // block,),
        [cf, ur, x, dh, keep, order, back, vectors, *far],
        [
            block_spec(block, 2 * width),
            part,
            part,
            split_spec(half, rows_dev, width, span // STEPS, 1),
            block_spec(block, LANES),
            fixed_spec(*order.shape),
            fixed_spec(*back.shape),
            fixed_spec(*vectors.shape),
        ]
        + [fixed_spec(2, rows, width)] * len(far),
        [shape_of(F32, tokens, width)] * 4
        + [
            shape_of(BF16, *dh.shape),
            shape_of(BF16, tokens, width),
            shape_of(F32, 2, rows, width),
            shape_of(F32, 2, SUBLANES, width),
        ],
        [part] * 4
        + [by_rows, part, fixed_spec(2, rows, width), fixed_spec(2, SUBLANES, width)],
        [pltpu.VMEM((rows, width), F32)]
        + [pltpu.VMEM((block, width), F32)] * 4
        + [pltpu.VMEM((block, width), BF16)],
        None,
        (80 * tokens * width, 36 * tokens * width),
    )


def retreat_kernel(layer, sums, dc_ref, dr_ref, prev_ref, cf_ref, keep_ref, vec_ref, *refs):
    if sums:
        ur_ref, mixed_ref = refs[:2]
        du_ref, small_ref, stat_ref, carry_s, forget_s, total_s, sum_s, cross_s = refs[-8:]
        far = refs[2:-8]
    else:
        back_ref = refs[0]
        du_ref, rows_ref, small_ref, carry_s, forget_s, total_s = refs[-6:]
        far = refs[1:-6]
    block, width = prev_ref.shape
    peep = row_at(vec_ref, layer, PEEP)

    @pl.when(pl.program_id(0) == 0)
    def _():
        first = incoming(far)
        carry_s[...] = jnp.zeros_like(carry_s) if first is None else first
        small_ref[...] = jnp.zeros_like(small_ref)

    def gates(here):
        forget_s[here, :] = forget_gate(cf_ref, here, vec_ref, layer)

    chunks(block, 64, gates)

    def one(at, state):
        total = dc_ref[at, :] + state
        total_s[at, :] = total
        return widen(keep_ref[at, :], width) * (peep * dr_ref[at, :] + forget_s[at, :] * total)

    carry_s[...] = over_time(one, carry_s[...], True)

    def halves(value):
        return sum(value[:, j : j + LANES] for j in range(0, width, LANES))

    def finish(here):
        forget = forget_s[here, :]
        slow = total_s[here, :] * (1.0 - forget)
        d_forget = slow * forget * (prev_ref[here, :] - cf_ref[here, :width])
        d_cand = slow.astype(BF16)
        d_gate = d_forget.astype(BF16)
        du_ref[here, :width] = d_cand
        du_ref[here, width:] = d_gate
        small_ref[...] += fold(d_forget)
        if sums:
            parts = [d_cand, d_gate, dr_ref[here, :].astype(BF16)]
            inputs = [cf_ref[here, :width], cf_ref[here, width:], ur_ref[here, :]]
            plain = cross = 0.0
            for third in range(3):
                at = slice(third * width, (third + 1) * width)
                du = parts[third].astype(F32)
                plain = plain + du * mixed_ref[0:1, at]
                cross = cross + du * (inputs[third] - mixed_ref[1:2, at])
            sum_s[here, :] = halves(plain)
            cross_s[here, :] = halves(cross)

    chunks(block, 32, finish)
    if sums:
        base = (pl.num_programs(0) - 1 - pl.program_id(0)) * (block // LANES)
        for b in range(block // LANES):
            here = slice(b * LANES, (b + 1) * LANES)
            stat_ref[0, pl.ds(base + b, 1), :] = jnp.sum(sum_s[here, :].T, axis=0, keepdims=True)
            stat_ref[1, pl.ds(base + b, 1), :] = jnp.sum(cross_s[here, :].T, axis=0, keepdims=True)
    else:
        to_rows(back_ref, du_ref, rows_ref)


def retreat(layer, dc, dr, prev, cf, keep, vectors, far, rows, span, awaited, back=None, ur=None, mixed=None):
    tokens, width = dc.shape
    block = rows * STEPS
    count = tokens // block
    sums = back is None
    part = turned_spec(block, width, count)
    both = turned_spec(block, 2 * width, count)
    rows_out = rows_spec(rows, 2 * width, span // STEPS, lambda i: count - 1 - i)
    outs = [shape_of(BF16, tokens, 2 * width)]
    specs = [both]
    scratch = [pltpu.VMEM((rows, width), F32)] + [pltpu.VMEM((block, width), F32)] * 2
    if sums:
        more, more_specs = [ur, mixed], [part, fixed_spec(*mixed.shape)]
        outs += [shape_of(F32, SUBLANES, width), shape_of(F32, 2, tokens // LANES, LANES)]
        specs += [fixed_spec(SUBLANES, width), fixed_spec(2, tokens // LANES, LANES)]
        scratch += [pltpu.VMEM((block, LANES), F32)] * 2
    else:
        more, more_specs = [back], [fixed_spec(*back.shape)]
        outs += [shape_of(BF16, 2, rows, span, 2 * width), shape_of(F32, SUBLANES, width)]
        specs += [rows_out, fixed_spec(SUBLANES, width)]
    return run(
        functools.partial(retreat_kernel, layer, sums),
        "retreat",
        (count,),
        [dc, dr, prev, cf, keep, vectors, *more, *far],
        [part] * 3
        + [both, turned_spec(block, LANES, count), fixed_spec(*vectors.shape)]
        + more_specs
        + [fixed_spec(2, rows, width)] * len(far),
        outs,
        specs,
        scratch,
        None,
        (60 * tokens * width, 30 * tokens * width),
        awaited,
    )


def back_product(pair, reset, w_pair, w_reset):
    contract = (((1,), (1,)), ((), ()))
    return lax.dot_general(pair, w_pair, contract, preferred_element_type=F32) + lax.dot_general(
        reset, w_reset, contract, preferred_element_type=F32
    )


def put_shares(share_of, outs):
    odd, even = outs
    for k in range(odd.shape[0]):
        odd[k] = share_of(k).astype(BF16)
        even[k] = share_of(odd.shape[0] + k)


def share_outs(count, rows, columns):
    return [shape_of(dtype, count // 2, rows, columns) for dtype in (BF16, F32)]


def back_features_kernel(count, order, pair_ref, reset_ref, *refs):
    def share_of(k):
        return back_product(
            pair_ref[...], reset_ref[...], refs[2 * k][...], refs[2 * k + 1][...]
        )

    put_shares(share_of, refs[-2:])


def back_features(order, pair, reset, matrix, awaited):
    tokens, width = reset.shape
    count = order.shape[0]
    block = tokens // 4
    specs = []
    for k in range(count):
        specs.append(pl.BlockSpec((width, 2 * width), lambda i, order, k=k: (order[k], 0)))
        specs.append(pl.BlockSpec((width, width), lambda i, order, k=k: (order[k], 2)))
    outs = share_outs(count, tokens, width)
    return run(
        functools.partial(back_features_kernel, count),
        "back_features",
        (4,),
        [pair, reset] + [matrix, matrix] * count,
        [block_spec(block, 2 * width), block_spec(block, width)] + specs,
        outs,
        [pl.BlockSpec((out.shape[0], block, width), lambda i, order: (0, i, 0)) for out in outs],
        (),
        order,
        (6 * count * tokens * width * width, 8 * count * tokens * width),
        awaited,
    )


def back_tokens_kernel(count, order, wp_ref, wr_ref, *refs):
    local = refs[-1].shape[1]

    def share_of(k):
        pair, reset = refs[2 * k : 2 * k + 2]
        return back_product(
            pair[0].reshape(local, pair.shape[-1]),
            reset[0].reshape(local, reset.shape[-1]),
            wp_ref[...],
            wr_ref[...],
        )

    put_shares(share_of, refs[-2:])


def back_tokens(order, pair, reset, w_pair, w_reset, awaited):
    two, rows, span, width = reset.shape
    model = w_pair.shape[0]
    count = order.shape[0]
    half = model // width // 2
    rows_dev = rows // half
    local = rows_dev * span
    block = model // 4
    specs = []
    for k in range(count):
        by_order = lambda i, order, k=k: (order[k] // half, order[k] % half, 0, 0)
        for columns in (2 * width, width):
            specs.append(pl.BlockSpec((1, rows_dev, span, columns), by_order))
    outs = share_outs(count, local, model)
    return run(
        functools.partial(back_tokens_kernel, count),
        "back_tokens",
        (4,),
        [w_pair, w_reset] + [pair, reset] * count,
        [block_spec(block, 2 * width), block_spec(block, width)] + specs,
        outs,
        [pl.BlockSpec((out.shape[0], local, block), lambda i, order: (0, 0, i)) for out in outs],
        (),
        order,
        (6 * count * local * model * width, 8 * count * local * model),
        awaited,
    )


def middle_back_kernel(layer, model, *refs):
    (
        kept_ref, core_ref, pair_ref, line_ref, high_ref, x_ref, mean_ref, scale_ref, stat_ref,
        cf_ref, ur_ref, below_x_ref, keep_ref, order_ref, back_ref, vec_ref, _,
    ) = refs[:17]
    (
        prev_ref, dr_ref, dc_ref, below_ref, du_ref, rows_ref, tot_ref, small_ref,
        carry_s, forget_s, state_s, drive_s, x_s, plain_s, cross_s, below_s,
    ) = refs[-16:]
    far = refs[17:-16]
    block, width = prev_ref.shape
    below = layer - 1

    def put(here, value):
        x_s[here, :] = value

    to_time(order_ref, below_x_ref[...].reshape(-1, STEPS, width), put)
    carry_forward(below, cf_ref, keep_ref, vec_ref, far, carry_s, forget_s, prev_ref, state_s)
    for b in range(block // LANES):
        row = pl.ds(pl.program_id(0) * (block // LANES) + b, 1)
        here = slice(b * LANES, (b + 1) * LANES)
        for s, out in enumerate((plain_s, cross_s)):
            out[here, :] = jnp.broadcast_to(stat_ref[s, row, :] / model, (LANES, LANES)).T

    @pl.when(pl.program_id(0) == 0)
    def _():
        small_ref[...] = jnp.zeros_like(small_ref)

    def finish(here):
        back = (
            kept_ref[0, here, :]
            + core_ref[0, here, :].astype(F32)
            + pair_ref[here, :].astype(F32)
            + line_ref[here, :].astype(F32)
        )
        scale = widen(scale_ref[here, :], width)
        xhat = (x_ref[here, :] - widen(mean_ref[here, :], width)) * scale
        dh = high_ref[here, :] + scale * (
            back * row_at(vec_ref, layer, GAIN)
            - widen(plain_s[here, :], width)
            - xhat * widen(cross_s[here, :], width)
        )
        small_ref[0] += fold(back * xhat)
        small_ref[1] += fold(back)
        gate = reset_gate(below, ur_ref, prev_ref, here, vec_ref)
        dr = dh * (state_s[here, :] - x_s[here, :]) * gate * (1.0 - gate)
        dc = dh * gate
        dr_ref[here, :] = dr
        dc_ref[here, :] = dc
        du_ref[here, :] = dr.astype(BF16)
        below_s[here, :] = (dh - dc).astype(BF16)
        keep = widen(keep_ref[here, :], width)
        decay = keep * forget_s[here, :]
        state_s[here, :] = decay
        drive_s[here, :] = keep * row_at(vec_ref, below, PEEP) * dr + decay * dc
        small_ref[2] += fold(dr * prev_ref[here, :])
        small_ref[3] += fold(dr)

    chunks(block, 32, finish)
    to_rows(back_ref, below_s, below_ref)
    to_rows(back_ref, du_ref, rows_ref)
    add_total(state_s, drive_s, tot_ref)


def middle_back(
    layer, model, kept, core, pair, line, high, x, mean, scale, stats, cf, ur, below_x, keep, order,
    back, vectors, out, far,
):
    tokens, width = ur.shape
    _, half, _, rows_dev, span, _ = below_x.shape
    rows = half * rows_dev
    block = rows * STEPS
    part = block_spec(block, width)
    last = kept.shape[0] - 1
    top = pl.BlockSpec((1, block, width), lambda i, *_: (last, i, 0))
    thin = block_spec(block, LANES)
    by_rows = rows_spec(rows, width, span // STEPS)
    held = pltpu.VMEM((block, width), F32)
    return run(
        functools.partial(middle_back_kernel, layer, model),
        "middle_back",
        (tokens // block,),
        [
            kept, core, pair, line, high, x, mean, scale, stats, cf, ur, below_x, keep, order, back,
            vectors, out, *far,
        ],
        [top, top, part, part, part, part, thin, thin, fixed_spec(*stats.shape)]
        + [
            block_spec(block, 2 * width),
            part,
            split_spec(half, rows_dev, width, span // STEPS, 0),
            thin,
            fixed_spec(*order.shape),
            fixed_spec(*back.shape),
            fixed_spec(*vectors.shape),
            pl.BlockSpec(memory_space=pl.ANY),
        ]
        + [fixed_spec(2, rows, width)] * len(far),
        [shape_of(F32, tokens, width)] * 3
        + [
            shape_of(BF16, *out.shape),
            shape_of(BF16, tokens, width),
            shape_of(BF16, 2, rows, span, width),
            shape_of(F32, 2, rows, width),
            shape_of(F32, 4, SUBLANES, width),
        ],
        [part, part, part, split_spec(half, rows_dev, width, span // STEPS, 1), part, by_rows]
        + [fixed_spec(2, rows, width), fixed_spec(4, SUBLANES, width)],
        [pltpu.VMEM((rows, width), F32)]
        + [held] * 4
        + [pltpu.VMEM((block, LANES), F32)] * 2
        + [pltpu.VMEM((block, width), BF16)],
        None,
        (80 * tokens * width, 44 * tokens * width),
        (),
        {16: 3},
    )


def first_back_kernel(kept_ref, core_ref, pair_ref, line_ref, x_ref, gain_ref, high_ref, out_ref, small_ref):
    local, model = x_ref.shape
    group, _, _, width = high_ref.shape

    @pl.when(pl.program_id(0) == 0)
    def _():
        small_ref[...] = jnp.zeros_like(small_ref)

    def part(here):
        wide = x_ref[here, :].astype(F32)
        centered = wide - jnp.mean(wide, axis=-1, keepdims=True)
        scale = lax.rsqrt(jnp.mean(centered * centered, axis=-1, keepdims=True) + 1e-05)
        xhat = centered * scale
        back = (
            kept_ref[0, here, :]
            + core_ref[0, here, :].astype(F32)
            + pair_ref[here, :].astype(F32)
            + line_ref[here, :].astype(F32)
        )
        scaled = back * gain_ref[0:1, :]
        small_ref[0] += fold(back * xhat)
        small_ref[1] += fold(back)
        total = scale * (
            scaled
            - jnp.mean(scaled, axis=-1, keepdims=True)
            - xhat * jnp.mean(scaled * xhat, axis=-1, keepdims=True)
        )
        for s in range(group):
            columns = slice(s * width, (s + 1) * width)
            out_ref[here, columns] = (
                total[:, columns] + high_ref[s, 0, here, :].astype(F32)
            ).astype(BF16)

    chunks(local, 16, part)


def first_back(kept, core, pair, line, x, gain, high):
    local, model = x.shape
    group, _, _, width = high.shape
    last = kept.shape[0] - 1
    block = local // 4
    top = pl.BlockSpec((1, block, model), lambda i, *_: (last, i, 0))
    flat = block_spec(block, model)
    return run(
        first_back_kernel,
        "first_back",
        (4,),
        [kept, core, pair, line, x, gain, high],
        [top, top, flat, flat, flat, fixed_spec(*gain.shape)]
        + [pl.BlockSpec((group, 1, block, width), lambda i, *_: (0, 1, i, 0))],
        [shape_of(BF16, local, model), shape_of(F32, 2, SUBLANES, model)],
        [flat, fixed_spec(2, SUBLANES, model)],
        cost=(30 * local * model, 16 * local * model),
    )


def weight_kernel(whole_ref, pair_ref, reset_ref, out_ref):
    both = pair_ref.shape[1]
    contract = (((0,), (0,)), ((), ()))
    for du_ref, at in ((pair_ref, slice(0, both)), (reset_ref, slice(both, out_ref.shape[1]))):
        out_ref[:, at] = lax.dot_general(
            whole_ref[...], du_ref[...], contract, preferred_element_type=F32
        ).astype(BF16)


def weight_term(whole, pair, reset, awaited=()):
    tokens, model = whole.shape
    width = reset.shape[1]
    block = model // 4
    return run(
        weight_kernel,
        "weight_term",
        (4,),
        [whole, pair, reset],
        [
            pl.BlockSpec((tokens, block), lambda k, *_: (0, k)),
            fixed_spec(*pair.shape),
            fixed_spec(*reset.shape),
        ],
        shape_of(BF16, model, 3 * width),
        block_spec(block, 3 * width),
        cost=(6 * tokens * model * width, 2 * tokens * model + 6 * model * width),
        awaited=awaited,
    )


def join_kernel(x_ref, out_ref):
    group, _, rows, width = x_ref.shape
    for s in range(group):
        out_ref[:, s * width : (s + 1) * width] = x_ref[s, 0]


def join(value):
    group, _, rows, width = value.shape
    return run(
        join_kernel,
        "join",
        (1,),
        [value],
        [fixed_spec(group, 1, rows, width)],
        shape_of(value.dtype, rows, group * width),
        fixed_spec(rows, group * width),
        cost=(0, 4 * rows * group * width),
    )


def join_weights_kernel(part_ref, out_ref):
    layers, _, total = out_ref.shape
    group = part_ref.shape[0]
    width = total // group // 3
    for layer in range(layers):
        for s in range(group):
            for third in range(3):
                start = third * group * width + s * width
                at = (3 * layer + third) * width
                out_ref[layer, :, start : start + width] = part_ref[s, :, at : at + width].astype(
                    F32
                )


def join_weights(part, layers):
    group, shard, total = part.shape
    shape = (layers, shard, group * total // layers)
    return run(
        join_weights_kernel,
        "join_weights",
        (1,),
        [part],
        [fixed_spec(*part.shape)],
        shape_of(F32, *shape),
        fixed_spec(*shape),
        cost=(0, 12 * group * shard * total),
    )


def swap(value, bits, size):
    return lax.ppermute(value, GROUP, [(i, i ^ bits) for i in range(size)])


def gather_group(a, b, size, awaited=()):
    pair_a = swap(a, PAIR, size)
    line_b = swap(b, LINE, size)
    a, b = after([a, b], pair_a, line_b, *awaited)
    pair_b = swap(b, PAIR, size)
    line_a = swap(a, LINE, size)
    far_a = swap(pair_a, LINE, size)
    far_b = swap(line_b, PAIR, size)
    halves = [a, b, line_a, line_b, pair_a, pair_b, far_a, far_b]
    cores = [swap(half, CORE, size) for half in halves]
    return [
        half
        for k in range(0, 8, 2)
        for half in (halves[k], halves[k + 1], cores[k], cores[k + 1])
    ]


def reduce_group(shares, size, stats, soon, filler):
    far_odd, far_even = shares((7, 6), ())
    far_core = swap(far_odd, CORE, size)
    filled = filler((far_odd,))
    far = (far_even[0] + far_core[0].astype(F32)).astype(BF16)
    half = far.shape[0] // 2
    far_a, far_b = after([far[:half], far[half:]], filled)
    by_pair = swap(far_a, PAIR, size)
    by_line = swap(far_b, LINE, size)
    odd, even = shares((5, 3, 1, 4, 2, 0), (far_a, far_b, *soon))
    core = swap(odd, CORE, size)
    stats = [part + swap(part, CORE, size) for part in stats]
    zeros = jnp.zeros_like(by_pair)
    by_line = jnp.concatenate([zeros, by_line]).astype(F32)
    by_pair = jnp.concatenate([by_pair, zeros]).astype(F32)
    pair = (even[0] + core[0].astype(F32) + by_line).astype(BF16)
    line = (even[1] + core[1].astype(F32) + by_pair).astype(BF16)
    if stats:
        stats = after(stats, pair, line)
        stats = [
            part + sum(swap(part, bits, size) for bits in (LINE, PAIR, LINE | PAIR))
            for part in stats
        ]
    return even, core, swap(pair, PAIR, size), swap(line, LINE, size), stats


def exchange(part, size, reverse):
    far = []
    for hop in reversed(range(1, size)):
        pairs = [(i, i + hop) for i in range(size - hop)]
        if reverse:
            pairs = [(b, a) for a, b in pairs]
        far.append(lax.ppermute(part, "ring", pairs))
    return far[::-1]


def spread_small(vectors, ring, size, awaited):
    me = lax.axis_index("ring")
    width = vectors.shape[1] // ring

    def part(hop):
        start = lax.rem(me + hop, ring) * width
        return lax.dynamic_slice_in_dim(vectors, start, width, 1)

    arrived = [
        lax.ppermute(part(hop), "ring", [(i, (i + hop) % ring) for i in range(ring)])
        for hop in range(1, ring)
    ]
    vectors = part(0) + sum(arrived)
    me = lax.axis_index(GROUP)
    bit = size // 2
    while bit:
        if bit == size // 2:
            (vectors,) = after([vectors], *awaited)
        width = vectors.shape[1] // 2
        mine = (me & bit) > 0
        low, high = vectors[:, :width], vectors[:, width:]
        vectors = jnp.where(mine, high, low) + swap(jnp.where(mine, low, high), bit, size)
        bit //= 2
    return vectors


def order_matrix(rows):
    index = np.arange(rows * SUB)
    return (index % rows * SUB + index // rows)[:, None] == index[None, :]


def to_group(value):
    return lax.all_to_all(value, GROUP, split_axis=0, concat_axis=0, tiled=True)


def body(
    inputs,
    out_grad,
    reset_flags,
    weights,
    ln_gain,
    layer_norm_bias,
    reset_peep,
    forget_bias,
    reset_bias,
):
    rows_dev, span, model = inputs.shape
    layers, shard, _ = weights.shape
    ring = lax.axis_size("ring")
    half = lax.axis_size("rows")
    group = 2 * half
    place = jnp.stack([lax.axis_index("ring"), lax.axis_index("pair"), lax.axis_index("rows")])
    place = place.astype(jnp.int32)
    me = lax.axis_index(GROUP)
    width = model // group
    rows = rows_dev * half
    local = rows_dev * span
    tokens = 2 * rows * span
    order = jnp.asarray(order_matrix(rows), BF16)
    back = jnp.asarray(order_matrix(rows).T, BF16)

    columns = columns_of(weights, 1, group, width)
    mine = send_columns(place, weights, 0, group, width, reset_flags)
    got = [mine[0]] + [swap(mine[k], k, group) for k in range(1, group)]
    *normed, split = first_norm(inputs, out_grad, ln_gain, layer_norm_bias, group, (mine[0],))
    pair_mine, reset_mine, flags = stack_columns(place, got, shard, (normed[0], columns))
    pair_w1 = lax.all_gather(pair_mine, "ring", axis=0, tiled=True)
    reset_w1 = lax.all_gather(reset_mine, "ring", axis=0, tiled=True)
    flags = flags[:, :rows_dev, :span].reshape(2, rows, span)
    keep = (1.0 - flags.astype(F32)).transpose(0, 2, 1).reshape(tokens, 1)
    keep = jnp.broadcast_to(keep, (tokens, LANES))
    vectors = jnp.stack([ln_gain, layer_norm_bias, reset_peep, forget_bias, reset_bias], axis=1)
    vectors = lax.dynamic_slice_in_dim(vectors.reshape(layers * 5, model), me * width, width, 1)
    vectors = jnp.pad(vectors, ((0, 16 - layers * 5), (0, 0)))
    pieces1 = gather_group(*after(normed, pair_mine), group, (keep, vectors))

    cf1, whole1, part = project(place, 0, pieces1, pair_w1, order, keep, vectors, rows, True)
    far1 = exchange(part, ring, False)
    (split,) = after([split], *pieces1)
    split = to_group(split).reshape(2, half, 2, rows_dev, span, width)
    (columns,) = after([columns], split, *far1)
    columns = to_group(columns)
    ur1 = reset_product(whole1, reset_w1, width)
    (columns,) = after([columns], ur1)
    w2 = lax.all_gather(
        columns.reshape(group * shard, 3 * width), "ring", axis=0, tiled=True
    )
    x2, stats = advance(0, cf1, ur1, split, keep, order, vectors, far1)
    stats = lax.all_gather(stats, GROUP)
    *normed, mean2, scale2 = middle_norm(1, model, x2, stats, vectors, rows)

    def mixed():
        def thirds(value):
            high = value.astype(BF16)
            middle = (value - high.astype(F32)).astype(BF16)
            low = (value - high.astype(F32) - middle.astype(F32)).astype(BF16)
            return [high, middle, low]

        lines = jnp.stack(thirds(ln_gain[1]) + thirds(layer_norm_bias[1]))
        lines = jnp.pad(lines, ((0, 10), (0, 0)))
        both = jnp.dot(lines, w2, preferred_element_type=F32)
        return jnp.pad(jnp.sum(both[:6].reshape(2, 3, 3 * width), axis=1), ((0, 6), (0, 0)))

    pieces2 = gather_group(*normed, group)

    cf2, whole2, part = project(place, 1, pieces2, w2, order, keep, vectors, rows, False)
    far = exchange(part, ring, False)
    ur2 = reset_product(whole2, w2, width)
    prev2, dr2, dc2, high2, out, du_r2, part, sums2 = turn(
        1, cf2, ur2, x2, split, keep, order, back, vectors, far
    )
    far = exchange(part, ring, True)

    def scatter(term):
        return lax.psum_scatter(term, "ring", scatter_dimension=0, tiled=True)

    du_p2, forget2, stats = retreat(
        1, dc2, dr2, prev2, cf2, keep, vectors, far, rows, span, (), ur=ur2, mixed=mixed()
    )

    def slices(slots):
        return jnp.stack([me ^ k for k in slots]).astype(jnp.int32)

    terms = []

    def weigh(whole, du_p, du_r, *others):
        def work(awaited):
            term = weight_term(whole, du_p, du_r, (*awaited, *others))
            terms.append(scatter(term).reshape(group, shard, 3 * width))
            return term

        return work

    kept, core, pair, line, (stats,) = reduce_group(
        lambda slots, awaited: back_features(
            slices(slots), du_p2, du_r2, w2, awaited
        ),
        group,
        (stats,),
        (),
        weigh(whole2, du_p2, du_r2),
    )

    prev1, dr1, dc1, high1, du_r1, rows_r1, part, sums1 = middle_back(
        1, model, kept, core, pair, line, high2, x2, mean2, scale2, stats, cf1, ur1, split, keep,
        order, back, vectors, out, far1,
    )
    far = exchange(part, ring, True)
    high = to_group(high1.reshape(group, 2, local, width))
    du_p1, rows_p1, forget1 = retreat(
        0, dc1, dr1, prev1, cf1, keep, vectors, far, rows, span, (), back=back
    )
    kept, core, pair, line, _ = reduce_group(
        lambda slots, awaited: back_tokens(
            slices(slots), rows_p1, rows_r1, pair_w1, reset_w1, awaited
        ),
        group,
        (),
        terms[:1],
        weigh(whole1, du_p1, du_r1, high),
    )
    outputs = join(high).reshape(rows_dev, span, model)
    (both,) = after([jnp.concatenate([terms[1], terms[0]], axis=2)], pair, line, outputs)
    both = to_group(both)
    input_grad, gains1 = first_back(
        kept, core, pair, line, inputs.reshape(local, model), ln_gain, high
    )
    input_grad = input_grad.reshape(rows_dev, span, model)
    weight_grad = join_weights(both, layers)

    def total(value):
        return jnp.sum(value, axis=-2)

    sums1 = total(sums1)
    sums2 = total(sums2)
    narrow = jnp.stack(
        [
            sums1[2], total(forget1), sums1[3],
            sums1[0], sums1[1], sums2[0], total(forget2), sums2[1],
        ]
    )
    narrow = lax.dynamic_update_slice(jnp.zeros((8, model), F32), narrow, (0, me * width))
    small = jnp.concatenate([total(gains1), narrow])
    small = spread_small(small, ring, group, (both,)).reshape(2, 5, shard)
    return (outputs, input_grad, weight_grad) + tuple(small[:, i] for i in range(5))


def solution(mesh):
    ring = mesh.shape["tm"] // 2
    fine = Mesh(
        mesh.devices.reshape(ring, 2, mesh.shape["rows"]), ("ring", "pair", "rows")
    )
    tm = ("ring", "pair")
    everything = ("ring", "pair", "rows")
    return jax.shard_map(
        body,
        mesh=fine,
        in_specs=(
            P("rows", tm, None),
            P("rows", tm, None),
            P("rows", tm),
            P(None, everything, None),
            P(),
            P(),
            P(),
            P(),
            P(),
        ),
        out_specs=(
            P("rows", tm, None),
            P("rows", tm, None),
            P(None, everything, None),
            P(None, everything),
            P(None, everything),
            P(None, everything),
            P(None, everything),
            P(None, everything),
        ),
        check_vma=False,
    )
```

```python
import functools

import jax
import jax.numpy as jnp
import numpy as np
from jax import lax
from jax.experimental import pallas as pl
from jax.experimental.pallas import tpu as pltpu
from jax.sharding import Mesh
from jax.sharding import PartitionSpec as P

LANES = 128
SUBLANES = 8
STEPS = 64
SUB = 32
VMEM_BYTES = 58 * 1024 * 1024
GAIN, BIAS, PEEP, FORGET, RESET = range(5)
BF16 = jnp.bfloat16
F32 = jnp.float32
GROUP = ("pair", "rows")
CORE, LINE, PAIR = 1, 2, 4


def shape_of(dtype, *shape):
    return jax.ShapeDtypeStruct(shape, dtype)


def run(
    kernel, name, grid, ins, in_specs, outs, out_specs, scratch=(), place=None, cost=(0, 0), awaited=(),
    aliases=None,
):
    scalars = 0 if place is None else 1
    first = scalars + len(ins)
    last = first + len(awaited)

    def body(*refs):
        kernel(*refs[:first], *refs[last:])

    function = pl.pallas_call(
        body,
        out_shape=outs,
        grid_spec=pltpu.PrefetchScalarGridSpec(
            num_scalar_prefetch=scalars,
            grid=grid,
            in_specs=list(in_specs) + [pl.BlockSpec(memory_space=pl.ANY)] * len(awaited),
            out_specs=out_specs,
            scratch_shapes=list(scratch),
        ),
        compiler_params=pltpu.CompilerParams(vmem_limit_bytes=VMEM_BYTES),
        cost_estimate=pl.CostEstimate(flops=cost[0], bytes_accessed=cost[1], transcendentals=0),
        input_output_aliases=aliases or {},
        name=name,
    )
    return function(*(() if place is None else (place,)), *ins, *awaited)


def quarter(index, width):
    return pl.ds(pl.multiple_of(index * width, width), width)


def fixed_spec(*shape):
    return pl.BlockSpec(shape, lambda *_: (0,) * len(shape))


def block_spec(block, width):
    return pl.BlockSpec((block, width), lambda i, *_: (i, 0))


def turned_spec(block, width, count):
    return pl.BlockSpec((block, width), lambda i, *_: (count - 1 - i, 0))


def rows_spec(rows, width, per, place_of=lambda i: i):
    return pl.BlockSpec(
        (1, rows, STEPS, width), lambda i, *_: (place_of(i) // per, 0, place_of(i) % per, 0)
    )


def split_spec(half, rows_dev, width, per, which):
    return pl.BlockSpec(
        (1, half, 1, rows_dev, STEPS, width), lambda i, *_: (i // per, 0, which, 0, i % per, 0)
    )


def row_at(vec_ref, layer, which):
    row = layer * 5 + which
    return vec_ref[row : row + 1, :]


def chunks(total, size, body, unroll=1):
    def one(i, carry):
        body(pl.ds(pl.multiple_of(i * size, size), size))
        return carry

    lax.fori_loop(0, total // size, one, 0, unroll=unroll)


def over_time(body, state, backward=False):
    def one(i, state):
        t = STEPS - 1 - i if backward else i
        return body(pl.ds(pl.multiple_of(t * SUBLANES, SUBLANES), SUBLANES), state)

    return lax.fori_loop(0, STEPS, one, state, unroll=8)


def widen(keep, width):
    return jnp.concatenate([keep] * (width // LANES), axis=1)


def incoming(far):
    state = None
    for ref in reversed(far):
        state = ref[1] if state is None else ref[0] * state + ref[1]
    return state


def exact(order, value):
    return jnp.dot(order, value, preferred_element_type=F32)


def to_time(order_ref, rows, put):
    block = order_ref.shape[0]
    for i in range(STEPS // SUB):
        part = rows[:, i * SUB : (i + 1) * SUB, :].reshape(block, rows.shape[-1])
        put(slice(i * block, (i + 1) * block), exact(order_ref[...], part))


def to_rows(back_ref, value_ref, out_ref):
    block = back_ref.shape[0]
    for i in range(STEPS // SUB):
        part = exact(back_ref[...], value_ref[i * block : (i + 1) * block, :])
        at = slice(i * SUB, (i + 1) * SUB)
        part = part.astype(BF16)
        if len(out_ref.shape) == 4:
            out_ref[0, :, at, :] = part.reshape(out_ref.shape[1], SUB, out_ref.shape[3])
        else:
            _, half, _, rows_dev, _, width = out_ref.shape
            out_ref[0, :, 0, :, at, :] = part.reshape(half, rows_dev, SUB, width)


def forget_gate(cf_ref, here, vec_ref, layer):
    width = cf_ref.shape[1] // 2
    return jax.nn.sigmoid(cf_ref[here, width:] + row_at(vec_ref, layer, FORGET))


def fold(value):
    return jnp.sum(value.reshape(-1, SUBLANES, value.shape[-1]), axis=0)


def after(values, *awaited):
    count = len(values)

    def nothing(*refs):
        pass

    return pl.pallas_call(
        nothing,
        out_shape=[shape_of(v.dtype, *v.shape) for v in values],
        in_specs=[pl.BlockSpec(memory_space=pl.ANY)] * (count + len(awaited)),
        out_specs=[pl.BlockSpec(memory_space=pl.ANY)] * count,
        input_output_aliases={i: i for i in range(count)},
        name="after",
    )(*values, *awaited)


def columns_kernel(group, width, weights_ref, out_ref):
    for s in range(group):
        for third in range(3):
            start = third * group * width + s * width
            out_ref[s, :, third * width : (third + 1) * width] = weights_ref[
                0, :, start : start + width
            ]


def columns_of(weights, layer, group, width, awaited=()):
    _, shard, total = weights.shape
    return run(
        functools.partial(columns_kernel, group, width),
        "columns_of",
        (1,),
        [weights],
        [pl.BlockSpec((1, shard, total), lambda i, *_: (layer, 0, 0))],
        shape_of(BF16, group, shard, 3 * width),
        fixed_spec(group, shard, 3 * width),
        cost=(0, 4 * shard * total),
        awaited=awaited,
    )


def pick_vectors_kernel(place, *refs):
    out_ref = refs[-1]
    count = len(refs) - 1
    layers = refs[0].shape[0]
    out_ref[...] = jnp.zeros_like(out_ref)
    for layer in range(layers):
        for which in range(count):
            row = layer * count + which
            out_ref[row : row + 1, :] = refs[which][layer : layer + 1, :]


def pick_vectors(place, vectors, width, half, awaited):
    layers = vectors[0].shape[0]
    mine = pl.BlockSpec((layers, width), lambda i, place: (0, place[1] * half + place[2]))
    return run(
        pick_vectors_kernel,
        "pick_vectors",
        (1,),
        vectors,
        [mine] * len(vectors),
        shape_of(F32, 16, width),
        fixed_spec(16, width),
        (),
        place,
        (0, 64 * width),
        awaited,
    )


def stack_columns_kernel(place, *refs):
    pieces, (pair_ref, reset_ref, flags_ref) = refs[:-3], refs[-3:]
    group = len(pieces)
    half = group // 2
    shard = pair_ref.shape[0] // group
    both = pair_ref.shape[1]
    for k in range(group):
        at = (place[1] ^ (k // half)) * half + (place[2] ^ (k % half))
        here = pl.ds(pl.multiple_of(at * shard, shard), shard)
        pair_ref[here, :] = pieces[k][:shard, :both]
        reset_ref[here, :] = pieces[k][:shard, both:]
        flags_ref[at] = pieces[k][shard:, :LANES]


def stack_columns(place, pieces, shard, awaited):
    group = len(pieces)
    rows, total = pieces[0].shape
    outs = [
        (group * shard, total // 3 * 2),
        (group * shard, total // 3),
        (group, rows - shard, LANES),
    ]
    return run(
        stack_columns_kernel,
        "stack_columns",
        (1,),
        pieces,
        [fixed_spec(rows, total)] * group,
        [shape_of(BF16, *out) for out in outs],
        [fixed_spec(*out) for out in outs],
        (),
        place,
        (0, 4 * group * shard * total),
        awaited,
    )


def send_columns_kernel(group, width, place, weights_ref, flags_ref, *outs):
    half = group // 2
    shard = weights_ref.shape[1]
    below = flags_ref[...].astype(F32)
    fill = jnp.zeros((outs[0].shape[0] - shard - below.shape[0], below.shape[1]), F32)
    below = jnp.concatenate([below, fill]).astype(BF16)
    for k in range(group):
        at = (place[1] ^ (k // half)) * half + (place[2] ^ (k % half))
        for third in range(3):
            start = pl.multiple_of(third * group * width + at * width, width)
            outs[k][:shard, third * width : (third + 1) * width] = weights_ref[
                0, :, pl.ds(start, width)
            ]
        outs[k][shard:, :] = jnp.zeros_like(outs[k][shard:, :])
        outs[k][shard:, : flags_ref.shape[1]] = below


def send_columns(place, weights, layer, group, width, flags):
    _, shard, total = weights.shape
    rows = shard + 2 * SUBLANES
    return run(
        functools.partial(send_columns_kernel, group, width),
        "send_columns",
        (1,),
        [weights, flags],
        [pl.BlockSpec((1, shard, total), lambda i, *_: (layer, 0, 0)), fixed_spec(*flags.shape)],
        [shape_of(BF16, rows, 3 * width)] * group,
        [fixed_spec(rows, 3 * width)] * group,
        (),
        place,
        (0, 4 * shard * total),
    )


def first_norm_kernel(group, x_ref, grad_ref, gain_ref, bias_ref, *refs):
    split_ref = refs[-1]
    rows, span, model = x_ref.shape
    width = model // group
    for i in range(rows):

        def part(here):
            wide = x_ref[i, here, :].astype(F32)
            centered = wide - jnp.mean(wide, axis=-1, keepdims=True)
            scale = lax.rsqrt(jnp.mean(centered * centered, axis=-1, keepdims=True) + 1e-05)
            refs[i][here, :] = (
                centered * scale * gain_ref[0:1, :] + bias_ref[0:1, :]
            ).astype(BF16)

        chunks(span, 16, part)
        for s in range(group):
            columns = slice(s * width, (s + 1) * width)
            split_ref[s, 0, i] = x_ref[i, :, columns]
            split_ref[s, 1, i] = grad_ref[i, :, columns]


def first_norm(x, grad, gain, bias, group, awaited):
    rows, span, model = x.shape
    split = (group, 2, rows, span, model // group)
    return run(
        functools.partial(first_norm_kernel, group),
        "first_norm",
        (1,),
        [x, grad, gain, bias],
        [fixed_spec(*a.shape) for a in (x, grad, gain, bias)],
        [shape_of(BF16, span, model)] * rows + [shape_of(BF16, *split)],
        [fixed_spec(span, model)] * rows + [fixed_spec(*split)],
        cost=(20 * rows * span * model, 8 * rows * span * model),
        awaited=awaited,
    )


def project_kernel(layer, gather, slots, place, *refs):
    pieces = refs[:slots]
    w_ref, order_ref, keep_ref, vec_ref = refs[slots : slots + 4]
    cf_ref, whole_ref, tot_ref, held, forget_s = refs[slots + 4 :]
    width = cf_ref.shape[1] // 2
    step = pl.program_id(0)
    gather(place, step, pieces, order_ref, held, whole_ref)
    cf_ref[...] = jnp.dot(whole_ref[...], w_ref[...], preferred_element_type=F32)

    def gates(here):
        forget_s[here, :] = forget_gate(cf_ref, here, vec_ref, layer)

    chunks(cf_ref.shape[0], 64, gates)

    @pl.when(step == 0)
    def _():
        tot_ref[0] = jnp.ones_like(tot_ref[0])
        tot_ref[1] = jnp.zeros_like(tot_ref[1])

    def one(at, state):
        forget = forget_s[at, :]
        decay = forget * widen(keep_ref[at, :], width)
        return state[0] * decay, state[1] * decay + (1.0 - forget) * cf_ref[at, :width]

    product, state = over_time(one, (tot_ref[0], tot_ref[1]))
    tot_ref[0] = product
    tot_ref[1] = state


def gather_rows(per, group, place, step, pieces, order_ref, held, whole_ref):
    half = group // 2
    other = (step // per) ^ place[1]
    for side in range(2):

        @pl.when(other == side)
        def _():
            for k in range(half):
                for i in range(2):
                    held[place[2] ^ k, i] = pieces[2 * (side * half + k) + i][...]

    def put(here, value):
        whole_ref[here, :] = value.astype(BF16)

    to_time(order_ref, held[...].reshape(-1, STEPS, whole_ref.shape[1]), put)


def gather_features(per, group, place, step, pieces, order_ref, held, whole_ref):
    half = group // 2
    width = whole_ref.shape[1] // group
    for side in range(2):

        @pl.when(step // per == side)
        def _():
            for k in range(group):
                at = (place[1] ^ (k // half)) * half + (place[2] ^ (k % half))
                whole_ref[:, quarter(at, width)] = pieces[2 * k + side][...]


def project(place, layer, pieces, matrix, order, keep, vectors, rows, by_rows):
    model = matrix.shape[0]
    width = vectors.shape[1]
    both = 2 * width
    tokens = keep.shape[0]
    block = rows * STEPS
    count = tokens // block
    per = count // 2
    group = model // width
    half = group // 2
    specs = []
    for k in range(group):
        for side in range(2):
            if by_rows:

                def index(i, place, needed=k // half):
                    mine = ((i // per) ^ place[1]) == needed
                    return (jnp.where(mine, i % per, 0), 0)

                specs.append(pl.BlockSpec((STEPS, model), index))
            elif side == 0:
                specs.append(
                    pl.BlockSpec((block, width), lambda i, place: (jnp.minimum(i, per - 1), 0))
                )
            else:
                specs.append(
                    pl.BlockSpec((block, width), lambda i, place: (jnp.maximum(i - per, 0), 0))
                )
    gather = functools.partial(gather_rows if by_rows else gather_features, per, group)
    held = pltpu.VMEM((half, 2, STEPS, model) if by_rows else (2 * SUBLANES, LANES), BF16)
    return run(
        functools.partial(project_kernel, layer, gather, len(pieces)),
        "project",
        (count,),
        [*pieces, matrix, order, keep, vectors],
        specs
        + [
            fixed_spec(model, both),
            fixed_spec(*order.shape),
            block_spec(block, LANES),
            fixed_spec(*vectors.shape),
        ],
        [
            shape_of(F32, tokens, both),
            shape_of(BF16, tokens, model),
            shape_of(F32, 2, rows, width),
        ],
        [block_spec(block, both), block_spec(block, model), fixed_spec(2, rows, width)],
        [held, pltpu.VMEM((block, width), F32)],
        place,
        (2 * tokens * model * both, 4 * tokens * model + 4 * tokens * both + 2 * model * both),
    )


def reset_kernel(x_ref, w_ref, out_ref):
    out_ref[...] = jnp.dot(x_ref[...], w_ref[...], preferred_element_type=F32)


def reset_product(whole, matrix, width):
    tokens, model = whole.shape
    last = matrix.shape[1] // width - 1
    block = tokens // 4
    return run(
        reset_kernel,
        "reset_product",
        (4,),
        [whole, matrix],
        [block_spec(block, model), pl.BlockSpec((model, width), lambda *_: (0, last))],
        shape_of(F32, tokens, width),
        block_spec(block, width),
        cost=(2 * tokens * model * width, 2 * tokens * model + 4 * tokens * width),
    )


def carry_forward(layer, cf_ref, keep_ref, vec_ref, far, carry_s, forget_s, prev_ref, state_s):
    width = prev_ref.shape[1]

    def gates(here):
        forget_s[here, :] = forget_gate(cf_ref, here, vec_ref, layer)

    chunks(forget_s.shape[0], 64, gates)

    @pl.when(pl.program_id(0) == 0)
    def _():
        first = incoming(far)
        carry_s[...] = jnp.zeros_like(carry_s) if first is None else first

    def one(at, state):
        forget = forget_s[at, :]
        prev = widen(keep_ref[at, :], width) * state
        new = forget * prev + (1.0 - forget) * cf_ref[at, :width]
        prev_ref[at, :] = prev
        state_s[at, :] = new
        return new

    carry_s[...] = over_time(one, carry_s[...])


def reset_gate(layer, ur_ref, prev_ref, here, vec_ref):
    return jax.nn.sigmoid(
        ur_ref[here, :]
        + row_at(vec_ref, layer, PEEP) * prev_ref[here, :]
        + row_at(vec_ref, layer, RESET)
    )


def advance_kernel(layer, cf_ref, ur_ref, x_ref, keep_ref, order_ref, vec_ref, *refs):
    xn_ref, stat_ref, carry_s, forget_s, prev_s, state_s, x_s = refs[-7:]
    far = refs[:-7]
    block, width = xn_ref.shape

    def put(here, value):
        x_s[here, :] = value

    to_time(order_ref, x_ref[...].reshape(-1, STEPS, width), put)
    carry_forward(layer, cf_ref, keep_ref, vec_ref, far, carry_s, forget_s, prev_s, state_s)

    def finish(here):
        gate = reset_gate(layer, ur_ref, prev_s, here, vec_ref)
        xn = gate * state_s[here, :] + (1.0 - gate) * x_s[here, :]
        xn_ref[here, :] = xn
        mean = jnp.mean(xn, axis=-1, keepdims=True)
        off = xn - mean
        spread = sum(off[:, j : j + LANES] * off[:, j : j + LANES] for j in range(0, width, LANES))
        x_s[here, :LANES] = jnp.broadcast_to(mean, (here.size, LANES))
        state_s[here, :LANES] = spread

    chunks(block, 64, finish)
    for b in range(block // LANES):
        here = slice(b * LANES, (b + 1) * LANES)
        row = pl.ds(pl.program_id(0) * (block // LANES) + b, 1)
        stat_ref[0, row, :] = x_s[here, :LANES].T[0:1, :]
        stat_ref[1, row, :] = jnp.sum(state_s[here, :LANES].T, axis=0, keepdims=True)


def advance(layer, cf, ur, x, keep, order, vectors, far):
    tokens, width = ur.shape
    _, half, _, rows_dev, span, _ = x.shape
    rows = half * rows_dev
    block = rows * STEPS
    part = block_spec(block, width)
    return run(
        functools.partial(advance_kernel, layer),
        "advance",
        (tokens // block,),
        [cf, ur, x, keep, order, vectors, *far],
        [
            block_spec(block, 2 * width),
            part,
            split_spec(half, rows_dev, width, span // STEPS, 0),
            block_spec(block, LANES),
            fixed_spec(*order.shape),
            fixed_spec(*vectors.shape),
        ]
        + [fixed_spec(2, rows, width)] * len(far),
        [shape_of(F32, tokens, width), shape_of(F32, 2, tokens // LANES, LANES)],
        [part, fixed_spec(2, tokens // LANES, LANES)],
        [pltpu.VMEM((rows, width), F32)] + [pltpu.VMEM((block, width), F32)] * 4,
        None,
        (60 * tokens * width, 22 * tokens * width),
    )


def norm_columns(stat_ref, block, width, model, mean_s, scale_s):
    group = stat_ref.shape[0]
    for b in range(block // LANES):
        row = pl.ds(pl.program_id(0) * (block // LANES) + b, 1)
        here = slice(b * LANES, (b + 1) * LANES)
        means = [stat_ref[s, 0, row, :] for s in range(group)]
        mean = sum(means) / group
        square = sum(stat_ref[s, 1, row, :] for s in range(group))
        between = sum((part - mean) * (part - mean) for part in means)
        scale = lax.rsqrt((square + between * width) / model + 1e-05)
        mean_s[here, :] = jnp.broadcast_to(mean, (LANES, LANES)).T
        scale_s[here, :] = jnp.broadcast_to(scale, (LANES, LANES)).T


def middle_norm_kernel(layer, model, xn_ref, stat_ref, vec_ref, a_ref, b_ref, mean_s, scale_s):
    block, width = xn_ref.shape
    norm_columns(stat_ref, block, width, model, mean_s, scale_s)
    per = pl.num_programs(0) // 2
    for side, normed_ref in enumerate((a_ref, b_ref)):

        @pl.when(pl.program_id(0) // per == side)
        def _():
            def part(here):
                normed_ref[here, :] = (
                    (xn_ref[here, :] - widen(mean_s[here, :], width))
                    * widen(scale_s[here, :], width)
                    * row_at(vec_ref, layer, GAIN)
                    + row_at(vec_ref, layer, BIAS)
                ).astype(BF16)

            chunks(block, 64, part)


def middle_norm(layer, model, xn, stats, vectors, rows):
    tokens, width = xn.shape
    block = rows * STEPS
    per = tokens // block // 2
    return run(
        functools.partial(middle_norm_kernel, layer, model),
        "middle_norm",
        (tokens // block,),
        [xn, stats, vectors],
        [block_spec(block, width), fixed_spec(*stats.shape), fixed_spec(*vectors.shape)],
        [shape_of(BF16, tokens // 2, width)] * 2,
        [
            pl.BlockSpec((block, width), lambda i, *_: (jnp.minimum(i, per - 1), 0)),
            pl.BlockSpec((block, width), lambda i, *_: (jnp.maximum(i - per, 0), 0)),
        ],
        [pltpu.VMEM((block, LANES), F32)] * 2,
        cost=(10 * tokens * width, 8 * tokens * width),
    )


def add_total(decay_s, drive_s, tot_ref):
    @pl.when(pl.program_id(0) == 0)
    def _():
        tot_ref[0] = jnp.ones_like(tot_ref[0])
        tot_ref[1] = jnp.zeros_like(tot_ref[1])

    def one(at, state):
        return state[0] * decay_s[at, :], state[1] + state[0] * drive_s[at, :]

    product, total = over_time(one, (tot_ref[0], tot_ref[1]))
    tot_ref[0] = product
    tot_ref[1] = total


def turn_kernel(layer, cf_ref, ur_ref, x_ref, dh_ref, keep_ref, order_ref, back_ref, vec_ref, *refs):
    prev_ref, dr_ref, dc_ref, high_ref, out_ref, du_ref, tot_ref, small_ref = refs[-14:-6]
    carry_s, forget_s, state_s, dh_s, drive_s, out_s = refs[-6:]
    far = refs[:-14]
    block, width = prev_ref.shape

    def put(here, value):
        dh_s[here, :] = value

    to_time(order_ref, dh_ref[...].reshape(-1, STEPS, width), put)
    carry_forward(layer, cf_ref, keep_ref, vec_ref, far, carry_s, forget_s, prev_ref, state_s)

    @pl.when(pl.program_id(0) == 0)
    def _():
        small_ref[...] = jnp.zeros_like(small_ref)

    def finish(here):
        state = state_s[here, :]
        x = x_ref[here, :]
        dh = dh_s[here, :]
        prev = prev_ref[here, :]
        gate = reset_gate(layer, ur_ref, prev_ref, here, vec_ref)
        out_s[here, :] = (gate * state + (1.0 - gate) * x).astype(BF16)
        dr = dh * (state - x) * gate * (1.0 - gate)
        dc = dh * gate
        dr_ref[here, :] = dr
        dc_ref[here, :] = dc
        du_ref[here, :] = dr.astype(BF16)
        high_ref[here, :] = dh - dc
        keep = widen(keep_ref[here, :], width)
        decay = keep * forget_s[here, :]
        state_s[here, :] = decay
        drive_s[here, :] = keep * row_at(vec_ref, layer, PEEP) * dr + decay * dc
        small_ref[0] += fold(dr * prev)
        small_ref[1] += fold(dr)

    chunks(block, 32, finish)
    to_rows(back_ref, out_s, out_ref)
    add_total(state_s, drive_s, tot_ref)


def turn(layer, cf, ur, x, dh, keep, order, back, vectors, far):
    tokens, width = ur.shape
    _, half, _, rows_dev, span, _ = dh.shape
    rows = half * rows_dev
    block = rows * STEPS
    part = block_spec(block, width)
    by_rows = split_spec(half, rows_dev, width, span // STEPS, 0)
    return run(
        functools.partial(turn_kernel, layer),
        "turn",
        (tokens // block,),
        [cf, ur, x, dh, keep, order, back, vectors, *far],
        [
            block_spec(block, 2 * width),
            part,
            part,
            split_spec(half, rows_dev, width, span // STEPS, 1),
            block_spec(block, LANES),
            fixed_spec(*order.shape),
            fixed_spec(*back.shape),
            fixed_spec(*vectors.shape),
        ]
        + [fixed_spec(2, rows, width)] * len(far),
        [shape_of(F32, tokens, width)] * 4
        + [
            shape_of(BF16, *dh.shape),
            shape_of(BF16, tokens, width),
            shape_of(F32, 2, rows, width),
            shape_of(F32, 2, SUBLANES, width),
        ],
        [part] * 4
        + [by_rows, part, fixed_spec(2, rows, width), fixed_spec(2, SUBLANES, width)],
        [pltpu.VMEM((rows, width), F32)]
        + [pltpu.VMEM((block, width), F32)] * 4
        + [pltpu.VMEM((block, width), BF16)],
        None,
        (80 * tokens * width, 36 * tokens * width),
    )


def retreat_kernel(layer, sums, dc_ref, dr_ref, prev_ref, cf_ref, keep_ref, vec_ref, *refs):
    if sums:
        ur_ref, mixed_ref = refs[:2]
        du_ref, small_ref, stat_ref, carry_s, forget_s, total_s, sum_s, cross_s = refs[-8:]
        far = refs[2:-8]
    else:
        back_ref = refs[0]
        du_ref, rows_ref, small_ref, carry_s, forget_s, total_s = refs[-6:]
        far = refs[1:-6]
    block, width = prev_ref.shape
    peep = row_at(vec_ref, layer, PEEP)

    @pl.when(pl.program_id(0) == 0)
    def _():
        first = incoming(far)
        carry_s[...] = jnp.zeros_like(carry_s) if first is None else first
        small_ref[...] = jnp.zeros_like(small_ref)

    def gates(here):
        forget_s[here, :] = forget_gate(cf_ref, here, vec_ref, layer)

    chunks(block, 64, gates)

    def one(at, state):
        total = dc_ref[at, :] + state
        total_s[at, :] = total
        return widen(keep_ref[at, :], width) * (peep * dr_ref[at, :] + forget_s[at, :] * total)

    carry_s[...] = over_time(one, carry_s[...], True)

    def halves(value):
        return sum(value[:, j : j + LANES] for j in range(0, width, LANES))

    def finish(here):
        forget = forget_s[here, :]
        slow = total_s[here, :] * (1.0 - forget)
        d_forget = slow * forget * (prev_ref[here, :] - cf_ref[here, :width])
        d_cand = slow.astype(BF16)
        d_gate = d_forget.astype(BF16)
        du_ref[here, :width] = d_cand
        du_ref[here, width:] = d_gate
        small_ref[...] += fold(d_forget)
        if sums:
            parts = [d_cand, d_gate, dr_ref[here, :].astype(BF16)]
            inputs = [cf_ref[here, :width], cf_ref[here, width:], ur_ref[here, :]]
            plain = cross = 0.0
            for third in range(3):
                at = slice(third * width, (third + 1) * width)
                du = parts[third].astype(F32)
                plain = plain + du * mixed_ref[0:1, at]
                cross = cross + du * (inputs[third] - mixed_ref[1:2, at])
            sum_s[here, :] = halves(plain)
            cross_s[here, :] = halves(cross)

    chunks(block, 32, finish)
    if sums:
        base = (pl.num_programs(0) - 1 - pl.program_id(0)) * (block // LANES)
        for b in range(block // LANES):
            here = slice(b * LANES, (b + 1) * LANES)
            stat_ref[0, pl.ds(base + b, 1), :] = jnp.sum(sum_s[here, :].T, axis=0, keepdims=True)
            stat_ref[1, pl.ds(base + b, 1), :] = jnp.sum(cross_s[here, :].T, axis=0, keepdims=True)
    else:
        to_rows(back_ref, du_ref, rows_ref)


def retreat(layer, dc, dr, prev, cf, keep, vectors, far, rows, span, awaited, back=None, ur=None, mixed=None):
    tokens, width = dc.shape
    block = rows * STEPS
    count = tokens // block
    sums = back is None
    part = turned_spec(block, width, count)
    both = turned_spec(block, 2 * width, count)
    rows_out = rows_spec(rows, 2 * width, span // STEPS, lambda i: count - 1 - i)
    outs = [shape_of(BF16, tokens, 2 * width)]
    specs = [both]
    scratch = [pltpu.VMEM((rows, width), F32)] + [pltpu.VMEM((block, width), F32)] * 2
    if sums:
        more, more_specs = [ur, mixed], [part, fixed_spec(*mixed.shape)]
        outs += [shape_of(F32, SUBLANES, width), shape_of(F32, 2, tokens // LANES, LANES)]
        specs += [fixed_spec(SUBLANES, width), fixed_spec(2, tokens // LANES, LANES)]
        scratch += [pltpu.VMEM((block, LANES), F32)] * 2
    else:
        more, more_specs = [back], [fixed_spec(*back.shape)]
        outs += [shape_of(BF16, 2, rows, span, 2 * width), shape_of(F32, SUBLANES, width)]
        specs += [rows_out, fixed_spec(SUBLANES, width)]
    return run(
        functools.partial(retreat_kernel, layer, sums),
        "retreat",
        (count,),
        [dc, dr, prev, cf, keep, vectors, *more, *far],
        [part] * 3
        + [both, turned_spec(block, LANES, count), fixed_spec(*vectors.shape)]
        + more_specs
        + [fixed_spec(2, rows, width)] * len(far),
        outs,
        specs,
        scratch,
        None,
        (60 * tokens * width, 30 * tokens * width),
        awaited,
    )


def back_product(pair, reset, w_pair, w_reset):
    contract = (((1,), (1,)), ((), ()))
    return lax.dot_general(pair, w_pair, contract, preferred_element_type=F32) + lax.dot_general(
        reset, w_reset, contract, preferred_element_type=F32
    )


def put_shares(share_of, outs):
    odd, even = outs
    for k in range(odd.shape[0]):
        odd[k] = share_of(k).astype(BF16)
        even[k] = share_of(odd.shape[0] + k).astype(BF16)


def share_outs(count, rows, columns):
    return [shape_of(BF16, count // 2, rows, columns)] * 2


def back_features_kernel(count, order, pair_ref, reset_ref, *refs):
    def share_of(k):
        return back_product(
            pair_ref[...], reset_ref[...], refs[2 * k][...], refs[2 * k + 1][...]
        )

    put_shares(share_of, refs[-2:])


def back_features(order, pair, reset, matrix, awaited):
    tokens, width = reset.shape
    count = order.shape[0]
    block = tokens // 4
    specs = []
    for k in range(count):
        specs.append(pl.BlockSpec((width, 2 * width), lambda i, order, k=k: (order[k], 0)))
        specs.append(pl.BlockSpec((width, width), lambda i, order, k=k: (order[k], 2)))
    outs = share_outs(count, tokens, width)
    return run(
        functools.partial(back_features_kernel, count),
        "back_features",
        (4,),
        [pair, reset] + [matrix, matrix] * count,
        [block_spec(block, 2 * width), block_spec(block, width)] + specs,
        outs,
        [pl.BlockSpec((out.shape[0], block, width), lambda i, order: (0, i, 0)) for out in outs],
        (),
        order,
        (6 * count * tokens * width * width, 8 * count * tokens * width),
        awaited,
    )


def back_tokens_kernel(count, order, wp_ref, wr_ref, *refs):
    local = refs[-1].shape[1]

    def share_of(k):
        pair, reset = refs[2 * k : 2 * k + 2]
        return back_product(
            pair[0].reshape(local, pair.shape[-1]),
            reset[0].reshape(local, reset.shape[-1]),
            wp_ref[...],
            wr_ref[...],
        )

    put_shares(share_of, refs[-2:])


def back_tokens(order, pair, reset, w_pair, w_reset, awaited):
    two, rows, span, width = reset.shape
    model = w_pair.shape[0]
    count = order.shape[0]
    half = model // width // 2
    rows_dev = rows // half
    local = rows_dev * span
    block = model // 4
    specs = []
    for k in range(count):
        by_order = lambda i, order, k=k: (order[k] // half, order[k] % half, 0, 0)
        for columns in (2 * width, width):
            specs.append(pl.BlockSpec((1, rows_dev, span, columns), by_order))
    outs = share_outs(count, local, model)
    return run(
        functools.partial(back_tokens_kernel, count),
        "back_tokens",
        (4,),
        [w_pair, w_reset] + [pair, reset] * count,
        [block_spec(block, 2 * width), block_spec(block, width)] + specs,
        outs,
        [pl.BlockSpec((out.shape[0], local, block), lambda i, order: (0, 0, i)) for out in outs],
        (),
        order,
        (6 * count * local * model * width, 8 * count * local * model),
        awaited,
    )


def middle_back_kernel(layer, model, *refs):
    (
        kept_ref, core_ref, pair_ref, line_ref, high_ref, x_ref, norm_ref, stat_ref,
        cf_ref, ur_ref, below_x_ref, keep_ref, order_ref, back_ref, vec_ref, _,
    ) = refs[:16]
    (
        prev_ref, dr_ref, dc_ref, below_ref, du_ref, rows_ref, tot_ref, small_ref,
        carry_s, forget_s, state_s, drive_s, x_s, plain_s, cross_s, mean_s, scale_s, below_s,
    ) = refs[-18:]
    far = refs[16:-18]
    block, width = prev_ref.shape
    below = layer - 1

    def put(here, value):
        x_s[here, :] = value

    to_time(order_ref, below_x_ref[...].reshape(-1, STEPS, width), put)
    carry_forward(below, cf_ref, keep_ref, vec_ref, far, carry_s, forget_s, prev_ref, state_s)
    for b in range(block // LANES):
        row = pl.ds(pl.program_id(0) * (block // LANES) + b, 1)
        here = slice(b * LANES, (b + 1) * LANES)
        for s, out in enumerate((plain_s, cross_s)):
            out[here, :] = jnp.broadcast_to(stat_ref[s, row, :] / model, (LANES, LANES)).T
    norm_columns(norm_ref, block, width, model, mean_s, scale_s)

    @pl.when(pl.program_id(0) == 0)
    def _():
        small_ref[...] = jnp.zeros_like(small_ref)

    def finish(here):
        back = (
            kept_ref[0, here, :].astype(F32)
            + core_ref[0, here, :].astype(F32)
            + pair_ref[here, :].astype(F32)
            + line_ref[here, :].astype(F32)
        )
        scale = widen(scale_s[here, :], width)
        xhat = (x_ref[here, :] - widen(mean_s[here, :], width)) * scale
        dh = high_ref[here, :] + scale * (
            back * row_at(vec_ref, layer, GAIN)
            - widen(plain_s[here, :], width)
            - xhat * widen(cross_s[here, :], width)
        )
        small_ref[0] += fold(back * xhat)
        small_ref[1] += fold(back)
        gate = reset_gate(below, ur_ref, prev_ref, here, vec_ref)
        dr = dh * (state_s[here, :] - x_s[here, :]) * gate * (1.0 - gate)
        dc = dh * gate
        dr_ref[here, :] = dr
        dc_ref[here, :] = dc
        du_ref[here, :] = dr.astype(BF16)
        below_s[here, :] = (dh - dc).astype(BF16)
        keep = widen(keep_ref[here, :], width)
        decay = keep * forget_s[here, :]
        state_s[here, :] = decay
        drive_s[here, :] = keep * row_at(vec_ref, below, PEEP) * dr + decay * dc
        small_ref[2] += fold(dr * prev_ref[here, :])
        small_ref[3] += fold(dr)

    chunks(block, 32, finish)
    to_rows(back_ref, below_s, below_ref)
    to_rows(back_ref, du_ref, rows_ref)
    add_total(state_s, drive_s, tot_ref)


def middle_back(
    layer, model, kept, core, pair, line, high, x, norm, stats, cf, ur, below_x, keep, order,
    back, vectors, out, far,
):
    tokens, width = ur.shape
    _, half, _, rows_dev, span, _ = below_x.shape
    rows = half * rows_dev
    block = rows * STEPS
    part = block_spec(block, width)
    last = kept.shape[0] - 1
    top = pl.BlockSpec((1, block, width), lambda i, *_: (last, i, 0))
    thin = block_spec(block, LANES)
    by_rows = rows_spec(rows, width, span // STEPS)
    held = pltpu.VMEM((block, width), F32)
    return run(
        functools.partial(middle_back_kernel, layer, model),
        "middle_back",
        (tokens // block,),
        [
            kept, core, pair, line, high, x, norm, stats, cf, ur, below_x, keep, order, back,
            vectors, out, *far,
        ],
        [top, top, part, part, part, part, fixed_spec(*norm.shape), fixed_spec(*stats.shape)]
        + [
            block_spec(block, 2 * width),
            part,
            split_spec(half, rows_dev, width, span // STEPS, 0),
            thin,
            fixed_spec(*order.shape),
            fixed_spec(*back.shape),
            fixed_spec(*vectors.shape),
            pl.BlockSpec(memory_space=pl.ANY),
        ]
        + [fixed_spec(2, rows, width)] * len(far),
        [shape_of(F32, tokens, width)] * 3
        + [
            shape_of(BF16, *out.shape),
            shape_of(BF16, tokens, width),
            shape_of(BF16, 2, rows, span, width),
            shape_of(F32, 2, rows, width),
            shape_of(F32, 4, SUBLANES, width),
        ],
        [part, part, part, split_spec(half, rows_dev, width, span // STEPS, 1), part, by_rows]
        + [fixed_spec(2, rows, width), fixed_spec(4, SUBLANES, width)],
        [pltpu.VMEM((rows, width), F32)]
        + [held] * 4
        + [pltpu.VMEM((block, LANES), F32)] * 4
        + [pltpu.VMEM((block, width), BF16)],
        None,
        (80 * tokens * width, 44 * tokens * width),
        (),
        {15: 3},
    )


def first_back_kernel(kept_ref, core_ref, pair_ref, line_ref, x_ref, gain_ref, high_ref, out_ref, small_ref):
    local, model = x_ref.shape
    group, _, _, width = high_ref.shape

    @pl.when(pl.program_id(0) == 0)
    def _():
        small_ref[...] = jnp.zeros_like(small_ref)

    def part(here):
        wide = x_ref[here, :].astype(F32)
        centered = wide - jnp.mean(wide, axis=-1, keepdims=True)
        scale = lax.rsqrt(jnp.mean(centered * centered, axis=-1, keepdims=True) + 1e-05)
        xhat = centered * scale
        back = (
            kept_ref[0, here, :].astype(F32)
            + core_ref[0, here, :].astype(F32)
            + pair_ref[here, :].astype(F32)
            + line_ref[here, :].astype(F32)
        )
        scaled = back * gain_ref[0:1, :]
        small_ref[0] += fold(back * xhat)
        small_ref[1] += fold(back)
        total = scale * (
            scaled
            - jnp.mean(scaled, axis=-1, keepdims=True)
            - xhat * jnp.mean(scaled * xhat, axis=-1, keepdims=True)
        )
        for s in range(group):
            columns = slice(s * width, (s + 1) * width)
            out_ref[here, columns] = (
                total[:, columns] + high_ref[s, 0, here, :].astype(F32)
            ).astype(BF16)

    chunks(local, 16, part)


def first_back(kept, core, pair, line, x, gain, high):
    local, model = x.shape
    group, _, _, width = high.shape
    last = kept.shape[0] - 1
    block = local // 4
    top = pl.BlockSpec((1, block, model), lambda i, *_: (last, i, 0))
    flat = block_spec(block, model)
    return run(
        first_back_kernel,
        "first_back",
        (4,),
        [kept, core, pair, line, x, gain, high],
        [top, top, flat, flat, flat, fixed_spec(*gain.shape)]
        + [pl.BlockSpec((group, 1, block, width), lambda i, *_: (0, 1, i, 0))],
        [shape_of(BF16, local, model), shape_of(F32, 2, SUBLANES, model)],
        [flat, fixed_spec(2, SUBLANES, model)],
        cost=(30 * local * model, 16 * local * model),
    )


def weight_kernel(whole_ref, pair_ref, reset_ref, out_ref):
    both = pair_ref.shape[1]
    contract = (((0,), (0,)), ((), ()))
    for du_ref, at in ((pair_ref, slice(0, both)), (reset_ref, slice(both, out_ref.shape[1]))):
        out_ref[:, at] = lax.dot_general(
            whole_ref[...], du_ref[...], contract, preferred_element_type=F32
        ).astype(BF16)


def weight_term(whole, pair, reset, awaited=()):
    tokens, model = whole.shape
    width = reset.shape[1]
    block = model // 4
    return run(
        weight_kernel,
        "weight_term",
        (4,),
        [whole, pair, reset],
        [
            pl.BlockSpec((tokens, block), lambda k, *_: (0, k)),
            fixed_spec(*pair.shape),
            fixed_spec(*reset.shape),
        ],
        shape_of(BF16, model, 3 * width),
        block_spec(block, 3 * width),
        cost=(6 * tokens * model * width, 2 * tokens * model + 6 * model * width),
        awaited=awaited,
    )


def join_kernel(x_ref, out_ref):
    group, _, rows, width = x_ref.shape
    for s in range(group):
        out_ref[:, s * width : (s + 1) * width] = x_ref[s, 0]


def join(value):
    group, _, rows, width = value.shape
    return run(
        join_kernel,
        "join",
        (1,),
        [value],
        [fixed_spec(group, 1, rows, width)],
        shape_of(value.dtype, rows, group * width),
        fixed_spec(rows, group * width),
        cost=(0, 4 * rows * group * width),
    )


def join_weights_kernel(part_ref, out_ref):
    layers, _, total = out_ref.shape
    group = part_ref.shape[0]
    width = total // group // 3
    for layer in range(layers):
        for s in range(group):
            for third in range(3):
                start = third * group * width + s * width
                at = (3 * layer + third) * width
                out_ref[layer, :, start : start + width] = part_ref[s, :, at : at + width].astype(
                    F32
                )


def join_weights(part, layers):
    group, shard, total = part.shape
    shape = (layers, shard, group * total // layers)
    return run(
        join_weights_kernel,
        "join_weights",
        (1,),
        [part],
        [fixed_spec(*part.shape)],
        shape_of(F32, *shape),
        fixed_spec(*shape),
        cost=(0, 12 * group * shard * total),
    )


def swap(value, bits, size):
    return lax.ppermute(value, GROUP, [(i, i ^ bits) for i in range(size)])


def gather_group(a, b, size, awaited=()):
    pair_a = swap(a, PAIR, size)
    line_b = swap(b, LINE, size)
    a, b = after([a, b], pair_a, line_b, *awaited)
    pair_b = swap(b, PAIR, size)
    line_a = swap(a, LINE, size)
    far_a = swap(pair_a, LINE, size)
    far_b = swap(line_b, PAIR, size)
    halves = [a, b, line_a, line_b, pair_a, pair_b, far_a, far_b]
    cores = [swap(half, CORE, size) for half in halves]
    return [
        half
        for k in range(0, 8, 2)
        for half in (halves[k], halves[k + 1], cores[k], cores[k + 1])
    ]


def reduce_group(shares, size, stats, soon, filler):
    far_odd, far_even = shares((7, 6), ())
    far_core = swap(far_odd, CORE, size)
    filled = filler((far_odd,))
    far = (far_even[0].astype(F32) + far_core[0].astype(F32)).astype(BF16)
    half = far.shape[0] // 2
    far_a, far_b = after([far[:half], far[half:]], filled)
    by_pair = swap(far_a, PAIR, size)
    by_line = swap(far_b, LINE, size)
    odd, even = shares((5, 3, 1, 4, 2, 0), (far_a, far_b, *soon))
    core = swap(odd, CORE, size)
    stats = [part + swap(part, CORE, size) for part in stats]
    zeros = jnp.zeros_like(by_pair)
    by_line = jnp.concatenate([zeros, by_line]).astype(F32)
    by_pair = jnp.concatenate([by_pair, zeros]).astype(F32)
    pair = (even[0].astype(F32) + core[0].astype(F32) + by_line).astype(BF16)
    line = (even[1].astype(F32) + core[1].astype(F32) + by_pair).astype(BF16)
    if stats:
        stats = after(stats, pair, line)
        stats = [
            part + sum(swap(part, bits, size) for bits in (LINE, PAIR, LINE | PAIR))
            for part in stats
        ]
    return even, core, swap(pair, PAIR, size), swap(line, LINE, size), stats


def exchange(part, size, reverse):
    far = []
    for hop in reversed(range(1, size)):
        pairs = [(i, i + hop) for i in range(size - hop)]
        if reverse:
            pairs = [(b, a) for a, b in pairs]
        far.append(lax.ppermute(part, "ring", pairs))
    return far[::-1]


def spread_small(vectors, ring, size, awaited):
    me = lax.axis_index("ring")
    width = vectors.shape[1] // ring

    def part(hop):
        start = lax.rem(me + hop, ring) * width
        return lax.dynamic_slice_in_dim(vectors, start, width, 1)

    arrived = [
        lax.ppermute(part(hop), "ring", [(i, (i + hop) % ring) for i in range(ring)])
        for hop in range(1, ring)
    ]
    vectors = part(0) + sum(arrived)
    me = lax.axis_index(GROUP)
    bit = size // 2
    while bit:
        if bit == size // 2:
            (vectors,) = after([vectors], *awaited)
        width = vectors.shape[1] // 2
        mine = (me & bit) > 0
        low, high = vectors[:, :width], vectors[:, width:]
        vectors = jnp.where(mine, high, low) + swap(jnp.where(mine, low, high), bit, size)
        bit //= 2
    return vectors


def order_matrix(rows):
    index = np.arange(rows * SUB)
    return (index % rows * SUB + index // rows)[:, None] == index[None, :]


def to_group(value):
    return lax.all_to_all(value, GROUP, split_axis=0, concat_axis=0, tiled=True)


def body(
    inputs,
    out_grad,
    reset_flags,
    weights,
    ln_gain,
    layer_norm_bias,
    reset_peep,
    forget_bias,
    reset_bias,
):
    rows_dev, span, model = inputs.shape
    layers, shard, _ = weights.shape
    ring = lax.axis_size("ring")
    half = lax.axis_size("rows")
    group = 2 * half
    place = jnp.stack([lax.axis_index("ring"), lax.axis_index("pair"), lax.axis_index("rows")])
    place = place.astype(jnp.int32)
    me = lax.axis_index(GROUP)
    width = model // group
    rows = rows_dev * half
    local = rows_dev * span
    tokens = 2 * rows * span
    order = jnp.asarray(order_matrix(rows), BF16)
    back = jnp.asarray(order_matrix(rows).T, BF16)

    mine = send_columns(place, weights, 0, group, width, reset_flags)
    got = [mine[0]] + [swap(mine[k], k, group) for k in range(1, group)]
    *normed, split = first_norm(inputs, out_grad, ln_gain, layer_norm_bias, group, (mine[0],))
    pair_mine, reset_mine, flags = stack_columns(place, got, shard, (normed[0],))
    pair_w1 = lax.all_gather(pair_mine, "ring", axis=0, tiled=True)
    reset_w1 = lax.all_gather(reset_mine, "ring", axis=0, tiled=True)
    flags = flags[:, :rows_dev, :span].reshape(2, rows, span)
    keep = (1.0 - flags.astype(F32)).transpose(0, 2, 1).reshape(tokens, 1)
    keep = jnp.broadcast_to(keep, (tokens, LANES))
    vectors = pick_vectors(
        place,
        [ln_gain, layer_norm_bias, reset_peep, forget_bias, reset_bias],
        width,
        half,
        (pair_mine,),
    )
    columns = columns_of(weights, 1, group, width, (pair_mine,))
    pieces1 = gather_group(*after(normed, pair_mine), group, (keep, vectors, columns))

    cf1, whole1, part = project(place, 0, pieces1, pair_w1, order, keep, vectors, rows, True)
    far1 = exchange(part, ring, False)
    (split,) = after([split], *pieces1)
    split = to_group(split).reshape(2, half, 2, rows_dev, span, width)
    (columns,) = after([columns], split, *far1)
    columns = to_group(columns)
    ur1 = reset_product(whole1, reset_w1, width)
    (columns,) = after([columns], ur1)
    w2 = lax.all_gather(
        columns.reshape(group * shard, 3 * width), "ring", axis=0, tiled=True
    )
    x2, stats = advance(0, cf1, ur1, split, keep, order, vectors, far1)
    stats = lax.all_gather(stats, GROUP)
    norm_stats = stats
    normed = middle_norm(1, model, x2, norm_stats, vectors, rows)

    def mixed():
        def thirds(value):
            high = value.astype(BF16)
            middle = (value - high.astype(F32)).astype(BF16)
            low = (value - high.astype(F32) - middle.astype(F32)).astype(BF16)
            return [high, middle, low]

        lines = jnp.stack(thirds(ln_gain[1]) + thirds(layer_norm_bias[1]))
        lines = jnp.pad(lines, ((0, 10), (0, 0)))
        both = jnp.dot(lines, w2, preferred_element_type=F32)
        return jnp.pad(jnp.sum(both[:6].reshape(2, 3, 3 * width), axis=1), ((0, 6), (0, 0)))

    pieces2 = gather_group(*normed, group)

    cf2, whole2, part = project(place, 1, pieces2, w2, order, keep, vectors, rows, False)
    far = exchange(part, ring, False)
    ur2 = reset_product(whole2, w2, width)
    prev2, dr2, dc2, high2, out, du_r2, part, sums2 = turn(
        1, cf2, ur2, x2, split, keep, order, back, vectors, far
    )
    far = exchange(part, ring, True)

    def scatter(term):
        return lax.psum_scatter(term, "ring", scatter_dimension=0, tiled=True)

    du_p2, forget2, stats = retreat(
        1, dc2, dr2, prev2, cf2, keep, vectors, far, rows, span, (), ur=ur2, mixed=mixed()
    )

    def slices(slots):
        return jnp.stack([me ^ k for k in slots]).astype(jnp.int32)

    terms = []

    def weigh(whole, du_p, du_r, *others):
        def work(awaited):
            term = weight_term(whole, du_p, du_r, (*awaited, *others))
            terms.append(scatter(term).reshape(group, shard, 3 * width))
            return term

        return work

    kept, core, pair, line, (stats,) = reduce_group(
        lambda slots, awaited: back_features(
            slices(slots), du_p2, du_r2, w2, awaited
        ),
        group,
        (stats,),
        (),
        weigh(whole2, du_p2, du_r2),
    )

    prev1, dr1, dc1, high1, du_r1, rows_r1, part, sums1 = middle_back(
        1, model, kept, core, pair, line, high2, x2, norm_stats, stats, cf1, ur1, split, keep,
        order, back, vectors, out, far1,
    )
    far = exchange(part, ring, True)
    high = to_group(high1.reshape(group, 2, local, width))
    du_p1, rows_p1, forget1 = retreat(
        0, dc1, dr1, prev1, cf1, keep, vectors, far, rows, span, (), back=back
    )
    kept, core, pair, line, _ = reduce_group(
        lambda slots, awaited: back_tokens(
            slices(slots), rows_p1, rows_r1, pair_w1, reset_w1, awaited
        ),
        group,
        (),
        terms[:1],
        weigh(whole1, du_p1, du_r1, high),
    )
    outputs = join(high).reshape(rows_dev, span, model)
    (both,) = after([jnp.concatenate([terms[1], terms[0]], axis=2)], pair, line, outputs)
    both = to_group(both)
    input_grad, gains1 = first_back(
        kept, core, pair, line, inputs.reshape(local, model), ln_gain, high
    )
    input_grad = input_grad.reshape(rows_dev, span, model)
    weight_grad = join_weights(both, layers)

    def total(value):
        return jnp.sum(value, axis=-2)

    sums1 = total(sums1)
    sums2 = total(sums2)
    narrow = jnp.stack(
        [
            sums1[2], total(forget1), sums1[3],
            sums1[0], sums1[1], sums2[0], total(forget2), sums2[1],
        ]
    )
    narrow = lax.dynamic_update_slice(jnp.zeros((8, model), F32), narrow, (0, me * width))
    small = jnp.concatenate([total(gains1), narrow])
    small = spread_small(small, ring, group, (both,)).reshape(2, 5, shard)
    return (outputs, input_grad, weight_grad) + tuple(small[:, i] for i in range(5))


def solution(mesh):
    ring = mesh.shape["tm"] // 2
    fine = Mesh(
        mesh.devices.reshape(ring, 2, mesh.shape["rows"]), ("ring", "pair", "rows")
    )
    tm = ("ring", "pair")
    everything = ("ring", "pair", "rows")
    return jax.shard_map(
        body,
        mesh=fine,
        in_specs=(
            P("rows", tm, None),
            P("rows", tm, None),
            P("rows", tm),
            P(None, everything, None),
            P(),
            P(),
            P(),
            P(),
            P(),
        ),
        out_specs=(
            P("rows", tm, None),
            P("rows", tm, None),
            P(None, everything, None),
            P(None, everything),
            P(None, everything),
            P(None, everything),
            P(None, everything),
            P(None, everything),
        ),
        check_vma=False,
    )
```

```python
import functools

import jax
import jax.numpy as jnp
import numpy as np
from jax import lax
from jax.experimental import pallas as pl
from jax.experimental.pallas import tpu as pltpu
from jax.sharding import Mesh
from jax.sharding import PartitionSpec as P

LANES = 128
SUBLANES = 8
STEPS = 64
SUB = 32
VMEM_BYTES = 58 * 1024 * 1024
GAIN, BIAS, PEEP, FORGET, RESET = range(5)
BF16 = jnp.bfloat16
F32 = jnp.float32
GROUP = ("pair", "rows")
CORE, LINE, PAIR = 1, 2, 4


def shape_of(dtype, *shape):
    return jax.ShapeDtypeStruct(shape, dtype)


def run(
    kernel, name, grid, ins, in_specs, outs, out_specs, scratch=(), place=None, cost=(0, 0), awaited=(),
    aliases=None,
):
    scalars = 0 if place is None else 1
    first = scalars + len(ins)
    last = first + len(awaited)

    def body(*refs):
        kernel(*refs[:first], *refs[last:])

    function = pl.pallas_call(
        body,
        out_shape=outs,
        grid_spec=pltpu.PrefetchScalarGridSpec(
            num_scalar_prefetch=scalars,
            grid=grid,
            in_specs=list(in_specs) + [pl.BlockSpec(memory_space=pl.ANY)] * len(awaited),
            out_specs=out_specs,
            scratch_shapes=list(scratch),
        ),
        compiler_params=pltpu.CompilerParams(vmem_limit_bytes=VMEM_BYTES),
        cost_estimate=pl.CostEstimate(flops=cost[0], bytes_accessed=cost[1], transcendentals=0),
        input_output_aliases=aliases or {},
        name=name,
    )
    return function(*(() if place is None else (place,)), *ins, *awaited)


def quarter(index, width):
    return pl.ds(pl.multiple_of(index * width, width), width)


def fixed_spec(*shape):
    return pl.BlockSpec(shape, lambda *_: (0,) * len(shape))


def block_spec(block, width):
    return pl.BlockSpec((block, width), lambda i, *_: (i, 0))


def turned_spec(block, width, count):
    return pl.BlockSpec((block, width), lambda i, *_: (count - 1 - i, 0))


def rows_spec(rows, width, per, place_of=lambda i: i):
    return pl.BlockSpec(
        (1, rows, STEPS, width), lambda i, *_: (place_of(i) // per, 0, place_of(i) % per, 0)
    )


def split_spec(half, rows_dev, width, per, which):
    return pl.BlockSpec(
        (1, half, 1, rows_dev, STEPS, width), lambda i, *_: (i // per, 0, which, 0, i % per, 0)
    )


def row_at(vec_ref, layer, which):
    row = layer * 5 + which
    return vec_ref[row : row + 1, :]


def chunks(total, size, body, unroll=1):
    def one(i, carry):
        body(pl.ds(pl.multiple_of(i * size, size), size))
        return carry

    lax.fori_loop(0, total // size, one, 0, unroll=unroll)


def over_time(body, state, backward=False):
    def one(i, state):
        t = STEPS - 1 - i if backward else i
        return body(pl.ds(pl.multiple_of(t * SUBLANES, SUBLANES), SUBLANES), state)

    return lax.fori_loop(0, STEPS, one, state, unroll=8)


def widen(keep, width):
    return jnp.concatenate([keep] * (width // LANES), axis=1)


def incoming(far):
    state = None
    for ref in reversed(far):
        state = ref[1] if state is None else ref[0] * state + ref[1]
    return state


def exact(order, value):
    return jnp.dot(order, value, preferred_element_type=F32)


def to_time(order_ref, rows, put):
    block = order_ref.shape[0]
    for i in range(STEPS // SUB):
        part = rows[:, i * SUB : (i + 1) * SUB, :].reshape(block, rows.shape[-1])
        put(slice(i * block, (i + 1) * block), exact(order_ref[...], part))


def to_rows(back_ref, value_ref, out_ref):
    block = back_ref.shape[0]
    for i in range(STEPS // SUB):
        part = exact(back_ref[...], value_ref[i * block : (i + 1) * block, :])
        at = slice(i * SUB, (i + 1) * SUB)
        part = part.astype(BF16)
        if len(out_ref.shape) == 4:
            out_ref[0, :, at, :] = part.reshape(out_ref.shape[1], SUB, out_ref.shape[3])
        else:
            _, half, _, rows_dev, _, width = out_ref.shape
            out_ref[0, :, 0, :, at, :] = part.reshape(half, rows_dev, SUB, width)


def forget_gate(cf_ref, here, vec_ref, layer):
    width = cf_ref.shape[1] // 2
    return jax.nn.sigmoid(cf_ref[here, width:] + row_at(vec_ref, layer, FORGET))


def fold(value):
    return jnp.sum(value.reshape(-1, SUBLANES, value.shape[-1]), axis=0)


def after(values, *awaited):
    count = len(values)

    def nothing(*refs):
        pass

    return pl.pallas_call(
        nothing,
        out_shape=[shape_of(v.dtype, *v.shape) for v in values],
        in_specs=[pl.BlockSpec(memory_space=pl.ANY)] * (count + len(awaited)),
        out_specs=[pl.BlockSpec(memory_space=pl.ANY)] * count,
        input_output_aliases={i: i for i in range(count)},
        name="after",
    )(*values, *awaited)


def columns_kernel(group, width, weights_ref, out_ref):
    for s in range(group):
        for third in range(3):
            start = third * group * width + s * width
            out_ref[s, :, third * width : (third + 1) * width] = weights_ref[
                0, :, start : start + width
            ]


def columns_of(weights, layer, group, width, awaited=()):
    _, shard, total = weights.shape
    return run(
        functools.partial(columns_kernel, group, width),
        "columns_of",
        (1,),
        [weights],
        [pl.BlockSpec((1, shard, total), lambda i, *_: (layer, 0, 0))],
        shape_of(BF16, group, shard, 3 * width),
        fixed_spec(group, shard, 3 * width),
        cost=(0, 4 * shard * total),
        awaited=awaited,
    )


def pick_vectors_kernel(place, *refs):
    out_ref = refs[-1]
    count = len(refs) - 1
    layers = refs[0].shape[0]
    out_ref[...] = jnp.zeros_like(out_ref)
    for layer in range(layers):
        for which in range(count):
            row = layer * count + which
            out_ref[row : row + 1, :] = refs[which][layer : layer + 1, :]


def pick_vectors(place, vectors, width, half, awaited):
    layers = vectors[0].shape[0]
    mine = pl.BlockSpec((layers, width), lambda i, place: (0, place[1] * half + place[2]))
    return run(
        pick_vectors_kernel,
        "pick_vectors",
        (1,),
        vectors,
        [mine] * len(vectors),
        shape_of(F32, 16, width),
        fixed_spec(16, width),
        (),
        place,
        (0, 64 * width),
        awaited,
    )


def stack_columns_kernel(place, *refs):
    pieces, (pair_ref, reset_ref, flags_ref) = refs[:-3], refs[-3:]
    group = len(pieces)
    half = group // 2
    shard = pair_ref.shape[0] // group
    both = pair_ref.shape[1]
    for k in range(group):
        at = (place[1] ^ (k // half)) * half + (place[2] ^ (k % half))
        here = pl.ds(pl.multiple_of(at * shard, shard), shard)
        pair_ref[here, :] = pieces[k][:shard, :both]
        reset_ref[here, :] = pieces[k][:shard, both:]
        flags_ref[at] = pieces[k][shard:, :LANES]


def stack_columns(place, pieces, shard, awaited):
    group = len(pieces)
    rows, total = pieces[0].shape
    outs = [
        (group * shard, total // 3 * 2),
        (group * shard, total // 3),
        (group, rows - shard, LANES),
    ]
    return run(
        stack_columns_kernel,
        "stack_columns",
        (1,),
        pieces,
        [fixed_spec(rows, total)] * group,
        [shape_of(BF16, *out) for out in outs],
        [fixed_spec(*out) for out in outs],
        (),
        place,
        (0, 4 * group * shard * total),
        awaited,
    )


def send_columns_kernel(group, width, place, weights_ref, flags_ref, *outs):
    half = group // 2
    shard = weights_ref.shape[1]
    below = flags_ref[...].astype(F32)
    fill = jnp.zeros((outs[0].shape[0] - shard - below.shape[0], below.shape[1]), F32)
    below = jnp.concatenate([below, fill]).astype(BF16)
    for k in range(group):
        at = (place[1] ^ (k // half)) * half + (place[2] ^ (k % half))
        for third in range(3):
            start = pl.multiple_of(third * group * width + at * width, width)
            outs[k][:shard, third * width : (third + 1) * width] = weights_ref[
                0, :, pl.ds(start, width)
            ]
        outs[k][shard:, :] = jnp.zeros_like(outs[k][shard:, :])
        outs[k][shard:, : flags_ref.shape[1]] = below


def send_columns(place, weights, layer, group, width, flags):
    _, shard, total = weights.shape
    rows = shard + 2 * SUBLANES
    return run(
        functools.partial(send_columns_kernel, group, width),
        "send_columns",
        (1,),
        [weights, flags],
        [pl.BlockSpec((1, shard, total), lambda i, *_: (layer, 0, 0)), fixed_spec(*flags.shape)],
        [shape_of(BF16, rows, 3 * width)] * group,
        [fixed_spec(rows, 3 * width)] * group,
        (),
        place,
        (0, 4 * shard * total),
    )


def first_norm_kernel(group, x_ref, grad_ref, gain_ref, bias_ref, *refs):
    split_ref = refs[-1]
    rows, span, model = x_ref.shape
    width = model // group
    for i in range(rows):

        def part(here):
            wide = x_ref[i, here, :].astype(F32)
            centered = wide - jnp.mean(wide, axis=-1, keepdims=True)
            scale = lax.rsqrt(jnp.mean(centered * centered, axis=-1, keepdims=True) + 1e-05)
            refs[i][here, :] = (
                centered * scale * gain_ref[0:1, :] + bias_ref[0:1, :]
            ).astype(BF16)

        chunks(span, 16, part)
        for s in range(group):
            columns = slice(s * width, (s + 1) * width)
            split_ref[s, 0, i] = x_ref[i, :, columns]
            split_ref[s, 1, i] = grad_ref[i, :, columns]


def first_norm(x, grad, gain, bias, group, awaited):
    rows, span, model = x.shape
    split = (group, 2, rows, span, model // group)
    return run(
        functools.partial(first_norm_kernel, group),
        "first_norm",
        (1,),
        [x, grad, gain, bias],
        [fixed_spec(*a.shape) for a in (x, grad, gain, bias)],
        [shape_of(BF16, span, model)] * rows + [shape_of(BF16, *split)],
        [fixed_spec(span, model)] * rows + [fixed_spec(*split)],
        cost=(20 * rows * span * model, 8 * rows * span * model),
        awaited=awaited,
    )


def project_kernel(layer, gather, slots, place, *refs):
    pieces = refs[:slots]
    w_ref, order_ref, keep_ref, vec_ref = refs[slots : slots + 4]
    cf_ref, whole_ref, tot_ref, held, forget_s = refs[slots + 4 :]
    width = cf_ref.shape[1] // 2
    step = pl.program_id(0)
    gather(place, step, pieces, order_ref, held, whole_ref)
    cf_ref[...] = jnp.dot(whole_ref[...], w_ref[...], preferred_element_type=F32)

    def gates(here):
        forget_s[here, :] = forget_gate(cf_ref, here, vec_ref, layer)

    chunks(cf_ref.shape[0], 64, gates)

    @pl.when(step == 0)
    def _():
        tot_ref[0] = jnp.ones_like(tot_ref[0])
        tot_ref[1] = jnp.zeros_like(tot_ref[1])

    def one(at, state):
        forget = forget_s[at, :]
        decay = forget * widen(keep_ref[at, :], width)
        return state[0] * decay, state[1] * decay + (1.0 - forget) * cf_ref[at, :width]

    product, state = over_time(one, (tot_ref[0], tot_ref[1]))
    tot_ref[0] = product
    tot_ref[1] = state


def gather_rows(per, group, place, step, pieces, order_ref, held, whole_ref):
    half = group // 2
    other = (step // per) ^ place[1]
    for side in range(2):

        @pl.when(other == side)
        def _():
            for k in range(half):
                for i in range(2):
                    held[place[2] ^ k, i] = pieces[2 * (side * half + k) + i][...]

    def put(here, value):
        whole_ref[here, :] = value.astype(BF16)

    to_time(order_ref, held[...].reshape(-1, STEPS, whole_ref.shape[1]), put)


def gather_features(per, group, place, step, pieces, order_ref, held, whole_ref):
    half = group // 2
    width = whole_ref.shape[1] // group
    for side in range(2):

        @pl.when(step // per == side)
        def _():
            for k in range(group):
                at = (place[1] ^ (k // half)) * half + (place[2] ^ (k % half))
                whole_ref[:, quarter(at, width)] = pieces[2 * k + side][...]


def project(place, layer, pieces, matrix, order, keep, vectors, rows, by_rows):
    model = matrix.shape[0]
    width = vectors.shape[1]
    both = 2 * width
    tokens = keep.shape[0]
    block = rows * STEPS
    count = tokens // block
    per = count // 2
    group = model // width
    half = group // 2
    specs = []
    for k in range(group):
        for side in range(2):
            if by_rows:

                def index(i, place, needed=k // half):
                    mine = ((i // per) ^ place[1]) == needed
                    return (jnp.where(mine, i % per, 0), 0)

                specs.append(pl.BlockSpec((STEPS, model), index))
            elif side == 0:
                specs.append(
                    pl.BlockSpec((block, width), lambda i, place: (jnp.minimum(i, per - 1), 0))
                )
            else:
                specs.append(
                    pl.BlockSpec((block, width), lambda i, place: (jnp.maximum(i - per, 0), 0))
                )
    gather = functools.partial(gather_rows if by_rows else gather_features, per, group)
    held = pltpu.VMEM((half, 2, STEPS, model) if by_rows else (2 * SUBLANES, LANES), BF16)
    return run(
        functools.partial(project_kernel, layer, gather, len(pieces)),
        "project",
        (count,),
        [*pieces, matrix, order, keep, vectors],
        specs
        + [
            fixed_spec(model, both),
            fixed_spec(*order.shape),
            block_spec(block, LANES),
            fixed_spec(*vectors.shape),
        ],
        [
            shape_of(F32, tokens, both),
            shape_of(BF16, tokens, model),
            shape_of(F32, 2, rows, width),
        ],
        [block_spec(block, both), block_spec(block, model), fixed_spec(2, rows, width)],
        [held, pltpu.VMEM((block, width), F32)],
        place,
        (2 * tokens * model * both, 4 * tokens * model + 4 * tokens * both + 2 * model * both),
    )


def reset_kernel(x_ref, w_ref, out_ref):
    out_ref[...] = jnp.dot(x_ref[...], w_ref[...], preferred_element_type=F32)


def reset_product(whole, matrix, width):
    tokens, model = whole.shape
    last = matrix.shape[1] // width - 1
    block = tokens // 4
    return run(
        reset_kernel,
        "reset_product",
        (4,),
        [whole, matrix],
        [block_spec(block, model), pl.BlockSpec((model, width), lambda *_: (0, last))],
        shape_of(F32, tokens, width),
        block_spec(block, width),
        cost=(2 * tokens * model * width, 2 * tokens * model + 4 * tokens * width),
    )


def carry_forward(layer, cf_ref, keep_ref, vec_ref, far, carry_s, forget_s, prev_ref, state_s):
    width = prev_ref.shape[1]

    def gates(here):
        forget_s[here, :] = forget_gate(cf_ref, here, vec_ref, layer)

    chunks(forget_s.shape[0], 64, gates)

    @pl.when(pl.program_id(0) == 0)
    def _():
        first = incoming(far)
        carry_s[...] = jnp.zeros_like(carry_s) if first is None else first

    def one(at, state):
        forget = forget_s[at, :]
        prev = widen(keep_ref[at, :], width) * state
        new = forget * prev + (1.0 - forget) * cf_ref[at, :width]
        prev_ref[at, :] = prev
        state_s[at, :] = new
        return new

    carry_s[...] = over_time(one, carry_s[...])


def reset_gate(layer, ur_ref, prev_ref, here, vec_ref):
    return jax.nn.sigmoid(
        ur_ref[here, :]
        + row_at(vec_ref, layer, PEEP) * prev_ref[here, :]
        + row_at(vec_ref, layer, RESET)
    )


def advance_kernel(layer, cf_ref, ur_ref, x_ref, keep_ref, order_ref, vec_ref, *refs):
    xn_ref, stat_ref, carry_s, forget_s, prev_s, state_s, x_s = refs[-7:]
    far = refs[:-7]
    block, width = xn_ref.shape

    def put(here, value):
        x_s[here, :] = value

    to_time(order_ref, x_ref[...].reshape(-1, STEPS, width), put)
    carry_forward(layer, cf_ref, keep_ref, vec_ref, far, carry_s, forget_s, prev_s, state_s)

    def finish(here):
        gate = reset_gate(layer, ur_ref, prev_s, here, vec_ref)
        xn = gate * state_s[here, :] + (1.0 - gate) * x_s[here, :]
        xn_ref[here, :] = xn
        mean = jnp.mean(xn, axis=-1, keepdims=True)
        off = xn - mean
        spread = sum(off[:, j : j + LANES] * off[:, j : j + LANES] for j in range(0, width, LANES))
        x_s[here, :LANES] = jnp.broadcast_to(mean, (here.size, LANES))
        state_s[here, :LANES] = spread

    chunks(block, 64, finish)
    for b in range(block // LANES):
        here = slice(b * LANES, (b + 1) * LANES)
        row = pl.ds(pl.program_id(0) * (block // LANES) + b, 1)
        stat_ref[0, row, :] = x_s[here, :LANES].T[0:1, :]
        stat_ref[1, row, :] = jnp.sum(state_s[here, :LANES].T, axis=0, keepdims=True)


def advance(layer, cf, ur, x, keep, order, vectors, far):
    tokens, width = ur.shape
    _, half, _, rows_dev, span, _ = x.shape
    rows = half * rows_dev
    block = rows * STEPS
    part = block_spec(block, width)
    return run(
        functools.partial(advance_kernel, layer),
        "advance",
        (tokens // block,),
        [cf, ur, x, keep, order, vectors, *far],
        [
            block_spec(block, 2 * width),
            part,
            split_spec(half, rows_dev, width, span // STEPS, 0),
            block_spec(block, LANES),
            fixed_spec(*order.shape),
            fixed_spec(*vectors.shape),
        ]
        + [fixed_spec(2, rows, width)] * len(far),
        [shape_of(F32, tokens, width), shape_of(F32, 2, tokens // LANES, LANES)],
        [part, fixed_spec(2, tokens // LANES, LANES)],
        [pltpu.VMEM((rows, width), F32)] + [pltpu.VMEM((block, width), F32)] * 4,
        None,
        (60 * tokens * width, 22 * tokens * width),
    )


def norm_columns(stat_ref, block, width, model, mean_s, scale_s):
    group = stat_ref.shape[0]
    for b in range(block // LANES):
        row = pl.ds(pl.program_id(0) * (block // LANES) + b, 1)
        here = slice(b * LANES, (b + 1) * LANES)
        means = [stat_ref[s, 0, row, :] for s in range(group)]
        mean = sum(means) / group
        square = sum(stat_ref[s, 1, row, :] for s in range(group))
        between = sum((part - mean) * (part - mean) for part in means)
        scale = lax.rsqrt((square + between * width) / model + 1e-05)
        mean_s[here, :] = jnp.broadcast_to(mean, (LANES, LANES)).T
        scale_s[here, :] = jnp.broadcast_to(scale, (LANES, LANES)).T


def middle_norm_kernel(layer, model, xn_ref, stat_ref, vec_ref, a_ref, b_ref, mean_s, scale_s):
    block, width = xn_ref.shape
    norm_columns(stat_ref, block, width, model, mean_s, scale_s)
    per = pl.num_programs(0) // 2
    for side, normed_ref in enumerate((a_ref, b_ref)):

        @pl.when(pl.program_id(0) // per == side)
        def _():
            def part(here):
                normed_ref[here, :] = (
                    (xn_ref[here, :] - widen(mean_s[here, :], width))
                    * widen(scale_s[here, :], width)
                    * row_at(vec_ref, layer, GAIN)
                    + row_at(vec_ref, layer, BIAS)
                ).astype(BF16)

            chunks(block, 64, part)


def middle_norm(layer, model, xn, stats, vectors, rows):
    tokens, width = xn.shape
    block = rows * STEPS
    per = tokens // block // 2
    return run(
        functools.partial(middle_norm_kernel, layer, model),
        "middle_norm",
        (tokens // block,),
        [xn, stats, vectors],
        [block_spec(block, width), fixed_spec(*stats.shape), fixed_spec(*vectors.shape)],
        [shape_of(BF16, tokens // 2, width)] * 2,
        [
            pl.BlockSpec((block, width), lambda i, *_: (jnp.minimum(i, per - 1), 0)),
            pl.BlockSpec((block, width), lambda i, *_: (jnp.maximum(i - per, 0), 0)),
        ],
        [pltpu.VMEM((block, LANES), F32)] * 2,
        cost=(10 * tokens * width, 8 * tokens * width),
    )


def add_total(decay_s, drive_s, tot_ref):
    @pl.when(pl.program_id(0) == 0)
    def _():
        tot_ref[0] = jnp.ones_like(tot_ref[0])
        tot_ref[1] = jnp.zeros_like(tot_ref[1])

    def one(at, state):
        return state[0] * decay_s[at, :], state[1] + state[0] * drive_s[at, :]

    product, total = over_time(one, (tot_ref[0], tot_ref[1]))
    tot_ref[0] = product
    tot_ref[1] = total


def turn_kernel(layer, cf_ref, ur_ref, x_ref, dh_ref, keep_ref, order_ref, back_ref, vec_ref, *refs):
    prev_ref, dr_ref, dc_ref, high_ref, out_ref, du_ref, tot_ref, small_ref = refs[-14:-6]
    carry_s, forget_s, state_s, dh_s, drive_s, out_s = refs[-6:]
    far = refs[:-14]
    block, width = prev_ref.shape

    def put(here, value):
        dh_s[here, :] = value

    to_time(order_ref, dh_ref[...].reshape(-1, STEPS, width), put)
    carry_forward(layer, cf_ref, keep_ref, vec_ref, far, carry_s, forget_s, prev_ref, state_s)

    @pl.when(pl.program_id(0) == 0)
    def _():
        small_ref[...] = jnp.zeros_like(small_ref)

    def finish(here):
        state = state_s[here, :]
        x = x_ref[here, :]
        dh = dh_s[here, :]
        prev = prev_ref[here, :]
        gate = reset_gate(layer, ur_ref, prev_ref, here, vec_ref)
        out_s[here, :] = (gate * state + (1.0 - gate) * x).astype(BF16)
        dr = dh * (state - x) * gate * (1.0 - gate)
        dc = dh * gate
        dr_ref[here, :] = dr
        dc_ref[here, :] = dc
        du_ref[here, :] = dr.astype(BF16)
        high_ref[here, :] = dh - dc
        keep = widen(keep_ref[here, :], width)
        decay = keep * forget_s[here, :]
        state_s[here, :] = decay
        drive_s[here, :] = keep * row_at(vec_ref, layer, PEEP) * dr + decay * dc
        small_ref[0] += fold(dr * prev)
        small_ref[1] += fold(dr)

    chunks(block, 32, finish)
    to_rows(back_ref, out_s, out_ref)
    add_total(state_s, drive_s, tot_ref)


def turn(layer, cf, ur, x, dh, keep, order, back, vectors, far):
    tokens, width = ur.shape
    _, half, _, rows_dev, span, _ = dh.shape
    rows = half * rows_dev
    block = rows * STEPS
    part = block_spec(block, width)
    by_rows = split_spec(half, rows_dev, width, span // STEPS, 0)
    return run(
        functools.partial(turn_kernel, layer),
        "turn",
        (tokens // block,),
        [cf, ur, x, dh, keep, order, back, vectors, *far],
        [
            block_spec(block, 2 * width),
            part,
            part,
            split_spec(half, rows_dev, width, span // STEPS, 1),
            block_spec(block, LANES),
            fixed_spec(*order.shape),
            fixed_spec(*back.shape),
            fixed_spec(*vectors.shape),
        ]
        + [fixed_spec(2, rows, width)] * len(far),
        [shape_of(F32, tokens, width)] * 4
        + [
            shape_of(BF16, *dh.shape),
            shape_of(BF16, tokens, width),
            shape_of(F32, 2, rows, width),
            shape_of(F32, 2, SUBLANES, width),
        ],
        [part] * 4
        + [by_rows, part, fixed_spec(2, rows, width), fixed_spec(2, SUBLANES, width)],
        [pltpu.VMEM((rows, width), F32)]
        + [pltpu.VMEM((block, width), F32)] * 4
        + [pltpu.VMEM((block, width), BF16)],
        None,
        (80 * tokens * width, 36 * tokens * width),
    )


def retreat_kernel(layer, sums, dc_ref, dr_ref, prev_ref, cf_ref, keep_ref, vec_ref, *refs):
    if sums:
        ur_ref, mixed_ref = refs[:2]
        du_ref, small_ref, stat_ref, carry_s, forget_s, total_s, sum_s, cross_s = refs[-8:]
        far = refs[2:-8]
    else:
        back_ref = refs[0]
        du_ref, rows_ref, small_ref, carry_s, forget_s, total_s = refs[-6:]
        far = refs[1:-6]
    block, width = prev_ref.shape
    peep = row_at(vec_ref, layer, PEEP)

    @pl.when(pl.program_id(0) == 0)
    def _():
        first = incoming(far)
        carry_s[...] = jnp.zeros_like(carry_s) if first is None else first
        small_ref[...] = jnp.zeros_like(small_ref)

    def gates(here):
        forget_s[here, :] = forget_gate(cf_ref, here, vec_ref, layer)

    chunks(block, 64, gates)

    def one(at, state):
        total = dc_ref[at, :] + state
        total_s[at, :] = total
        return widen(keep_ref[at, :], width) * (peep * dr_ref[at, :] + forget_s[at, :] * total)

    carry_s[...] = over_time(one, carry_s[...], True)

    def halves(value):
        return sum(value[:, j : j + LANES] for j in range(0, width, LANES))

    def finish(here):
        forget = forget_s[here, :]
        slow = total_s[here, :] * (1.0 - forget)
        d_forget = slow * forget * (prev_ref[here, :] - cf_ref[here, :width])
        d_cand = slow.astype(BF16)
        d_gate = d_forget.astype(BF16)
        du_ref[here, :width] = d_cand
        du_ref[here, width:] = d_gate
        small_ref[...] += fold(d_forget)
        if sums:
            parts = [d_cand, d_gate, dr_ref[here, :].astype(BF16)]
            inputs = [cf_ref[here, :width], cf_ref[here, width:], ur_ref[here, :]]
            plain = cross = 0.0
            for third in range(3):
                at = slice(third * width, (third + 1) * width)
                du = parts[third].astype(F32)
                plain = plain + du * mixed_ref[0:1, at]
                cross = cross + du * (inputs[third] - mixed_ref[1:2, at])
            sum_s[here, :] = halves(plain)
            cross_s[here, :] = halves(cross)

    chunks(block, 32, finish)
    if sums:
        base = (pl.num_programs(0) - 1 - pl.program_id(0)) * (block // LANES)
        for b in range(block // LANES):
            here = slice(b * LANES, (b + 1) * LANES)
            stat_ref[0, pl.ds(base + b, 1), :] = jnp.sum(sum_s[here, :].T, axis=0, keepdims=True)
            stat_ref[1, pl.ds(base + b, 1), :] = jnp.sum(cross_s[here, :].T, axis=0, keepdims=True)
    else:
        to_rows(back_ref, du_ref, rows_ref)


def retreat(layer, dc, dr, prev, cf, keep, vectors, far, rows, span, awaited, back=None, ur=None, mixed=None):
    tokens, width = dc.shape
    block = rows * STEPS
    count = tokens // block
    sums = back is None
    part = turned_spec(block, width, count)
    both = turned_spec(block, 2 * width, count)
    rows_out = rows_spec(rows, 2 * width, span // STEPS, lambda i: count - 1 - i)
    outs = [shape_of(BF16, tokens, 2 * width)]
    specs = [both]
    scratch = [pltpu.VMEM((rows, width), F32)] + [pltpu.VMEM((block, width), F32)] * 2
    if sums:
        more, more_specs = [ur, mixed], [part, fixed_spec(*mixed.shape)]
        outs += [shape_of(F32, SUBLANES, width), shape_of(F32, 2, tokens // LANES, LANES)]
        specs += [fixed_spec(SUBLANES, width), fixed_spec(2, tokens // LANES, LANES)]
        scratch += [pltpu.VMEM((block, LANES), F32)] * 2
    else:
        more, more_specs = [back], [fixed_spec(*back.shape)]
        outs += [shape_of(BF16, 2, rows, span, 2 * width), shape_of(F32, SUBLANES, width)]
        specs += [rows_out, fixed_spec(SUBLANES, width)]
    return run(
        functools.partial(retreat_kernel, layer, sums),
        "retreat",
        (count,),
        [dc, dr, prev, cf, keep, vectors, *more, *far],
        [part] * 3
        + [both, turned_spec(block, LANES, count), fixed_spec(*vectors.shape)]
        + more_specs
        + [fixed_spec(2, rows, width)] * len(far),
        outs,
        specs,
        scratch,
        None,
        (60 * tokens * width, 30 * tokens * width),
        awaited,
    )


def back_product(pair, reset, w_pair, w_reset):
    contract = (((1,), (1,)), ((), ()))
    return lax.dot_general(pair, w_pair, contract, preferred_element_type=F32) + lax.dot_general(
        reset, w_reset, contract, preferred_element_type=F32
    )


def put_shares(share_of, outs):
    odd, even = outs
    for k in range(odd.shape[0]):
        odd[k] = share_of(k).astype(BF16)
        even[k] = share_of(odd.shape[0] + k).astype(BF16)


def share_outs(count, rows, columns):
    return [shape_of(BF16, count // 2, rows, columns)] * 2


def back_features_kernel(count, order, pair_ref, reset_ref, *refs):
    def share_of(k):
        return back_product(
            pair_ref[...], reset_ref[...], refs[2 * k][...], refs[2 * k + 1][...]
        )

    put_shares(share_of, refs[-2:])


def back_features(order, pair, reset, matrix, awaited):
    tokens, width = reset.shape
    count = order.shape[0]
    block = tokens // 4
    specs = []
    for k in range(count):
        specs.append(pl.BlockSpec((width, 2 * width), lambda i, order, k=k: (order[k], 0)))
        specs.append(pl.BlockSpec((width, width), lambda i, order, k=k: (order[k], 2)))
    outs = share_outs(count, tokens, width)
    return run(
        functools.partial(back_features_kernel, count),
        "back_features",
        (4,),
        [pair, reset] + [matrix, matrix] * count,
        [block_spec(block, 2 * width), block_spec(block, width)] + specs,
        outs,
        [pl.BlockSpec((out.shape[0], block, width), lambda i, order: (0, i, 0)) for out in outs],
        (),
        order,
        (6 * count * tokens * width * width, 8 * count * tokens * width),
        awaited,
    )


def back_tokens_kernel(count, order, wp_ref, wr_ref, *refs):
    local = refs[-1].shape[1]

    def share_of(k):
        pair, reset = refs[2 * k : 2 * k + 2]
        return back_product(
            pair[0].reshape(local, pair.shape[-1]),
            reset[0].reshape(local, reset.shape[-1]),
            wp_ref[...],
            wr_ref[...],
        )

    put_shares(share_of, refs[-2:])


def back_tokens(order, pair, reset, w_pair, w_reset, awaited):
    two, rows, span, width = reset.shape
    model = w_pair.shape[0]
    count = order.shape[0]
    half = model // width // 2
    rows_dev = rows // half
    local = rows_dev * span
    block = model // 4
    specs = []
    for k in range(count):
        by_order = lambda i, order, k=k: (order[k] // half, order[k] % half, 0, 0)
        for columns in (2 * width, width):
            specs.append(pl.BlockSpec((1, rows_dev, span, columns), by_order))
    outs = share_outs(count, local, model)
    return run(
        functools.partial(back_tokens_kernel, count),
        "back_tokens",
        (4,),
        [w_pair, w_reset] + [pair, reset] * count,
        [block_spec(block, 2 * width), block_spec(block, width)] + specs,
        outs,
        [pl.BlockSpec((out.shape[0], local, block), lambda i, order: (0, 0, i)) for out in outs],
        (),
        order,
        (6 * count * local * model * width, 8 * count * local * model),
        awaited,
    )


def middle_back_kernel(layer, model, *refs):
    (
        kept_ref, core_ref, pair_ref, line_ref, high_ref, x_ref, norm_ref, stat_ref,
        cf_ref, ur_ref, below_x_ref, keep_ref, order_ref, back_ref, vec_ref, _,
    ) = refs[:16]
    (
        prev_ref, dr_ref, dc_ref, below_ref, du_ref, rows_ref, tot_ref, small_ref,
        carry_s, forget_s, state_s, drive_s, x_s, plain_s, cross_s, mean_s, scale_s, below_s,
    ) = refs[-18:]
    far = refs[16:-18]
    block, width = prev_ref.shape
    below = layer - 1

    def put(here, value):
        x_s[here, :] = value

    to_time(order_ref, below_x_ref[...].reshape(-1, STEPS, width), put)
    carry_forward(below, cf_ref, keep_ref, vec_ref, far, carry_s, forget_s, prev_ref, state_s)
    for b in range(block // LANES):
        row = pl.ds(pl.program_id(0) * (block // LANES) + b, 1)
        here = slice(b * LANES, (b + 1) * LANES)
        for s, out in enumerate((plain_s, cross_s)):
            out[here, :] = jnp.broadcast_to(stat_ref[s, row, :] / model, (LANES, LANES)).T
    norm_columns(norm_ref, block, width, model, mean_s, scale_s)

    @pl.when(pl.program_id(0) == 0)
    def _():
        small_ref[...] = jnp.zeros_like(small_ref)

    def finish(here):
        back = (
            kept_ref[0, here, :].astype(F32)
            + core_ref[0, here, :].astype(F32)
            + pair_ref[here, :].astype(F32)
            + line_ref[here, :].astype(F32)
        )
        scale = widen(scale_s[here, :], width)
        xhat = (x_ref[here, :] - widen(mean_s[here, :], width)) * scale
        dh = high_ref[here, :] + scale * (
            back * row_at(vec_ref, layer, GAIN)
            - widen(plain_s[here, :], width)
            - xhat * widen(cross_s[here, :], width)
        )
        small_ref[0] += fold(back * xhat)
        small_ref[1] += fold(back)
        gate = reset_gate(below, ur_ref, prev_ref, here, vec_ref)
        dr = dh * (state_s[here, :] - x_s[here, :]) * gate * (1.0 - gate)
        dc = dh * gate
        dr_ref[here, :] = dr
        dc_ref[here, :] = dc
        du_ref[here, :] = dr.astype(BF16)
        below_s[here, :] = (dh - dc).astype(BF16)
        keep = widen(keep_ref[here, :], width)
        decay = keep * forget_s[here, :]
        state_s[here, :] = decay
        drive_s[here, :] = keep * row_at(vec_ref, below, PEEP) * dr + decay * dc
        small_ref[2] += fold(dr * prev_ref[here, :])
        small_ref[3] += fold(dr)

    chunks(block, 32, finish)
    to_rows(back_ref, below_s, below_ref)
    to_rows(back_ref, du_ref, rows_ref)
    add_total(state_s, drive_s, tot_ref)


def middle_back(
    layer, model, kept, core, pair, line, high, x, norm, stats, cf, ur, below_x, keep, order,
    back, vectors, out, far,
):
    tokens, width = ur.shape
    _, half, _, rows_dev, span, _ = below_x.shape
    rows = half * rows_dev
    block = rows * STEPS
    part = block_spec(block, width)
    last = kept.shape[0] - 1
    top = pl.BlockSpec((1, block, width), lambda i, *_: (last, i, 0))
    thin = block_spec(block, LANES)
    by_rows = rows_spec(rows, width, span // STEPS)
    held = pltpu.VMEM((block, width), F32)
    return run(
        functools.partial(middle_back_kernel, layer, model),
        "middle_back",
        (tokens // block,),
        [
            kept, core, pair, line, high, x, norm, stats, cf, ur, below_x, keep, order, back,
            vectors, out, *far,
        ],
        [top, top, part, part, part, part, fixed_spec(*norm.shape), fixed_spec(*stats.shape)]
        + [
            block_spec(block, 2 * width),
            part,
            split_spec(half, rows_dev, width, span // STEPS, 0),
            thin,
            fixed_spec(*order.shape),
            fixed_spec(*back.shape),
            fixed_spec(*vectors.shape),
            pl.BlockSpec(memory_space=pl.ANY),
        ]
        + [fixed_spec(2, rows, width)] * len(far),
        [shape_of(F32, tokens, width)] * 3
        + [
            shape_of(BF16, *out.shape),
            shape_of(BF16, tokens, width),
            shape_of(BF16, 2, rows, span, width),
            shape_of(F32, 2, rows, width),
            shape_of(F32, 4, SUBLANES, width),
        ],
        [part, part, part, split_spec(half, rows_dev, width, span // STEPS, 1), part, by_rows]
        + [fixed_spec(2, rows, width), fixed_spec(4, SUBLANES, width)],
        [pltpu.VMEM((rows, width), F32)]
        + [held] * 4
        + [pltpu.VMEM((block, LANES), F32)] * 4
        + [pltpu.VMEM((block, width), BF16)],
        None,
        (80 * tokens * width, 44 * tokens * width),
        (),
        {15: 3},
    )


def first_back_kernel(kept_ref, core_ref, pair_ref, line_ref, x_ref, gain_ref, high_ref, out_ref, small_ref):
    local, model = x_ref.shape
    group, _, _, width = high_ref.shape

    @pl.when(pl.program_id(0) == 0)
    def _():
        small_ref[...] = jnp.zeros_like(small_ref)

    def part(here):
        wide = x_ref[here, :].astype(F32)
        centered = wide - jnp.mean(wide, axis=-1, keepdims=True)
        scale = lax.rsqrt(jnp.mean(centered * centered, axis=-1, keepdims=True) + 1e-05)
        xhat = centered * scale
        back = (
            kept_ref[0, here, :].astype(F32)
            + core_ref[0, here, :].astype(F32)
            + pair_ref[here, :].astype(F32)
            + line_ref[here, :].astype(F32)
        )
        scaled = back * gain_ref[0:1, :]
        small_ref[0] += fold(back * xhat)
        small_ref[1] += fold(back)
        total = scale * (
            scaled
            - jnp.mean(scaled, axis=-1, keepdims=True)
            - xhat * jnp.mean(scaled * xhat, axis=-1, keepdims=True)
        )
        for s in range(group):
            columns = slice(s * width, (s + 1) * width)
            out_ref[here, columns] = (
                total[:, columns] + high_ref[s, 0, here, :].astype(F32)
            ).astype(BF16)

    chunks(local, 16, part)


def first_back(kept, core, pair, line, x, gain, high):
    local, model = x.shape
    group, _, _, width = high.shape
    last = kept.shape[0] - 1
    block = local // 4
    top = pl.BlockSpec((1, block, model), lambda i, *_: (last, i, 0))
    flat = block_spec(block, model)
    return run(
        first_back_kernel,
        "first_back",
        (4,),
        [kept, core, pair, line, x, gain, high],
        [top, top, flat, flat, flat, fixed_spec(*gain.shape)]
        + [pl.BlockSpec((group, 1, block, width), lambda i, *_: (0, 1, i, 0))],
        [shape_of(BF16, local, model), shape_of(F32, 2, SUBLANES, model)],
        [flat, fixed_spec(2, SUBLANES, model)],
        cost=(30 * local * model, 16 * local * model),
    )


def weight_kernel(whole_ref, pair_ref, reset_ref, out_ref):
    both = pair_ref.shape[1]
    contract = (((0,), (0,)), ((), ()))
    for du_ref, at in ((pair_ref, slice(0, both)), (reset_ref, slice(both, out_ref.shape[1]))):
        out_ref[:, at] = lax.dot_general(
            whole_ref[...], du_ref[...], contract, preferred_element_type=F32
        ).astype(BF16)


def weight_term(whole, pair, reset, awaited=()):
    tokens, model = whole.shape
    width = reset.shape[1]
    block = model // 4
    return run(
        weight_kernel,
        "weight_term",
        (4,),
        [whole, pair, reset],
        [
            pl.BlockSpec((tokens, block), lambda k, *_: (0, k)),
            fixed_spec(*pair.shape),
            fixed_spec(*reset.shape),
        ],
        shape_of(BF16, model, 3 * width),
        block_spec(block, 3 * width),
        cost=(6 * tokens * model * width, 2 * tokens * model + 6 * model * width),
        awaited=awaited,
    )


def join_kernel(x_ref, out_ref):
    group, _, rows, width = x_ref.shape
    for s in range(group):
        out_ref[:, s * width : (s + 1) * width] = x_ref[s, 0]


def join(value):
    group, _, rows, width = value.shape
    return run(
        join_kernel,
        "join",
        (1,),
        [value],
        [fixed_spec(group, 1, rows, width)],
        shape_of(value.dtype, rows, group * width),
        fixed_spec(rows, group * width),
        cost=(0, 4 * rows * group * width),
    )


def join_weights_kernel(part_ref, out_ref):
    layers, _, total = out_ref.shape
    group = part_ref.shape[0]
    width = total // group // 3
    for layer in range(layers):
        for s in range(group):
            for third in range(3):
                start = third * group * width + s * width
                at = (3 * layer + third) * width
                out_ref[layer, :, start : start + width] = part_ref[s, :, at : at + width].astype(
                    F32
                )


def join_weights(part, layers):
    group, shard, total = part.shape
    shape = (layers, shard, group * total // layers)
    return run(
        join_weights_kernel,
        "join_weights",
        (1,),
        [part],
        [fixed_spec(*part.shape)],
        shape_of(F32, *shape),
        fixed_spec(*shape),
        cost=(0, 12 * group * shard * total),
    )


def swap(value, bits, size):
    return lax.ppermute(value, GROUP, [(i, i ^ bits) for i in range(size)])


def gather_group(a, b, size, awaited=()):
    pair_a = swap(a, PAIR, size)
    line_b = swap(b, LINE, size)
    a, b = after([a, b], pair_a, line_b, *awaited)
    pair_b = swap(b, PAIR, size)
    line_a = swap(a, LINE, size)
    far_a = swap(pair_a, LINE, size)
    far_b = swap(line_b, PAIR, size)
    halves = [a, b, line_a, line_b, pair_a, pair_b, far_a, far_b]
    cores = [swap(half, CORE, size) for half in halves]
    return [
        half
        for k in range(0, 8, 2)
        for half in (halves[k], halves[k + 1], cores[k], cores[k + 1])
    ]


def reduce_group(shares, size, stats, soon, filler):
    far_odd, far_even = shares((7, 6), ())
    far_core = swap(far_odd, CORE, size)
    filled = filler((far_odd,))
    far = (far_even[0].astype(F32) + far_core[0].astype(F32)).astype(BF16)
    half = far.shape[0] // 2
    far_a, far_b = after([far[:half], far[half:]], filled)
    by_pair = swap(far_a, PAIR, size)
    by_line = swap(far_b, LINE, size)
    odd, even = shares((5, 3, 1, 4, 2, 0), (far_a, far_b, *soon))
    core = swap(odd, CORE, size)
    stats = [part + swap(part, CORE, size) for part in stats]
    zeros = jnp.zeros_like(by_pair)
    by_line = jnp.concatenate([zeros, by_line]).astype(F32)
    by_pair = jnp.concatenate([by_pair, zeros]).astype(F32)
    pair = (even[0].astype(F32) + core[0].astype(F32) + by_line).astype(BF16)
    line = (even[1].astype(F32) + core[1].astype(F32) + by_pair).astype(BF16)
    if stats:
        stats = after(stats, pair, line)
        stats = [
            part + sum(swap(part, bits, size) for bits in (LINE, PAIR, LINE | PAIR))
            for part in stats
        ]
    return even, core, swap(pair, PAIR, size), swap(line, LINE, size), stats


def exchange(part, size, reverse):
    far = []
    for hop in reversed(range(1, size)):
        pairs = [(i, i + hop) for i in range(size - hop)]
        if reverse:
            pairs = [(b, a) for a, b in pairs]
        far.append(lax.ppermute(part, "ring", pairs))
    return far[::-1]


def spread_small(vectors, ring, size, awaited):
    me = lax.axis_index("ring")
    width = vectors.shape[1] // ring

    def part(hop):
        start = lax.rem(me + hop, ring) * width
        return lax.dynamic_slice_in_dim(vectors, start, width, 1)

    arrived = [
        lax.ppermute(part(hop), "ring", [(i, (i + hop) % ring) for i in range(ring)])
        for hop in range(1, ring)
    ]
    vectors = part(0) + sum(arrived)
    (vectors,) = after([vectors], *awaited)
    width = vectors.shape[1] // 2
    mine = lax.axis_index("pair") > 0
    low, high = vectors[:, :width], vectors[:, width:]
    half = size // 2
    vectors = jnp.where(mine, high, low) + swap(jnp.where(mine, low, high), half, size)
    me = lax.axis_index("rows")
    width = width // half

    def slice_of(k):
        return lax.dynamic_slice_in_dim(vectors, (me ^ k) * width, width, 1)

    return slice_of(0) + sum(swap(slice_of(k), k, size) for k in range(1, half))


def order_matrix(rows):
    index = np.arange(rows * SUB)
    return (index % rows * SUB + index // rows)[:, None] == index[None, :]


def to_group(value):
    return lax.all_to_all(value, GROUP, split_axis=0, concat_axis=0, tiled=True)


def body(
    inputs,
    out_grad,
    reset_flags,
    weights,
    ln_gain,
    layer_norm_bias,
    reset_peep,
    forget_bias,
    reset_bias,
):
    rows_dev, span, model = inputs.shape
    layers, shard, _ = weights.shape
    ring = lax.axis_size("ring")
    half = lax.axis_size("rows")
    group = 2 * half
    place = jnp.stack([lax.axis_index("ring"), lax.axis_index("pair"), lax.axis_index("rows")])
    place = place.astype(jnp.int32)
    me = lax.axis_index(GROUP)
    width = model // group
    rows = rows_dev * half
    local = rows_dev * span
    tokens = 2 * rows * span
    order = jnp.asarray(order_matrix(rows), BF16)
    back = jnp.asarray(order_matrix(rows).T, BF16)

    mine = send_columns(place, weights, 0, group, width, reset_flags)
    got = [mine[0]] + [swap(mine[k], k, group) for k in range(1, group)]
    *normed, split = first_norm(inputs, out_grad, ln_gain, layer_norm_bias, group, (mine[0],))
    pair_mine, reset_mine, flags = stack_columns(place, got, shard, (normed[0],))
    pair_w1 = lax.all_gather(pair_mine, "ring", axis=0, tiled=True)
    reset_w1 = lax.all_gather(reset_mine, "ring", axis=0, tiled=True)
    flags = flags[:, :rows_dev, :span].reshape(2, rows, span)
    keep = (1.0 - flags.astype(F32)).transpose(0, 2, 1).reshape(tokens, 1)
    keep = jnp.broadcast_to(keep, (tokens, LANES))
    vectors = pick_vectors(
        place,
        [ln_gain, layer_norm_bias, reset_peep, forget_bias, reset_bias],
        width,
        half,
        (pair_mine,),
    )
    columns = columns_of(weights, 1, group, width, (pair_mine,))
    pieces1 = gather_group(*after(normed, pair_mine), group, (keep, vectors, columns))

    cf1, whole1, part = project(place, 0, pieces1, pair_w1, order, keep, vectors, rows, True)
    far1 = exchange(part, ring, False)
    (split,) = after([split], *pieces1)
    split = to_group(split).reshape(2, half, 2, rows_dev, span, width)
    (columns,) = after([columns], split, *far1)
    columns = to_group(columns)
    ur1 = reset_product(whole1, reset_w1, width)
    (columns,) = after([columns], ur1)
    w2 = lax.all_gather(
        columns.reshape(group * shard, 3 * width), "ring", axis=0, tiled=True
    )
    x2, stats = advance(0, cf1, ur1, split, keep, order, vectors, far1)
    stats = lax.all_gather(stats, GROUP)
    norm_stats = stats
    normed = middle_norm(1, model, x2, norm_stats, vectors, rows)

    def mixed():
        def thirds(value):
            high = value.astype(BF16)
            middle = (value - high.astype(F32)).astype(BF16)
            low = (value - high.astype(F32) - middle.astype(F32)).astype(BF16)
            return [high, middle, low]

        lines = jnp.stack(thirds(ln_gain[1]) + thirds(layer_norm_bias[1]))
        lines = jnp.pad(lines, ((0, 10), (0, 0)))
        both = jnp.dot(lines, w2, preferred_element_type=F32)
        return jnp.pad(jnp.sum(both[:6].reshape(2, 3, 3 * width), axis=1), ((0, 6), (0, 0)))

    pieces2 = gather_group(*normed, group)

    cf2, whole2, part = project(place, 1, pieces2, w2, order, keep, vectors, rows, False)
    far = exchange(part, ring, False)
    ur2 = reset_product(whole2, w2, width)
    prev2, dr2, dc2, high2, out, du_r2, part, sums2 = turn(
        1, cf2, ur2, x2, split, keep, order, back, vectors, far
    )
    far = exchange(part, ring, True)

    def scatter(term):
        return lax.psum_scatter(term, "ring", scatter_dimension=0, tiled=True)

    du_p2, forget2, stats = retreat(
        1, dc2, dr2, prev2, cf2, keep, vectors, far, rows, span, (), ur=ur2, mixed=mixed()
    )

    def slices(slots):
        return jnp.stack([me ^ k for k in slots]).astype(jnp.int32)

    terms = []

    def weigh(whole, du_p, du_r, *others):
        def work(awaited):
            term = weight_term(whole, du_p, du_r, (*awaited, *others))
            terms.append(scatter(term).reshape(group, shard, 3 * width))
            return term

        return work

    kept, core, pair, line, (stats,) = reduce_group(
        lambda slots, awaited: back_features(
            slices(slots), du_p2, du_r2, w2, awaited
        ),
        group,
        (stats,),
        (),
        weigh(whole2, du_p2, du_r2),
    )

    prev1, dr1, dc1, high1, du_r1, rows_r1, part, sums1 = middle_back(
        1, model, kept, core, pair, line, high2, x2, norm_stats, stats, cf1, ur1, split, keep,
        order, back, vectors, out, far1,
    )
    far = exchange(part, ring, True)
    high = to_group(high1.reshape(group, 2, local, width))
    du_p1, rows_p1, forget1 = retreat(
        0, dc1, dr1, prev1, cf1, keep, vectors, far, rows, span, (), back=back
    )
    kept, core, pair, line, _ = reduce_group(
        lambda slots, awaited: back_tokens(
            slices(slots), rows_p1, rows_r1, pair_w1, reset_w1, awaited
        ),
        group,
        (),
        terms[:1],
        weigh(whole1, du_p1, du_r1, high),
    )
    outputs = join(high).reshape(rows_dev, span, model)
    (both,) = after([jnp.concatenate([terms[1], terms[0]], axis=2)], pair, line, outputs)
    both = to_group(both)
    input_grad, gains1 = first_back(
        kept, core, pair, line, inputs.reshape(local, model), ln_gain, high
    )
    input_grad = input_grad.reshape(rows_dev, span, model)
    weight_grad = join_weights(both, layers)

    def total(value):
        return jnp.sum(value, axis=-2)

    sums1 = total(sums1)
    sums2 = total(sums2)
    narrow = jnp.stack(
        [
            sums1[2], total(forget1), sums1[3],
            sums1[0], sums1[1], sums2[0], total(forget2), sums2[1],
        ]
    )
    narrow = lax.dynamic_update_slice(jnp.zeros((8, model), F32), narrow, (0, me * width))
    small = jnp.concatenate([total(gains1), narrow])
    small = spread_small(small, ring, group, (both,)).reshape(2, 5, shard)
    return (outputs, input_grad, weight_grad) + tuple(small[:, i] for i in range(5))


def solution(mesh):
    ring = mesh.shape["tm"] // 2
    fine = Mesh(
        mesh.devices.reshape(ring, 2, mesh.shape["rows"]), ("ring", "pair", "rows")
    )
    tm = ("ring", "pair")
    everything = ("ring", "pair", "rows")
    return jax.shard_map(
        body,
        mesh=fine,
        in_specs=(
            P("rows", tm, None),
            P("rows", tm, None),
            P("rows", tm),
            P(None, everything, None),
            P(),
            P(),
            P(),
            P(),
            P(),
        ),
        out_specs=(
            P("rows", tm, None),
            P("rows", tm, None),
            P(None, everything, None),
            P(None, everything),
            P(None, everything),
            P(None, everything),
            P(None, everything),
            P(None, everything),
        ),
        check_vma=False,
    )
```
